128 devices in a mesh: group: 16 (over y, x_hi, core), blk: 8 (over x_lo, z).
Axes of the slice: x: 4 (x_hi: 2, x_lo: 2; x = x_hi * 2 + x_lo), y: 4, z: 4, core: 2. Of those that a mesh axis runs over, the one named last changes fastest.
Arguments:
- embeddings: float32 [65536, 768], P(('group', 'blk')), may hold values from -6 to 6
- clusters: int32 [65536], P(('group', 'blk')), may hold values from 0 to 63, as said below
- indices: int32 [65536], P(('group', 'blk')), may hold values from 0 to 65535, each once
Outputs:
- nearest: float32 [65536], P(('group', 'blk'))
The draws below stay inside these ranges and needn't reach their ends.
Inputs may be any that keep to these rules, and one draw needn't show every extreme that they name: The cluster c is owned by group c mod 16. Of one device's 512 points at most 64 lie in clusters of one owner group, and every device has exactly 64 points in clusters of one owner group, the same group for all devices. Of one device's points at most 16 lie in any one cluster, and exactly that many in each cluster of that group. `indices`: each number appears once.
All inputs are finite; a program needn't handle non-finite values.
Results may differ from the reference program's by a relative error of at most 0.0003.
Values sent between devices are 32-bit elements; how exact they have to be, the bound alone decides.
No kernel may reach another device: no remote copies, remote signals or barrier semaphores. Data moves between devices by JAX's collectives and lax.ppermute only.
A program may use at most 128 MiB of HBM per device.

```python
import jax
import jax.numpy as jnp
from jax import lax

E = 768
P_DEV = 512
CL_GROUP = 4
POINTS = 65536
N_GROUP = 16
N_BLK = 8


def draw_clusters(key, part):
    key = jax.random.fold_in(key, 11)
    key_hot, key_bump, key_order, key_sub = jax.random.split(key, 4)
    groups = N_GROUP
    devices = N_GROUP * N_BLK
    capacity = 2 * P_DEV // groups
    remain = P_DEV - capacity
    hot = jax.random.randint(key_hot, (), 0, groups)
    position = jnp.arange(remain)
    bump = jax.random.randint(key_bump, (devices, remain), 0, 2)
    others = (position[None, :] % (groups - 1) + bump) % (groups - 1)
    target = (hot + 1 + others) % groups
    owners = jnp.concatenate([jnp.full((devices, capacity), hot, jnp.int32), target.astype(jnp.int32)], axis=1)
    row_keys = jax.random.split(key_order, devices)
    owners = jax.vmap(lambda row_key, row: jax.random.permutation(row_key, row))(row_keys, owners)
    onehot = (owners[:, :, None] == jnp.arange(groups)[None, None, :]).astype(jnp.int32)
    rank = jnp.sum((jnp.cumsum(onehot, axis=1) - onehot) * onehot, axis=2)
    offset = jax.random.randint(key_sub, (devices, groups), 0, CL_GROUP)
    shifted = jnp.sum(onehot * offset[:, None, :], axis=2)
    within = (rank + shifted) % CL_GROUP
    return (owners + groups * within).reshape(devices * P_DEV).astype(jnp.int32)


def block_scale(rng, shape, pieces, low, largest):
    def one(axis_at, parts):
        draws = jax.random.uniform(jax.random.fold_in(jax.random.fold_in(rng, 6), axis_at), (parts,), jnp.float32, low / len(pieces), largest / len(pieces))
        return jnp.repeat(jnp.exp(draws), shape[axis_at] // parts).reshape((-1,) + (1,) * (len(shape) - axis_at - 1))

    gain = one(*pieces[0])
    for cut in pieces[1:]:
        gain = gain * one(*cut)
    return gain


def bell_draw(rng, shape, scale, reach, shards=(), held_as=jnp.bfloat16):
    factor_of = block_scale(rng, shape, shards, -0.22, 0.18) if shards else 1.0
    values = jax.random.normal(rng, shape, jnp.float32) * scale * factor_of
    return jnp.minimum(jnp.maximum(values, -reach), reach).astype(held_as)


def setup_inputs(seed: int = 0) -> dict:
    keys = jax.random.split(jax.random.key(seed), 4)
    return {
        "embeddings": bell_draw(keys[0], (POINTS, E), 1.0, 6.0, ((0, 128),), jnp.float32),
        "clusters": draw_clusters(jax.random.fold_in(keys[3], 71), 0),
        "indices": jax.random.permutation(keys[2], POINTS).astype(jnp.int32),
    }


EPS = 1e-06

def reference(embeddings, clusters, indices):
    unit = embeddings * lax.rsqrt(lax.optimization_barrier(jnp.sum(embeddings * embeddings, axis=1, keepdims=True)) + EPS)
    order = jnp.argsort(clusters, stable=True)
    sorted_unit = unit[order]
    sorted_cl = clusters[order]
    sorted_ix = indices[order]
    block = min(512, POINTS)
    count = POINTS // block
    unit_blocks = sorted_unit.reshape(count, block, E)
    cl_blocks = sorted_cl.reshape(count, block)
    ix_blocks = sorted_ix.reshape(count, block)
    lowest = cl_blocks[:, 0]
    highest = cl_blocks[:, -1]

    def row_block(row):
        rows = unit_blocks[row]
        row_cl = cl_blocks[row]
        row_ix = ix_blocks[row]

        def column_step(best, col):

            def work(current):
                sims = lax.dot_general(rows, unit_blocks[col], (((1,), (1,)), ((), ())), precision=lax.Precision.HIGHEST, preferred_element_type=jnp.float32)
                valid = (row_cl[:, None] == cl_blocks[col][None, :]) & (ix_blocks[col][None, :] < row_ix[:, None])
                return jnp.maximum(current, lax.optimization_barrier(jnp.max(jnp.where(valid, sims, -1.0), axis=1)))
            touching = (lowest[col] <= highest[row]) & (highest[col] >= lowest[row])
            return (lax.cond(touching, work, lambda current: current, best), None)
        best, unused = lax.scan(column_step, jnp.full((block,), -1.0, jnp.float32), jnp.arange(count))
        return best
    best = lax.map(row_block, jnp.arange(count))
    return jnp.zeros((POINTS,), jnp.float32).at[order].set(best.reshape(POINTS))
```

```python
import functools

import jax
import jax.numpy as jnp
from jax import lax
from jax.experimental import pallas as pl
from jax.experimental.pallas import tpu as pltpu
from jax.sharding import Mesh, PartitionSpec as P

EPS = 1e-06
EMPTY = 1e9
TILE = 256
NT = (((1,), (1,)), ((), ()))
VMEM = pl.BlockSpec(memory_space=pltpu.VMEM)
PARAMS = pltpu.CompilerParams(vmem_limit_bytes=48 * 1024 * 1024)


def split(values):
    high = values.astype(jnp.bfloat16)
    low = (values - high.astype(jnp.float32)).astype(jnp.bfloat16)
    return high, low


def dot_f32(a, b, dims):
    return lax.dot_general(a, b, dims, preferred_element_type=jnp.float32)


def place_kernel(emb_ref, cl_ref, ix_ref, send_ref, rank_ref):
    chips, length, lanes = send_ref.shape
    count, width = emb_ref.shape
    slots = 16
    cl = cl_ref[...]
    ix = ix_ref[...]
    along = jnp.broadcast_to(cl.astype(jnp.float32), (count, count))
    down = along.T
    before = lax.broadcasted_iota(jnp.int32, (count, count), 0) < lax.broadcasted_iota(
        jnp.int32, (count, count), 1
    )
    rank = jnp.sum(
        jnp.where((along == down) & before, 1.0, 0.0), axis=0, keepdims=True
    ).astype(jnp.int32)
    rank_ref[...] = rank
    target = cl * slots + rank
    x = emb_ref[...]
    unit = x * lax.rsqrt(jnp.sum(x * x, axis=1, keepdims=True) + EPS)
    high, low = split(unit)
    mm = (((1,), (0,)), ((), ()))
    rows = chips * slots
    block = 256
    for r in range(0, rows, block):
        place = (
            lax.broadcasted_iota(jnp.int32, (block, count), 0) + r == target
        ).astype(jnp.float32).astype(jnp.bfloat16)
        moved = dot_f32(place, high, mm) + dot_f32(place, low, mm)
        c0, c1 = r // slots, (r + block) // slots
        for k in range(width // lanes):
            send_ref[c0:c1, k * slots : (k + 1) * slots, :] = moved[
                :, k * lanes : (k + 1) * lanes
            ].reshape(c1 - c0, slots, lanes)
    owner = (lax.broadcasted_iota(jnp.int32, (chips, count), 0) == cl).astype(
        jnp.float32
    ).astype(jnp.bfloat16)
    at_rank = lax.broadcasted_iota(jnp.int32, (lanes, count), 0) == rank
    tag = ix + 1
    tag_high = jnp.where(at_rank, (tag // 256).astype(jnp.float32), 0.0).astype(jnp.bfloat16)
    tag_low = jnp.where(at_rank, (tag % 256).astype(jnp.float32), 0.0).astype(jnp.bfloat16)
    tags = 256.0 * dot_f32(owner, tag_high, NT) + dot_f32(owner, tag_low, NT)
    send_ref[:, length - 8 :, :] = jnp.broadcast_to(tags[:, None, :], (chips, 8, lanes))


def unpack(held_ref, high_ref, low_ref):
    chips, length, lanes = held_ref.shape
    slots = 16
    rows = chips * slots
    for k in range((length - 8) // slots):
        part = held_ref[:, k * slots : (k + 1) * slots, :].reshape(rows, lanes)
        high, low = split(part)
        high_ref[:, k * lanes : (k + 1) * lanes] = high
        low_ref[:, k * lanes : (k + 1) * lanes] = low
    tags = held_ref[:, length - 8 : length - 7, :]
    spread = jnp.broadcast_to(tags, (chips, slots, lanes)).reshape(rows, lanes)
    lane = lax.broadcasted_iota(jnp.int32, (rows, lanes), 1)
    row = lax.broadcasted_iota(jnp.int32, (rows, lanes), 0)
    down = jnp.sum(jnp.where(lane == row % slots, spread, 0.0), axis=1, keepdims=True)
    down = jnp.where(down == 0.0, EMPTY, down)
    down = jnp.broadcast_to(down, (rows, lanes))
    return down, down.T[:1, :]


def products(high_i, low_i, high_j, low_j):
    return dot_f32(high_i, high_j, NT) + (
        dot_f32(high_i, low_j, NT) + dot_f32(low_i, high_j, NT)
    )


def lane_max(masked, lanes):
    best = masked[:, :lanes]
    for at in range(lanes, masked.shape[1], lanes):
        best = jnp.maximum(best, masked[:, at : at + lanes])
    return best


def own_kernel(held_ref, high_ref, low_ref, down_ref, best_ref, across_ref):
    down, along = unpack(held_ref, high_ref, low_ref)
    rows, lanes = down.shape
    down_ref[...] = down
    best_ref[...] = jnp.full((rows, lanes), -1.0, jnp.float32)
    across_ref[...] = jnp.full(across_ref.shape, -1.0, jnp.float32)
    for i in range(0, rows, TILE):
        si = slice(i, i + TILE)
        high_i, low_i = high_ref[si, :], low_ref[si, :]
        row_ix = down[si, :1]
        best = best_ref[si, :]
        for j in range(i, rows, TILE):
            sj = slice(j, j + TILE)
            sims = products(high_i, low_i, high_ref[sj, :], low_ref[sj, :])
            col_ix = along[:, sj]
            best = jnp.maximum(best, lane_max(jnp.where(col_ix < row_ix, sims, -1.0), lanes))
            if j > i:
                across_ref[:, sj] = jnp.maximum(
                    across_ref[:, sj],
                    jnp.max(jnp.where(row_ix < col_ix, sims, -1.0), axis=0, keepdims=True),
                )
        best_ref[si, :] = best


def other_kernel(held_ref, high_ref, low_ref, down_ref, best_ref, across_ref, out_ref, high_o, low_o):
    unused, along = unpack(held_ref, high_o, low_o)
    rows, lanes = down_ref.shape
    slots = 16
    total = jnp.broadcast_to(across_ref[:1, :], (lanes, rows)).T
    for i in range(0, rows, TILE):
        si = slice(i, i + TILE)
        high_i, low_i = high_ref[si, :], low_ref[si, :]
        row_ix = down_ref[si, :1]
        best = jnp.maximum(best_ref[si, :], total[si, :])
        for j in range(0, rows, TILE):
            sj = slice(j, j + TILE)
            sims = products(high_i, low_i, high_o[sj, :], low_o[sj, :])
            best = jnp.maximum(
                best, lane_max(jnp.where(along[:, sj] < row_ix, sims, -1.0), lanes)
            )
        best = jnp.max(best, axis=1, keepdims=True)
        lane = lax.broadcasted_iota(jnp.int32, (TILE, lanes), 1)
        row = lax.broadcasted_iota(jnp.int32, (TILE, lanes), 0)
        picked = jnp.where(lane == row % slots, best, -2.0).reshape(TILE // slots, slots, lanes)
        out_ref[i // slots : (i + TILE) // slots, :] = jnp.max(picked, axis=1)


def pick_kernel(answer_ref, cl_ref, rank_ref, out_ref):
    chips, lanes = answer_ref.shape
    count = cl_ref.shape[1]
    owner = (lax.broadcasted_iota(jnp.int32, (chips, count), 0) == cl_ref[...]).astype(
        jnp.float32
    ).astype(jnp.bfloat16)
    tn = (((0,), (0,)), ((), ()))
    answer = answer_ref[...]
    high, rest = split(answer)
    middle, low = split(answer - high.astype(jnp.float32))
    by_rank = dot_f32(high, owner, tn) + (dot_f32(middle, owner, tn) + dot_f32(low, owner, tn))
    at_rank = lax.broadcasted_iota(jnp.int32, (lanes, count), 0) == rank_ref[...]
    out_ref[...] = jnp.sum(jnp.where(at_rank, by_rank, 0.0), axis=0, keepdims=True)


def on_device(embeddings, clusters, indices):
    count, width = embeddings.shape
    chip_axes = ("y", "x_hi", "x_lo", "z")
    chips, slots, lanes = 64, 16, 128
    rows = chips * slots
    length = slots * width // lanes + 8
    cl = clusters.reshape(1, count)
    ix = indices.reshape(1, count)
    f32 = functools.partial(jax.ShapeDtypeStruct, dtype=jnp.float32)
    bf16 = functools.partial(jax.ShapeDtypeStruct, dtype=jnp.bfloat16)
    sending, rank = pl.pallas_call(
        place_kernel,
        out_shape=(f32((chips, length, lanes)), jax.ShapeDtypeStruct((1, count), jnp.int32)),
        in_specs=[VMEM] * 3,
        out_specs=(VMEM, VMEM),
        compiler_params=PARAMS,
        name="place",
    )(embeddings, cl, ix)
    held = lax.all_to_all(sending, chip_axes, split_axis=0, concat_axis=0, tiled=True)
    other = lax.ppermute(held, "core", [(0, 1), (1, 0)])
    flops = 2 * rows * rows * width * 3
    high, low, down, best, across = pl.pallas_call(
        own_kernel,
        out_shape=(
            bf16((rows, width)),
            bf16((rows, width)),
            f32((rows, lanes)),
            f32((rows, lanes)),
            f32((8, rows)),
        ),
        in_specs=[VMEM],
        out_specs=(VMEM,) * 5,
        compiler_params=PARAMS,
        cost_estimate=pl.CostEstimate(flops=flops, bytes_accessed=8 << 20, transcendentals=0),
        name="own",
    )(held)
    result = pl.pallas_call(
        other_kernel,
        out_shape=f32((chips, lanes)),
        in_specs=[VMEM] * 6,
        out_specs=VMEM,
        scratch_shapes=[
            pltpu.VMEM((rows, width), jnp.bfloat16),
            pltpu.VMEM((rows, width), jnp.bfloat16),
        ],
        compiler_params=PARAMS,
        cost_estimate=pl.CostEstimate(flops=flops, bytes_accessed=8 << 20, transcendentals=0),
        name="other",
    )(other, high, low, down, best, across)
    answer = lax.all_to_all(
        result.reshape(chips, 1, lanes), chip_axes, split_axis=0, concat_axis=0, tiled=True
    ).reshape(chips, lanes)
    out = pl.pallas_call(
        pick_kernel,
        out_shape=f32((1, count)),
        in_specs=[VMEM] * 3,
        out_specs=VMEM,
        compiler_params=PARAMS,
        name="pick",
    )(answer, cl, rank)
    return out.reshape(count)


def solution(mesh):
    fine = Mesh(mesh.devices.reshape(4, 2, 2, 2, 4), ("y", "x_hi", "core", "x_lo", "z"))
    points = ("y", "x_hi", "core", "x_lo", "z")
    return jax.shard_map(
        on_device,
        mesh=fine,
        in_specs=(P(points, None), P(points), P(points)),
        out_specs=P(points),
        check_vma=False,
    )
```

```python
import functools

import jax
import jax.numpy as jnp
from jax import lax
from jax.experimental import pallas as pl
from jax.experimental.pallas import tpu as pltpu
from jax.sharding import Mesh, PartitionSpec as P

EPS = 1e-06
EMPTY = 1e9
TILE = 256
NT = (((1,), (1,)), ((), ()))
VMEM = pl.BlockSpec(memory_space=pltpu.VMEM)
PARAMS = pltpu.CompilerParams(vmem_limit_bytes=20 * 1024 * 1024)


def split(values):
    high = values.astype(jnp.bfloat16)
    low = (values - high.astype(jnp.float32)).astype(jnp.bfloat16)
    return high, low


def dot_f32(a, b, dims):
    return lax.dot_general(a, b, dims, preferred_element_type=jnp.float32)


def place_kernel(emb_hbm, cl_hbm, ix_hbm, send_ref, rank_ref, emb, cl_ref, ix_ref, emb_sem, cl_sem, ix_sem):
    count, width = emb.shape
    slots, lanes, turn, chips = 16, 128, 8, 64
    parts = 4
    step = count // parts
    copies = [
        pltpu.make_async_copy(
            emb_hbm.at[pl.ds(p * step, step)], emb.at[pl.ds(p * step, step)], emb_sem.at[p]
        )
        for p in range(parts)
    ]
    cl_copy = pltpu.make_async_copy(cl_hbm, cl_ref, cl_sem)
    ix_copy = pltpu.make_async_copy(ix_hbm, ix_ref, ix_sem)
    cl_copy.start()
    ix_copy.start()
    for copy in copies:
        copy.start()
    cl_copy.wait()
    ix_copy.wait()
    cl = cl_ref[...]
    ix = ix_ref[...]
    along = jnp.broadcast_to(cl.astype(jnp.float32), (count, count))
    down = along.T
    before = lax.broadcasted_iota(jnp.int32, (count, count), 0) < lax.broadcasted_iota(
        jnp.int32, (count, count), 1
    )
    rank = jnp.sum(
        jnp.where((along == down) & before, 1.0, 0.0), axis=0, keepdims=True
    ).astype(jnp.int32)
    rank_ref[...] = rank
    target = cl * slots + (rank + cl % turn) % slots
    owner = (lax.broadcasted_iota(jnp.int32, (chips, count), 0) == cl).astype(
        jnp.float32
    ).astype(jnp.bfloat16)
    at_rank = lax.broadcasted_iota(jnp.int32, (lanes, count), 0) == rank
    tag = ix + 1
    tag_high = jnp.where(at_rank, (tag // 256).astype(jnp.float32), 0.0).astype(jnp.bfloat16)
    tag_low = jnp.where(at_rank, (tag % 256).astype(jnp.float32), 0.0).astype(jnp.bfloat16)
    tags = 256.0 * dot_f32(owner, tag_high, NT) + dot_f32(owner, tag_low, NT)
    highs, lows = [], []
    for p in range(parts):
        copies[p].wait()
        x = emb[p * step : (p + 1) * step, :]
        unit = x * lax.rsqrt(jnp.sum(x * x, axis=1, keepdims=True) + EPS)
        high, low = split(unit)
        highs.append(high)
        lows.append(low)
    high = jnp.concatenate(highs, axis=0)
    low = jnp.concatenate(lows, axis=0)
    mm = (((1,), (0,)), ((), ()))
    chunks = width // lanes
    sub = lax.broadcasted_iota(jnp.int32, (8, lanes), 0)
    block = 2 * turn * slots
    for r in range(0, chips * slots, block):
        place = (
            lax.broadcasted_iota(jnp.int32, (block, count), 0) + r == target
        ).astype(jnp.float32).astype(jnp.bfloat16)
        moved = dot_f32(place, high, mm) + dot_f32(place, low, mm)
        for g in range(2):
            base = (r // slots + g * turn) * (chunks * slots + 1)

            def head(a, k):
                at = (g * turn + a) * slots
                return moved[at : at + 8, k * lanes : (k + 1) * lanes]

            def tag_of(a):
                at = r // slots + g * turn + a
                return jnp.broadcast_to(tags[at : at + 1, :], (8, lanes))

            for a in range(turn):
                for k in range(chunks):
                    tile = head(a, k)
                    if k > 0 and a > 0:
                        tile = jnp.where(sub < a, head(a, k - 1), tile)
                    elif k == 0 and a > 0:
                        tile = jnp.where(sub == a - 1, tag_of(a - 1), tile)
                        if a > 1:
                            tile = jnp.where(sub < a - 1, head(a - 1, chunks - 1), tile)
                    at = base + 8 * (12 * a + 2 * k)
                    send_ref[at : at + 8, :] = tile
                    whole = (g * turn + a) * slots + 8
                    send_ref[at + 8 : at + 16, :] = moved[
                        whole : whole + 8, k * lanes : (k + 1) * lanes
                    ]
            at = base + 8 * 12 * turn
            send_ref[at : at + 8, :] = jnp.where(
                sub == turn - 1, tag_of(turn - 1), head(turn - 1, chunks - 1)
            )


def slot_of(rows, lanes):
    row = lax.broadcasted_iota(jnp.int32, (rows, lanes), 0)
    return (row % 16 + 16 - (row // 16) % 8) % 16


def unpack(held_ref, first, chips, high_ref, low_ref, spread_ref):
    slots, lanes, turn = 16, 128, 8
    chunks = high_ref.shape[1] // lanes
    sub = lax.broadcasted_iota(jnp.int32, (8, lanes), 0)
    for s in range(first, first + chips):
        a = s % turn
        base = 97 * (s - a)

        def tile(t):
            at = base + 8 * t
            return held_ref[at : at + 8, :]

        for k in range(chunks):
            t = 12 * a + 2 * k
            top = tile(t)
            if a > 0:
                top = jnp.where(sub < a, tile(t + 2), top)
            high, low = split(jnp.concatenate([top, tile(t + 1)], axis=0))
            high_ref[s * slots : (s + 1) * slots, k * lanes : (k + 1) * lanes] = high
            low_ref[s * slots : (s + 1) * slots, k * lanes : (k + 1) * lanes] = low
        at = base + 97 * a + 96
        spread_ref[s * slots : (s + 1) * slots, :] = jnp.broadcast_to(
            held_ref[at : at + 1, :], (slots, lanes)
        )


def tags_of(spread, slot):
    lanes = spread.shape[1]
    lane = lax.broadcasted_iota(jnp.int32, spread.shape, 1)
    down = jnp.sum(jnp.where(lane == slot, spread, 0.0), axis=1, keepdims=True)
    down = jnp.where(down == 0.0, EMPTY, down)
    return jnp.broadcast_to(down, spread.shape)


def products(high_i, low_i, high_j, low_j):
    return dot_f32(high_i, high_j, NT) + (
        dot_f32(high_i, low_j, NT) + dot_f32(low_i, high_j, NT)
    )


def own_kernel(held_ref, high_ref, low_ref, down_ref, best_ref, across_ref, spread_ref):
    rows, lanes = down_ref.shape
    slot = slot_of(TILE, lanes)
    best_ref[...] = jnp.full((rows, lanes), -1.0, jnp.float32)
    for j in range(0, rows, TILE):
        sj = slice(j, j + TILE)
        unpack(held_ref, j // 16, TILE // 16, high_ref, low_ref, spread_ref)
        down_j = tags_of(spread_ref[sj, :], slot)
        down_ref[sj, :] = down_j
        along = jnp.concatenate(
            [down_j[c : c + lanes, :].T[:1, :] for c in range(0, TILE, lanes)], axis=1
        )
        end = j + TILE
        sims = products(high_ref[:end, :], low_ref[:end, :], high_ref[sj, :], low_ref[sj, :])
        down = down_ref[:end, :]
        best = best_ref[:end, :]
        for c in range(0, TILE, lanes):
            col_ix = along[:, c : c + lanes]
            part = sims[:, c : c + lanes]
            best = jnp.maximum(best, jnp.where(col_ix < down, part, -1.0))
            over = jnp.full((1, lanes), -1.0, jnp.float32)
            if j > 0:
                over = jnp.max(
                    jnp.where(down[:j] < col_ix, part[:j], -1.0), axis=0, keepdims=True
                )
            across_ref[:, j + c : j + c + lanes] = jnp.broadcast_to(over, (8, lanes))
        best_ref[:end, :] = best


def other_kernel(
    held_ref, high_ref, low_ref, down_ref, best_ref, across_ref, out_ref, high_o, low_o, spread_ref, total_ref
):
    rows, lanes = down_ref.shape
    slots = 16
    slot = slot_of(TILE, lanes)
    total_ref[...] = jnp.maximum(
        best_ref[...], jnp.broadcast_to(across_ref[:1, :], (lanes, rows)).T
    )
    for j in range(0, rows, TILE):
        sj = slice(j, j + TILE)
        unpack(held_ref, j // 16, TILE // 16, high_o, low_o, spread_ref)
        down_j = tags_of(spread_ref[sj, :], slot)
        sims = products(high_ref[...], low_ref[...], high_o[sj, :], low_o[sj, :])
        best = total_ref[...]
        for c in range(0, TILE, lanes):
            col_ix = down_j[c : c + lanes, :].T[:1, :]
            best = jnp.maximum(
                best, jnp.where(col_ix < down_ref[...], sims[:, c : c + lanes], -1.0)
            )
        total_ref[...] = best
    lane = lax.broadcasted_iota(jnp.int32, (TILE, lanes), 1)
    for i in range(0, rows, TILE):
        best = jnp.max(total_ref[i : i + TILE, :], axis=1, keepdims=True)
        picked = jnp.where(lane == slot, best, -2.0).reshape(TILE // slots, slots, lanes)
        out_ref[i // slots : (i + TILE) // slots, :] = jnp.max(picked, axis=1)


def pick_kernel(answer_ref, cl_ref, rank_ref, out_ref):
    chips, lanes = answer_ref.shape
    count = cl_ref.shape[1]
    owner = (lax.broadcasted_iota(jnp.int32, (chips, count), 0) == cl_ref[...]).astype(
        jnp.float32
    ).astype(jnp.bfloat16)
    tn = (((0,), (0,)), ((), ()))
    answer = answer_ref[...]
    high, rest = split(answer)
    middle, low = split(answer - high.astype(jnp.float32))
    by_rank = dot_f32(high, owner, tn) + (dot_f32(middle, owner, tn) + dot_f32(low, owner, tn))
    at_rank = lax.broadcasted_iota(jnp.int32, (lanes, count), 0) == rank_ref[...]
    out_ref[...] = jnp.sum(jnp.where(at_rank, by_rank, 0.0), axis=0, keepdims=True)


def on_device(embeddings, clusters, indices):
    count, width = embeddings.shape
    chip_axes = ("y", "x_hi", "x_lo", "z")
    chips, slots, lanes = 64, 16, 128
    rows = chips * slots
    length = slots * width // lanes + 1
    cl = clusters.reshape(1, count)
    ix = indices.reshape(1, count)
    f32 = functools.partial(jax.ShapeDtypeStruct, dtype=jnp.float32)
    bf16 = functools.partial(jax.ShapeDtypeStruct, dtype=jnp.bfloat16)
    dma = pltpu.SemaphoreType.DMA
    sending, rank = pl.pallas_call(
        place_kernel,
        out_shape=(f32((chips * length, lanes)), jax.ShapeDtypeStruct((1, count), jnp.int32)),
        in_specs=[pl.BlockSpec(memory_space=pltpu.HBM)] * 3,
        out_specs=(VMEM, VMEM),
        scratch_shapes=[
            pltpu.VMEM((count, width), jnp.float32),
            pltpu.VMEM((1, count), jnp.int32),
            pltpu.VMEM((1, count), jnp.int32),
            dma((4,)),
            dma,
            dma,
        ],
        compiler_params=PARAMS,
        name="place",
    )(*(pltpu.with_memory_space_constraint(v, pltpu.HBM) for v in (embeddings, cl, ix)))
    held = lax.all_to_all(
        sending.reshape(chips * length, 1, lanes), chip_axes, split_axis=0, concat_axis=0, tiled=True
    )
    other = lax.ppermute(held, "core", [(0, 1), (1, 0)]).reshape(chips * length, lanes)
    held = held.reshape(chips * length, lanes)
    flops = 2 * rows * rows * width * 3
    high, low, down, best, across = pl.pallas_call(
        own_kernel,
        out_shape=(
            bf16((rows, width)),
            bf16((rows, width)),
            f32((rows, lanes)),
            f32((rows, lanes)),
            f32((8, rows)),
        ),
        in_specs=[VMEM],
        out_specs=(VMEM,) * 5,
        scratch_shapes=[pltpu.VMEM((rows, lanes), jnp.float32)],
        compiler_params=PARAMS,
        cost_estimate=pl.CostEstimate(flops=flops, bytes_accessed=8 << 20, transcendentals=0),
        name="own",
    )(held)
    result = pl.pallas_call(
        other_kernel,
        out_shape=f32((chips, lanes)),
        in_specs=[VMEM] * 6,
        out_specs=VMEM,
        scratch_shapes=[
            pltpu.VMEM((rows, width), jnp.bfloat16),
            pltpu.VMEM((rows, width), jnp.bfloat16),
            pltpu.VMEM((rows, lanes), jnp.float32),
            pltpu.VMEM((rows, lanes), jnp.float32),
        ],
        compiler_params=PARAMS,
        cost_estimate=pl.CostEstimate(flops=flops, bytes_accessed=8 << 20, transcendentals=0),
        name="other",
    )(other, high, low, down, best, across)
    answer = lax.all_to_all(
        result.reshape(chips, 1, lanes), chip_axes, split_axis=0, concat_axis=0, tiled=True
    ).reshape(chips, lanes)
    out = pl.pallas_call(
        pick_kernel,
        out_shape=f32((1, count)),
        in_specs=[VMEM] * 3,
        out_specs=VMEM,
        compiler_params=PARAMS,
        name="pick",
    )(answer, cl, rank)
    return out.reshape(count)


def solution(mesh):
    fine = Mesh(mesh.devices.reshape(4, 2, 2, 2, 4), ("y", "x_hi", "core", "x_lo", "z"))
    points = ("y", "x_hi", "core", "x_lo", "z")
    return jax.shard_map(
        on_device,
        mesh=fine,
        in_specs=(P(points, None), P(points), P(points)),
        out_specs=P(points),
        check_vma=False,
    )
```

```python
import functools

import jax
import jax.numpy as jnp
from jax import lax
from jax.experimental import pallas as pl
from jax.experimental.pallas import tpu as pltpu
from jax.sharding import Mesh, PartitionSpec as P

EPS = 1e-06
EMPTY = 1e9
TILE = 256
POINTS = ("y", "x_hi", "core", "x_lo", "z")
NT = (((1,), (1,)), ((), ()))
VMEM = pl.BlockSpec(memory_space=pltpu.VMEM)
PARAMS = pltpu.CompilerParams(vmem_limit_bytes=20 * 1024 * 1024)


def split(values):
    high = values.astype(jnp.bfloat16)
    low = (values - high.astype(jnp.float32)).astype(jnp.bfloat16)
    return high, low


def dot_f32(a, b, dims):
    return lax.dot_general(a, b, dims, preferred_element_type=jnp.float32)


def place_kernel(emb_hbm, cl_hbm, ix_hbm, send_ref, rank_ref, emb, cl_ref, ix_ref, emb_sem, cl_sem, ix_sem):
    count, width = emb.shape
    slots, lanes, turn, chips = 16, 128, 8, 64
    parts = 4
    step = count // parts
    copies = [
        pltpu.make_async_copy(
            emb_hbm.at[pl.ds(p * step, step)], emb.at[pl.ds(p * step, step)], emb_sem.at[p]
        )
        for p in range(parts)
    ]
    cl_copy = pltpu.make_async_copy(cl_hbm, cl_ref, cl_sem)
    ix_copy = pltpu.make_async_copy(ix_hbm, ix_ref, ix_sem)
    cl_copy.start()
    ix_copy.start()
    for copy in copies:
        copy.start()
    cl_copy.wait()
    ix_copy.wait()
    cl = cl_ref[...]
    ix = ix_ref[...]
    along = jnp.broadcast_to(cl.astype(jnp.float32), (count, count))
    down = along.T
    before = lax.broadcasted_iota(jnp.int32, (count, count), 0) < lax.broadcasted_iota(
        jnp.int32, (count, count), 1
    )
    rank = jnp.sum(
        jnp.where((along == down) & before, 1.0, 0.0), axis=0, keepdims=True
    ).astype(jnp.int32)
    rank_ref[...] = rank
    target = cl * slots + (rank + cl % turn) % slots
    owner = (lax.broadcasted_iota(jnp.int32, (chips, count), 0) == cl).astype(
        jnp.float32
    ).astype(jnp.bfloat16)
    at_rank = lax.broadcasted_iota(jnp.int32, (lanes, count), 0) == rank
    tag = ix + 1
    tag_high = jnp.where(at_rank, (tag // 256).astype(jnp.float32), 0.0).astype(jnp.bfloat16)
    tag_low = jnp.where(at_rank, (tag % 256).astype(jnp.float32), 0.0).astype(jnp.bfloat16)
    tags = 256.0 * dot_f32(owner, tag_high, NT) + dot_f32(owner, tag_low, NT)
    highs, lows = [], []
    for p in range(parts):
        copies[p].wait()
        x = emb[p * step : (p + 1) * step, :]
        unit = x * lax.rsqrt(jnp.sum(x * x, axis=1, keepdims=True) + EPS)
        high, low = split(unit)
        highs.append(high)
        lows.append(low)
    high = jnp.concatenate(highs, axis=0)
    low = jnp.concatenate(lows, axis=0)
    mm = (((1,), (0,)), ((), ()))
    chunks = width // lanes
    sub = lax.broadcasted_iota(jnp.int32, (8, lanes), 0)
    block = 2 * turn * slots
    for r in range(0, chips * slots, block):
        place = (
            lax.broadcasted_iota(jnp.int32, (block, count), 0) + r == target
        ).astype(jnp.float32).astype(jnp.bfloat16)
        moved = dot_f32(place, high, mm) + dot_f32(place, low, mm)
        for g in range(2):
            base = (r // slots + g * turn) * (chunks * slots + 1)

            def head(a, k):
                at = (g * turn + a) * slots
                return moved[at : at + 8, k * lanes : (k + 1) * lanes]

            def tag_of(a):
                at = r // slots + g * turn + a
                return jnp.broadcast_to(tags[at : at + 1, :], (8, lanes))

            for a in range(turn):
                for k in range(chunks):
                    tile = head(a, k)
                    if k > 0 and a > 0:
                        tile = jnp.where(sub < a, head(a, k - 1), tile)
                    elif k == 0 and a > 0:
                        tile = jnp.where(sub == a - 1, tag_of(a - 1), tile)
                        if a > 1:
                            tile = jnp.where(sub < a - 1, head(a - 1, chunks - 1), tile)
                    at = base + 8 * (12 * a + 2 * k)
                    send_ref[at : at + 8, :] = tile
                    whole = (g * turn + a) * slots + 8
                    send_ref[at + 8 : at + 16, :] = moved[
                        whole : whole + 8, k * lanes : (k + 1) * lanes
                    ]
            at = base + 8 * 12 * turn
            send_ref[at : at + 8, :] = jnp.where(
                sub == turn - 1, tag_of(turn - 1), head(turn - 1, chunks - 1)
            )


def slot_of(rows, lanes):
    row = lax.broadcasted_iota(jnp.int32, (rows, lanes), 0)
    return (row % 16 + 16 - (row // 16) % 8) % 16


def unpack(held_ref, first, chips, high_ref, low_ref, spread_ref):
    slots, lanes, turn = 16, 128, 8
    chunks = high_ref.shape[1] // lanes
    sub = lax.broadcasted_iota(jnp.int32, (8, lanes), 0)
    for s in range(first, first + chips):
        a = s % turn
        base = 97 * (s - a)

        def tile(t):
            at = base + 8 * t
            return held_ref[at : at + 8, :]

        for k in range(chunks):
            t = 12 * a + 2 * k
            top = tile(t)
            if a > 0:
                top = jnp.where(sub < a, tile(t + 2), top)
            high, low = split(jnp.concatenate([top, tile(t + 1)], axis=0))
            high_ref[s * slots : (s + 1) * slots, k * lanes : (k + 1) * lanes] = high
            low_ref[s * slots : (s + 1) * slots, k * lanes : (k + 1) * lanes] = low
        at = base + 97 * a + 96
        spread_ref[s * slots : (s + 1) * slots, :] = jnp.broadcast_to(
            held_ref[at : at + 1, :], (slots, lanes)
        )


def tags_of(spread, slot):
    lanes = spread.shape[1]
    lane = lax.broadcasted_iota(jnp.int32, spread.shape, 1)
    down = jnp.sum(jnp.where(lane == slot, spread, 0.0), axis=1, keepdims=True)
    down = jnp.where(down == 0.0, EMPTY, down)
    return jnp.broadcast_to(down, spread.shape)


def products(high_i, low_i, high_j, low_j):
    return dot_f32(high_i, high_j, NT) + (
        dot_f32(high_i, low_j, NT) + dot_f32(low_i, high_j, NT)
    )


def own_kernel(held_ref, high_ref, low_ref, down_ref, best_ref, across_ref, spread_ref):
    rows, lanes = down_ref.shape
    slot = slot_of(TILE, lanes)
    best_ref[...] = jnp.full((rows, lanes), -1.0, jnp.float32)
    for j in range(0, rows, TILE):
        sj = slice(j, j + TILE)
        unpack(held_ref, j // 16, TILE // 16, high_ref, low_ref, spread_ref)
        down_j = tags_of(spread_ref[sj, :], slot)
        down_ref[sj, :] = down_j
        along = jnp.concatenate(
            [down_j[c : c + lanes, :].T[:1, :] for c in range(0, TILE, lanes)], axis=1
        )
        end = j + TILE
        sims = products(high_ref[:end, :], low_ref[:end, :], high_ref[sj, :], low_ref[sj, :])
        down = down_ref[:end, :]
        best = best_ref[:end, :]
        for c in range(0, TILE, lanes):
            col_ix = along[:, c : c + lanes]
            part = sims[:, c : c + lanes]
            best = jnp.maximum(best, jnp.where(col_ix < down, part, -1.0))
            over = jnp.full((1, lanes), -1.0, jnp.float32)
            if j > 0:
                over = jnp.max(
                    jnp.where(down[:j] < col_ix, part[:j], -1.0), axis=0, keepdims=True
                )
            across_ref[:, j + c : j + c + lanes] = jnp.broadcast_to(over, (8, lanes))
        best_ref[:end, :] = best


def by_slot(best, slot):
    slots = 16
    rows, lanes = best.shape
    lane = lax.broadcasted_iota(jnp.int32, (rows, lanes), 1)
    picked = jnp.where(lane == slot, best, -2.0).reshape(rows // slots, slots, lanes)
    return jnp.max(picked, axis=1)


def other_kernel(
    held_ref, high_ref, low_ref, down_ref, best_ref, across_ref, out_ref, high_o, low_o, spread_ref, total_ref
):
    rows, lanes = down_ref.shape
    half = rows // 2
    slot = slot_of(TILE, lanes)
    core = lax.axis_index("core")
    total_ref[...] = jnp.maximum(
        best_ref[...], jnp.broadcast_to(across_ref[:1, :], (lanes, rows)).T
    )
    over = []
    for j in range(0, rows, TILE):
        sj = slice(j, j + TILE)
        unpack(held_ref, j // 16, TILE // 16, high_o, low_o, spread_ref)
        down_j = tags_of(spread_ref[sj, :], slot)
        start = core * half if j < half else (1 - core) * half
        mine = pl.ds(pl.multiple_of(start, half), half)
        sims = products(high_ref[mine, :], low_ref[mine, :], high_o[sj, :], low_o[sj, :])
        down = down_ref[mine, :]
        best = total_ref[mine, :]
        for c in range(0, TILE, lanes):
            col_ix = down_j[c : c + lanes, :].T[:1, :]
            part = sims[:, c : c + lanes]
            best = jnp.maximum(best, jnp.where(col_ix < down, part, -1.0))
            over.append(jnp.max(jnp.where(down < col_ix, part, -1.0), axis=0, keepdims=True))
        total_ref[mine, :] = best
    per_chip, per_tile = 16, TILE // 16
    for i in range(0, rows, TILE):
        own = by_slot(jnp.max(total_ref[i : i + TILE, :], axis=1, keepdims=True) + jnp.zeros((TILE, lanes), jnp.float32), slot)
        cols = jnp.concatenate(
            [
                jnp.broadcast_to(over[(i + c) // lanes], (lanes, lanes)).T
                for c in range(0, TILE, lanes)
            ],
            axis=0,
        )
        other = by_slot(cols, slot)
        for g in range(0, per_tile, 8):
            at = 2 * (i // per_chip + g)
            own_g, other_g = own[g : g + 8, :], other[g : g + 8, :]
            out_ref[at : at + 8, :] = jnp.where(core == 0, own_g, other_g)
            out_ref[at + 8 : at + 16, :] = jnp.where(core == 0, other_g, own_g)


def pick_kernel(answer_ref, cl_ref, rank_ref, out_ref):
    lanes = answer_ref.shape[1]
    chips = answer_ref.shape[0] // 2
    count = cl_ref.shape[1]
    owner = (lax.broadcasted_iota(jnp.int32, (chips, count), 0) == cl_ref[...]).astype(
        jnp.float32
    ).astype(jnp.bfloat16)
    tn = (((0,), (0,)), ((), ()))
    answer = jnp.max(answer_ref[...].reshape(chips // 8, 2, 8, lanes), axis=1).reshape(chips, lanes)
    high, rest = split(answer)
    middle, low = split(answer - high.astype(jnp.float32))
    by_rank = dot_f32(high, owner, tn) + (dot_f32(middle, owner, tn) + dot_f32(low, owner, tn))
    at_rank = lax.broadcasted_iota(jnp.int32, (lanes, count), 0) == rank_ref[...]
    out_ref[...] = jnp.sum(jnp.where(at_rank, by_rank, 0.0), axis=0, keepdims=True)


def on_device(embeddings, clusters, indices):
    count, width = embeddings.shape
    chip_axes = ("y", "x_hi", "x_lo", "z")
    chips, slots, lanes = 64, 16, 128
    rows = chips * slots
    length = slots * width // lanes + 1
    cl = clusters.reshape(1, count)
    ix = indices.reshape(1, count)
    f32 = functools.partial(jax.ShapeDtypeStruct, dtype=jnp.float32)
    bf16 = functools.partial(jax.ShapeDtypeStruct, dtype=jnp.bfloat16)
    dma = pltpu.SemaphoreType.DMA
    sending, rank = pl.pallas_call(
        place_kernel,
        out_shape=(f32((chips * length, lanes)), jax.ShapeDtypeStruct((1, count), jnp.int32)),
        in_specs=[pl.BlockSpec(memory_space=pltpu.HBM)] * 3,
        out_specs=(VMEM, VMEM),
        scratch_shapes=[
            pltpu.VMEM((count, width), jnp.float32),
            pltpu.VMEM((1, count), jnp.int32),
            pltpu.VMEM((1, count), jnp.int32),
            dma((4,)),
            dma,
            dma,
        ],
        compiler_params=PARAMS,
        name="place",
    )(*(pltpu.with_memory_space_constraint(v, pltpu.HBM) for v in (embeddings, cl, ix)))
    held = lax.all_to_all(
        sending.reshape(chips * length, 1, lanes), chip_axes, split_axis=0, concat_axis=0, tiled=True
    )
    other = lax.ppermute(held, "core", [(0, 1), (1, 0)]).reshape(chips * length, lanes)
    held = held.reshape(chips * length, lanes)
    flops = 2 * rows * rows * width * 3
    high, low, down, best, across = pl.pallas_call(
        own_kernel,
        out_shape=(
            bf16((rows, width)),
            bf16((rows, width)),
            f32((rows, lanes)),
            f32((rows, lanes)),
            f32((8, rows)),
        ),
        in_specs=[VMEM],
        out_specs=(VMEM,) * 5,
        scratch_shapes=[pltpu.VMEM((rows, lanes), jnp.float32)],
        compiler_params=PARAMS,
        cost_estimate=pl.CostEstimate(flops=flops, bytes_accessed=8 << 20, transcendentals=0),
        name="own",
    )(held)
    result = pl.pallas_call(
        other_kernel,
        out_shape=f32((2 * chips, lanes)),
        in_specs=[VMEM] * 6,
        out_specs=VMEM,
        scratch_shapes=[
            pltpu.VMEM((rows, width), jnp.bfloat16),
            pltpu.VMEM((rows, width), jnp.bfloat16),
            pltpu.VMEM((rows, lanes), jnp.float32),
            pltpu.VMEM((rows, lanes), jnp.float32),
        ],
        compiler_params=PARAMS,
        cost_estimate=pl.CostEstimate(flops=flops, bytes_accessed=8 << 20, transcendentals=0),
        name="other",
    )(other, high, low, down, best, across)
    answer = lax.all_to_all(
        result.reshape(2 * chips, 1, lanes), POINTS, split_axis=0, concat_axis=0, tiled=True
    ).reshape(2 * chips, lanes)
    out = pl.pallas_call(
        pick_kernel,
        out_shape=f32((1, count)),
        in_specs=[VMEM] * 3,
        out_specs=VMEM,
        compiler_params=PARAMS,
        name="pick",
    )(answer, cl, rank)
    return out.reshape(count)


def solution(mesh):
    fine = Mesh(mesh.devices.reshape(4, 2, 2, 2, 4), POINTS)
    return jax.shard_map(
        on_device,
        mesh=fine,
        in_specs=(P(POINTS, None), P(POINTS), P(POINTS)),
        out_specs=P(POINTS),
        check_vma=False,
    )
```

```python
import functools

import jax
import jax.numpy as jnp
from jax import lax
from jax.experimental import pallas as pl
from jax.experimental.pallas import tpu as pltpu
from jax.sharding import Mesh, PartitionSpec as P

EPS = 1e-06
EMPTY = 1e9
TILE = 256
POINTS = ("y", "x_hi", "core", "x_lo", "z")
NT = (((1,), (1,)), ((), ()))
VMEM = pl.BlockSpec(memory_space=pltpu.VMEM)
PARAMS = pltpu.CompilerParams(vmem_limit_bytes=20 * 1024 * 1024)


def split(values):
    high = values.astype(jnp.bfloat16)
    low = (values - high.astype(jnp.float32)).astype(jnp.bfloat16)
    return high, low


def dot_f32(a, b, dims):
    return lax.dot_general(a, b, dims, preferred_element_type=jnp.float32)


def place_kernel(emb_hbm, cl_hbm, ix_hbm, send_ref, rank_ref, emb, cl_ref, ix_ref, emb_sem, cl_sem, ix_sem):
    count, width = emb.shape
    slots, lanes, turn, chips = 16, 128, 8, 64
    parts = 2
    step = count // parts
    copies = [
        pltpu.make_async_copy(
            emb_hbm.at[pl.ds(p * step, step)], emb.at[pl.ds(p * step, step)], emb_sem.at[p]
        )
        for p in range(parts)
    ]
    cl_copy = pltpu.make_async_copy(cl_hbm, cl_ref, cl_sem)
    ix_copy = pltpu.make_async_copy(ix_hbm, ix_ref, ix_sem)
    cl_copy.start()
    ix_copy.start()
    for copy in copies:
        copy.start()
    cl_copy.wait()
    ix_copy.wait()
    cl = cl_ref[...]
    ix = ix_ref[...]
    along = jnp.broadcast_to(cl.astype(jnp.float32), (count, count))
    down = along.T
    before = lax.broadcasted_iota(jnp.int32, (count, count), 0) < lax.broadcasted_iota(
        jnp.int32, (count, count), 1
    )
    rank = jnp.sum(
        jnp.where((along == down) & before, 1.0, 0.0), axis=0, keepdims=True
    ).astype(jnp.int32)
    rank_ref[...] = rank
    target = cl * slots + (rank + cl % turn) % slots
    owner = (lax.broadcasted_iota(jnp.int32, (chips, count), 0) == cl).astype(
        jnp.float32
    ).astype(jnp.bfloat16)
    at_rank = lax.broadcasted_iota(jnp.int32, (lanes, count), 0) == rank
    tag = ix + 1
    tag_high = jnp.where(at_rank, (tag // 256).astype(jnp.float32), 0.0).astype(jnp.bfloat16)
    tag_low = jnp.where(at_rank, (tag % 256).astype(jnp.float32), 0.0).astype(jnp.bfloat16)
    tags = 256.0 * dot_f32(owner, tag_high, NT) + dot_f32(owner, tag_low, NT)
    highs, lows = [], []
    for p in range(parts):
        copies[p].wait()
        x = emb[p * step : (p + 1) * step, :]
        unit = x * lax.rsqrt(jnp.sum(x * x, axis=1, keepdims=True) + EPS)
        high, low = split(unit)
        highs.append(high)
        lows.append(low)
    high = jnp.concatenate(highs, axis=0)
    low = jnp.concatenate(lows, axis=0)
    mm = (((1,), (0,)), ((), ()))
    chunks = width // lanes
    sub = lax.broadcasted_iota(jnp.int32, (8, lanes), 0)
    block = 2 * turn * slots
    for r in range(0, chips * slots, block):
        place = (
            lax.broadcasted_iota(jnp.int32, (block, count), 0) + r == target
        ).astype(jnp.float32).astype(jnp.bfloat16)
        moved = dot_f32(place, high, mm) + dot_f32(place, low, mm)
        for g in range(2):
            base = (r // slots + g * turn) * (chunks * slots + 1)

            def head(a, k):
                at = (g * turn + a) * slots
                return moved[at : at + 8, k * lanes : (k + 1) * lanes]

            def tag_of(a):
                at = r // slots + g * turn + a
                return jnp.broadcast_to(tags[at : at + 1, :], (8, lanes))

            for a in range(turn):
                for k in range(chunks):
                    tile = head(a, k)
                    if k > 0 and a > 0:
                        tile = jnp.where(sub < a, head(a, k - 1), tile)
                    elif k == 0 and a > 0:
                        tile = jnp.where(sub == a - 1, tag_of(a - 1), tile)
                        if a > 1:
                            tile = jnp.where(sub < a - 1, head(a - 1, chunks - 1), tile)
                    at = base + 8 * (12 * a + 2 * k)
                    send_ref[at : at + 8, :] = tile
                    whole = (g * turn + a) * slots + 8
                    send_ref[at + 8 : at + 16, :] = moved[
                        whole : whole + 8, k * lanes : (k + 1) * lanes
                    ]
            at = base + 8 * 12 * turn
            send_ref[at : at + 8, :] = jnp.where(
                sub == turn - 1, tag_of(turn - 1), head(turn - 1, chunks - 1)
            )


def slot_of(rows, lanes):
    row = lax.broadcasted_iota(jnp.int32, (rows, lanes), 0)
    return (row % 16 + 16 - (row // 16) % 8) % 16


def unpack(held_ref, first, chips, high_ref, low_ref, spread_ref):
    slots, lanes, turn = 16, 128, 8
    chunks = high_ref.shape[1] // lanes
    sub = lax.broadcasted_iota(jnp.int32, (8, lanes), 0)
    for s in range(first, first + chips):
        a = s % turn
        base = 97 * (s - a)

        def tile(t):
            at = base + 8 * t
            return held_ref[at : at + 8, :]

        for k in range(chunks):
            t = 12 * a + 2 * k
            top = tile(t)
            if a > 0:
                top = jnp.where(sub < a, tile(t + 2), top)
            high, low = split(jnp.concatenate([top, tile(t + 1)], axis=0))
            high_ref[s * slots : (s + 1) * slots, k * lanes : (k + 1) * lanes] = high
            low_ref[s * slots : (s + 1) * slots, k * lanes : (k + 1) * lanes] = low
        at = base + 97 * a + 96
        spread_ref[s * slots : (s + 1) * slots, :] = jnp.broadcast_to(
            held_ref[at : at + 1, :], (slots, lanes)
        )


def tags_of(spread, slot):
    lanes = spread.shape[1]
    lane = lax.broadcasted_iota(jnp.int32, spread.shape, 1)
    down = jnp.sum(jnp.where(lane == slot, spread, 0.0), axis=1, keepdims=True)
    down = jnp.where(down == 0.0, EMPTY, down)
    return jnp.broadcast_to(down, spread.shape)


def products(high_i, low_i, high_j, low_j):
    return dot_f32(high_i, high_j, NT) + (
        dot_f32(high_i, low_j, NT) + dot_f32(low_i, high_j, NT)
    )


def by_slot(best, slot):
    slots = 16
    rows, lanes = best.shape
    lane = lax.broadcasted_iota(jnp.int32, (rows, lanes), 1)
    picked = jnp.where(lane == slot, best, -2.0).reshape(rows // slots, slots, lanes)
    return jnp.max(picked, axis=1)


def own_kernel(held_ref, high_ref, low_ref, down_ref, best_ref, spread_ref):
    rows, lanes = down_ref.shape
    slot = slot_of(TILE, lanes)
    for j in range(0, rows, TILE):
        sj = slice(j, j + TILE)
        unpack(held_ref, j // 16, TILE // 16, high_ref, low_ref, spread_ref)
        down_j = tags_of(spread_ref[sj, :], slot)
        down_ref[sj, :] = down_j
        best_ref[sj, :] = jnp.full((TILE, lanes), -1.0, jnp.float32)
        end = j + TILE
        sims = products(high_ref[:end, :], low_ref[:end, :], high_ref[sj, :], low_ref[sj, :])
        down = down_ref[:end, :]
        best = best_ref[:end, :]
        over = []
        for c in range(0, TILE, lanes):
            col_ix = down_j[c : c + lanes, :].T[:1, :]
            part = sims[:, c : c + lanes]
            best = jnp.maximum(best, jnp.where(col_ix < down, part, -1.0))
            if j > 0:
                top = jnp.max(
                    jnp.where(down[:j] < col_ix, part[:j], -1.0), axis=0, keepdims=True
                )
                over.append(jnp.broadcast_to(top, (lanes, lanes)).T)
        if j > 0:
            best_ref[:j, :] = best[:j]
            best_ref[sj, :] = jnp.maximum(best[j:], jnp.concatenate(over, axis=0))
        else:
            best_ref[sj, :] = best


def other_kernel(
    held_ref, high_ref, low_ref, down_ref, best_ref, out_ref, high_o, low_o, spread_ref, total_ref
):
    rows, lanes = down_ref.shape
    half = rows // 2
    chips = rows // 16
    per_tile = TILE // 16
    slot = slot_of(TILE, lanes)
    core = lax.axis_index("core")
    mine_at = pl.multiple_of(core * chips, chips)
    other_at = pl.multiple_of((1 - core) * chips, chips)
    for j in range(0, rows, TILE):
        sj = slice(j, j + TILE)
        unpack(held_ref, j // 16, TILE // 16, high_o, low_o, spread_ref)
        down_j = tags_of(spread_ref[sj, :], slot)
        start = core * half if j < half else (1 - core) * half
        mine = pl.ds(pl.multiple_of(start, half), half)
        sims = products(high_ref[mine, :], low_ref[mine, :], high_o[sj, :], low_o[sj, :])
        down = down_ref[mine, :]
        best = best_ref[mine, :] if j % half == 0 else total_ref[mine, :]
        over = []
        for c in range(0, TILE, lanes):
            col_ix = down_j[c : c + lanes, :].T[:1, :]
            part = sims[:, c : c + lanes]
            best = jnp.maximum(best, jnp.where(col_ix < down, part, -1.0))
            top = jnp.max(jnp.where(down < col_ix, part, -1.0), axis=0, keepdims=True)
            over.append(jnp.broadcast_to(top, (lanes, lanes)).T)
        at = pl.ds(pl.multiple_of(other_at + j // 16, 8), per_tile)
        out_ref[at, :] = by_slot(jnp.concatenate(over, axis=0), slot)
        if j % half == 0:
            total_ref[mine, :] = best
        else:
            best = jnp.broadcast_to(jnp.max(best, axis=1, keepdims=True), best.shape)
            first = pl.multiple_of(mine_at + start // 16, 8)
            for i in range(0, half, TILE):
                out_ref[pl.ds(pl.multiple_of(first + i // 16, 8), per_tile), :] = by_slot(
                    best[i : i + TILE], slot
                )


def pick_kernel(answer_ref, cl_ref, rank_ref, out_ref):
    lanes = answer_ref.shape[1]
    chips = answer_ref.shape[0] // 2
    count = cl_ref.shape[1]
    owner = (lax.broadcasted_iota(jnp.int32, (chips, count), 0) == cl_ref[...]).astype(
        jnp.float32
    ).astype(jnp.bfloat16)
    tn = (((0,), (0,)), ((), ()))
    answer = jnp.maximum(answer_ref[:chips, :], answer_ref[chips:, :])
    high, rest = split(answer)
    middle, low = split(answer - high.astype(jnp.float32))
    by_rank = dot_f32(high, owner, tn) + (dot_f32(middle, owner, tn) + dot_f32(low, owner, tn))
    at_rank = lax.broadcasted_iota(jnp.int32, (lanes, count), 0) == rank_ref[...]
    out_ref[...] = jnp.sum(jnp.where(at_rank, by_rank, 0.0), axis=0, keepdims=True)


def on_device(embeddings, clusters, indices):
    count, width = embeddings.shape
    chip_axes = ("z", "y", "x_hi", "x_lo")
    chips, slots, lanes = 64, 16, 128
    rows = chips * slots
    length = slots * width // lanes + 1
    cl = clusters.reshape(1, count)
    ix = indices.reshape(1, count)
    f32 = functools.partial(jax.ShapeDtypeStruct, dtype=jnp.float32)
    bf16 = functools.partial(jax.ShapeDtypeStruct, dtype=jnp.bfloat16)
    dma = pltpu.SemaphoreType.DMA
    sending, rank = pl.pallas_call(
        place_kernel,
        out_shape=(f32((chips * length, lanes)), jax.ShapeDtypeStruct((1, count), jnp.int32)),
        in_specs=[pl.BlockSpec(memory_space=pltpu.HBM)] * 3,
        out_specs=(VMEM, VMEM),
        scratch_shapes=[
            pltpu.VMEM((count, width), jnp.float32),
            pltpu.VMEM((1, count), jnp.int32),
            pltpu.VMEM((1, count), jnp.int32),
            dma((2,)),
            dma,
            dma,
        ],
        compiler_params=PARAMS,
        name="place",
    )(*(pltpu.with_memory_space_constraint(v, pltpu.HBM) for v in (embeddings, cl, ix)))
    held = lax.all_to_all(
        sending.reshape(chips * length, 1, lanes), chip_axes, split_axis=0, concat_axis=0, tiled=True
    )
    other = lax.ppermute(held, "core", [(0, 1), (1, 0)]).reshape(chips * length, lanes)
    held = held.reshape(chips * length, lanes)
    flops = 2 * rows * rows * width * 3
    high, low, down, best = pl.pallas_call(
        own_kernel,
        out_shape=(
            bf16((rows, width)),
            bf16((rows, width)),
            f32((rows, lanes)),
            f32((rows, lanes)),
        ),
        in_specs=[VMEM],
        out_specs=(VMEM,) * 4,
        scratch_shapes=[pltpu.VMEM((rows, lanes), jnp.float32)],
        compiler_params=PARAMS,
        cost_estimate=pl.CostEstimate(flops=flops, bytes_accessed=8 << 20, transcendentals=0),
        name="own",
    )(held)
    result = pl.pallas_call(
        other_kernel,
        out_shape=f32((2 * chips, lanes)),
        in_specs=[VMEM] * 5,
        out_specs=VMEM,
        scratch_shapes=[
            pltpu.VMEM((rows, width), jnp.bfloat16),
            pltpu.VMEM((rows, width), jnp.bfloat16),
            pltpu.VMEM((rows, lanes), jnp.float32),
            pltpu.VMEM((rows, lanes), jnp.float32),
        ],
        compiler_params=PARAMS,
        cost_estimate=pl.CostEstimate(flops=flops, bytes_accessed=8 << 20, transcendentals=0),
        name="other",
    )(other, high, low, down, best)
    answer = lax.all_to_all(
        result.reshape(2 * chips, 1, lanes), ("core",) + chip_axes, split_axis=0, concat_axis=0, tiled=True
    ).reshape(2 * chips, lanes)
    out = pl.pallas_call(
        pick_kernel,
        out_shape=f32((1, count)),
        in_specs=[VMEM] * 3,
        out_specs=VMEM,
        compiler_params=PARAMS,
        name="pick",
    )(answer, cl, rank)
    return out.reshape(count)


def solution(mesh):
    fine = Mesh(mesh.devices.reshape(4, 2, 2, 2, 4), POINTS)
    return jax.shard_map(
        on_device,
        mesh=fine,
        in_specs=(P(POINTS, None), P(POINTS), P(POINTS)),
        out_specs=P(POINTS),
        check_vma=False,
    )
```

```python
import functools

import jax
import jax.numpy as jnp
from jax import lax
from jax.experimental import pallas as pl
from jax.experimental.pallas import tpu as pltpu
from jax.sharding import Mesh, PartitionSpec as P

EPS = 1e-06
EMPTY = 1e9
TILE = 256
POINTS = ("y", "x_hi", "core", "x_lo", "z")
NT = (((1,), (1,)), ((), ()))
VMEM = pl.BlockSpec(memory_space=pltpu.VMEM)
PARAMS = pltpu.CompilerParams(vmem_limit_bytes=20 * 1024 * 1024)


def split(values):
    high = values.astype(jnp.bfloat16)
    low = (values - high.astype(jnp.float32)).astype(jnp.bfloat16)
    return high, low


def dot_f32(a, b, dims):
    return lax.dot_general(a, b, dims, preferred_element_type=jnp.float32)


def place_kernel(emb_hbm, cl_hbm, ix_hbm, send_ref, rank_ref, emb, cl_ref, ix_ref, emb_sem, cl_sem, ix_sem):
    count, width = emb.shape
    slots, lanes, turn, chips = 16, 128, 8, 64
    parts = 2
    step = count // parts
    copies = [
        pltpu.make_async_copy(
            emb_hbm.at[pl.ds(p * step, step)], emb.at[pl.ds(p * step, step)], emb_sem.at[p]
        )
        for p in range(parts)
    ]
    cl_copy = pltpu.make_async_copy(cl_hbm, cl_ref, cl_sem)
    ix_copy = pltpu.make_async_copy(ix_hbm, ix_ref, ix_sem)
    cl_copy.start()
    ix_copy.start()
    for copy in copies:
        copy.start()
    cl_copy.wait()
    ix_copy.wait()
    cl = cl_ref[...]
    ix = ix_ref[...]
    along = jnp.broadcast_to(cl.astype(jnp.float32), (count, count))
    down = along.T
    before = lax.broadcasted_iota(jnp.int32, (count, count), 0) < lax.broadcasted_iota(
        jnp.int32, (count, count), 1
    )
    rank = jnp.sum(
        jnp.where((along == down) & before, 1.0, 0.0), axis=0, keepdims=True
    ).astype(jnp.int32)
    rank_ref[...] = rank
    target = cl * slots + (rank + cl % turn) % slots
    owner = (lax.broadcasted_iota(jnp.int32, (chips, count), 0) == cl).astype(
        jnp.float32
    ).astype(jnp.bfloat16)
    at_rank = lax.broadcasted_iota(jnp.int32, (lanes, count), 0) == rank
    tag = ix + 1
    tag_high = jnp.where(at_rank, (tag // 256).astype(jnp.float32), 0.0).astype(jnp.bfloat16)
    tag_low = jnp.where(at_rank, (tag % 256).astype(jnp.float32), 0.0).astype(jnp.bfloat16)
    tags = 256.0 * dot_f32(owner, tag_high, NT) + dot_f32(owner, tag_low, NT)
    highs, lows = [], []
    for p in range(parts):
        copies[p].wait()
        x = emb[p * step : (p + 1) * step, :]
        unit = x * lax.rsqrt(jnp.sum(x * x, axis=1, keepdims=True) + EPS)
        high, low = split(unit)
        highs.append(high)
        lows.append(low)
    high = jnp.concatenate(highs, axis=0)
    low = jnp.concatenate(lows, axis=0)
    mm = (((1,), (0,)), ((), ()))
    chunks = width // lanes
    sub = lax.broadcasted_iota(jnp.int32, (8, lanes), 0)
    block = 2 * turn * slots
    for r in range(0, chips * slots, block):
        place = (
            lax.broadcasted_iota(jnp.int32, (block, count), 0) + r == target
        ).astype(jnp.float32).astype(jnp.bfloat16)
        moved = dot_f32(place, high, mm) + dot_f32(place, low, mm)
        for g in range(2):
            base = (r // slots + g * turn) * (chunks * slots + 1)

            def head(a, k):
                at = (g * turn + a) * slots
                return moved[at : at + 8, k * lanes : (k + 1) * lanes]

            def tag_of(a):
                at = r // slots + g * turn + a
                return jnp.broadcast_to(tags[at : at + 1, :], (8, lanes))

            for a in range(turn):
                for k in range(chunks):
                    tile = head(a, k)
                    if k > 0 and a > 0:
                        tile = jnp.where(sub < a, head(a, k - 1), tile)
                    elif k == 0 and a > 0:
                        tile = jnp.where(sub == a - 1, tag_of(a - 1), tile)
                        if a > 1:
                            tile = jnp.where(sub < a - 1, head(a - 1, chunks - 1), tile)
                    at = base + 8 * (12 * a + 2 * k)
                    send_ref[at : at + 8, :] = tile
                    whole = (g * turn + a) * slots + 8
                    send_ref[at + 8 : at + 16, :] = moved[
                        whole : whole + 8, k * lanes : (k + 1) * lanes
                    ]
            at = base + 8 * 12 * turn
            send_ref[at : at + 8, :] = jnp.where(
                sub == turn - 1, tag_of(turn - 1), head(turn - 1, chunks - 1)
            )


def slot_of(rows, lanes):
    row = lax.broadcasted_iota(jnp.int32, (rows, lanes), 0)
    return (row % 16 + 16 - (row // 16) % 8) % 16


def unpack(held_ref, first, chips, high_ref, low_ref, spread_ref):
    slots, lanes, turn = 16, 128, 8
    chunks = high_ref.shape[1] // lanes
    sub = lax.broadcasted_iota(jnp.int32, (8, lanes), 0)
    for s in range(first, first + chips):
        a = s % turn
        base = 97 * (s - a)

        def tile(t):
            at = base + 8 * t
            return held_ref[at : at + 8, :]

        for k in range(chunks):
            t = 12 * a + 2 * k
            top = tile(t)
            if a > 0:
                top = jnp.where(sub < a, tile(t + 2), top)
            high, low = split(jnp.concatenate([top, tile(t + 1)], axis=0))
            high_ref[s * slots : (s + 1) * slots, k * lanes : (k + 1) * lanes] = high
            low_ref[s * slots : (s + 1) * slots, k * lanes : (k + 1) * lanes] = low
        at = base + 97 * a + 96
        spread_ref[s * slots : (s + 1) * slots, :] = jnp.broadcast_to(
            held_ref[at : at + 1, :], (slots, lanes)
        )


def tags_of(spread, slot):
    lanes = spread.shape[1]
    lane = lax.broadcasted_iota(jnp.int32, spread.shape, 1)
    down = jnp.sum(jnp.where(lane == slot, spread, 0.0), axis=1, keepdims=True)
    down = jnp.where(down == 0.0, EMPTY, down)
    return jnp.broadcast_to(down, spread.shape)


def products(high_i, low_i, high_j, low_j):
    return dot_f32(high_i, high_j, NT) + (
        dot_f32(high_i, low_j, NT) + dot_f32(low_i, high_j, NT)
    )


def by_slot(best, slot):
    slots = 16
    rows, lanes = best.shape
    lane = lax.broadcasted_iota(jnp.int32, (rows, lanes), 1)
    picked = jnp.where(lane == slot, best, -2.0).reshape(rows // slots, slots, lanes)
    return jnp.max(picked, axis=1)


def own_kernel(held_ref, high_ref, low_ref, down_ref, best_ref, spread_ref):
    rows, lanes = down_ref.shape
    slot = slot_of(TILE, lanes)
    for j in range(0, rows, TILE):
        sj = slice(j, j + TILE)
        unpack(held_ref, j // 16, TILE // 16, high_ref, low_ref, spread_ref)
        down_j = tags_of(spread_ref[sj, :], slot)
        down_ref[sj, :] = down_j
        best_ref[sj, :] = jnp.full((TILE, lanes), -1.0, jnp.float32)
        end = j + TILE
        sims = products(high_ref[:end, :], low_ref[:end, :], high_ref[sj, :], low_ref[sj, :])
        down = down_ref[:end, :]
        best = best_ref[:end, :]
        over = []
        for c in range(0, TILE, lanes):
            col_ix = down_j[c : c + lanes, :].T[:1, :]
            part = sims[:, c : c + lanes]
            best = jnp.maximum(best, jnp.where(col_ix < down, part, -1.0))
            if j > 0:
                top = jnp.max(
                    jnp.where(down[:j] < col_ix, part[:j], -1.0), axis=0, keepdims=True
                )
                over.append(jnp.broadcast_to(top, (lanes, lanes)).T)
        if j > 0:
            best_ref[:j, :] = best[:j]
            best_ref[sj, :] = jnp.maximum(best[j:], jnp.concatenate(over, axis=0))
        else:
            best_ref[sj, :] = best


def cross(held_ref, high_ref, low_ref, down_ref, start, high_o, low_o, spread_ref, best_ref, total_ref):
    half, lanes = high_o.shape[0], down_ref.shape[1]
    slot = slot_of(TILE, lanes)
    mine = pl.ds(pl.multiple_of(start, half), half)
    cols = []
    for j in range(0, half, TILE):
        sj = slice(j, j + TILE)
        unpack(held_ref, j // 16, TILE // 16, high_o, low_o, spread_ref)
        down_j = tags_of(spread_ref[sj, :], slot)
        sims = products(high_ref[mine, :], low_ref[mine, :], high_o[sj, :], low_o[sj, :])
        down = down_ref[mine, :]
        best = best_ref[mine, :] if j == 0 else total_ref[...]
        over = []
        for c in range(0, TILE, lanes):
            col_ix = down_j[c : c + lanes, :].T[:1, :]
            part = sims[:, c : c + lanes]
            best = jnp.maximum(best, jnp.where(col_ix < down, part, -1.0))
            top = jnp.max(jnp.where(down < col_ix, part, -1.0), axis=0, keepdims=True)
            over.append(jnp.broadcast_to(top, (lanes, lanes)).T)
        cols.append(by_slot(jnp.concatenate(over, axis=0), slot))
        total_ref[...] = best
    rows = []
    best = jnp.broadcast_to(jnp.max(total_ref[...], axis=1, keepdims=True), (half, lanes))
    for i in range(0, half, TILE):
        rows.append(by_slot(best[i : i + TILE], slot))
    return jnp.concatenate(rows, axis=0), jnp.concatenate(cols, axis=0)


def first_kernel(
    held_ref, high_ref, low_ref, down_ref, best_ref, row_ref, col_ref, high_o, low_o, spread_ref, total_ref
):
    start = lax.axis_index("core") * high_o.shape[0]
    row_ref[...], col_ref[...] = cross(
        held_ref, high_ref, low_ref, down_ref, start, high_o, low_o, spread_ref, best_ref, total_ref
    )


def second_kernel(
    held_ref, high_ref, low_ref, down_ref, best_ref, row_ref, col_ref, out_ref, high_o, low_o, spread_ref, total_ref
):
    core = lax.axis_index("core")
    rows, cols = cross(
        held_ref,
        high_ref,
        low_ref,
        down_ref,
        (1 - core) * high_o.shape[0],
        high_o,
        low_o,
        spread_ref,
        best_ref,
        total_ref,
    )
    chips = out_ref.shape[0] // 4
    first = core == 0
    own = jnp.where(first, row_ref[...], rows), jnp.where(first, rows, row_ref[...])
    other = col_ref[...], cols
    for h in range(2):
        out_ref[h * chips : (h + 1) * chips, :] = jnp.where(first, own[h], other[h])
        out_ref[(2 + h) * chips : (3 + h) * chips, :] = jnp.where(first, other[h], own[h])


def pick_kernel(answer_ref, cl_ref, rank_ref, out_ref):
    lanes = answer_ref.shape[1]
    chips = answer_ref.shape[0] // 2
    count = cl_ref.shape[1]
    owner = (lax.broadcasted_iota(jnp.int32, (chips, count), 0) == cl_ref[...]).astype(
        jnp.float32
    ).astype(jnp.bfloat16)
    tn = (((0,), (0,)), ((), ()))
    answer = jnp.maximum(answer_ref[:chips, :], answer_ref[chips:, :])
    high, rest = split(answer)
    middle, low = split(answer - high.astype(jnp.float32))
    by_rank = dot_f32(high, owner, tn) + (dot_f32(middle, owner, tn) + dot_f32(low, owner, tn))
    at_rank = lax.broadcasted_iota(jnp.int32, (lanes, count), 0) == rank_ref[...]
    out_ref[...] = jnp.sum(jnp.where(at_rank, by_rank, 0.0), axis=0, keepdims=True)


def on_device(embeddings, clusters, indices):
    count, width = embeddings.shape
    chip_axes = ("z", "y", "x_hi", "x_lo")
    chips, slots, lanes = 64, 16, 128
    rows = chips * slots
    length = slots * width // lanes + 1
    cl = clusters.reshape(1, count)
    ix = indices.reshape(1, count)
    f32 = functools.partial(jax.ShapeDtypeStruct, dtype=jnp.float32)
    bf16 = functools.partial(jax.ShapeDtypeStruct, dtype=jnp.bfloat16)
    dma = pltpu.SemaphoreType.DMA
    sending, rank = pl.pallas_call(
        place_kernel,
        out_shape=(f32((chips * length, lanes)), jax.ShapeDtypeStruct((1, count), jnp.int32)),
        in_specs=[pl.BlockSpec(memory_space=pltpu.HBM)] * 3,
        out_specs=(VMEM, VMEM),
        scratch_shapes=[
            pltpu.VMEM((count, width), jnp.float32),
            pltpu.VMEM((1, count), jnp.int32),
            pltpu.VMEM((1, count), jnp.int32),
            dma((2,)),
            dma,
            dma,
        ],
        compiler_params=PARAMS,
        name="place",
    )(*(pltpu.with_memory_space_constraint(v, pltpu.HBM) for v in (embeddings, cl, ix)))
    held = lax.all_to_all(
        sending.reshape(chips * length, 1, lanes), chip_axes, split_axis=0, concat_axis=0, tiled=True
    )
    part = chips * length // 2
    arrived = [
        lax.ppermute(held[h * part : (h + 1) * part], "core", [(0, 1), (1, 0)]).reshape(part, lanes)
        for h in range(2)
    ]
    held = held.reshape(chips * length, lanes)
    flops = 2 * rows * rows * width * 3
    high, low, down, best = pl.pallas_call(
        own_kernel,
        out_shape=(
            bf16((rows, width)),
            bf16((rows, width)),
            f32((rows, lanes)),
            f32((rows, lanes)),
        ),
        in_specs=[VMEM],
        out_specs=(VMEM,) * 4,
        scratch_shapes=[pltpu.VMEM((rows, lanes), jnp.float32)],
        compiler_params=PARAMS,
        cost_estimate=pl.CostEstimate(flops=flops, bytes_accessed=8 << 20, transcendentals=0),
        name="own",
    )(held)
    half = rows // 2
    scratch = [
        pltpu.VMEM((half, width), jnp.bfloat16),
        pltpu.VMEM((half, width), jnp.bfloat16),
        pltpu.VMEM((half, lanes), jnp.float32),
        pltpu.VMEM((half, lanes), jnp.float32),
    ]
    cost = pl.CostEstimate(flops=flops // 4, bytes_accessed=2 << 20, transcendentals=0)
    row, col = pl.pallas_call(
        first_kernel,
        out_shape=(f32((chips // 2, lanes)),) * 2,
        in_specs=[VMEM] * 5,
        out_specs=(VMEM,) * 2,
        scratch_shapes=scratch,
        compiler_params=PARAMS,
        cost_estimate=cost,
        name="first",
    )(arrived[0], high, low, down, best)
    result = pl.pallas_call(
        second_kernel,
        out_shape=f32((2 * chips, lanes)),
        in_specs=[VMEM] * 7,
        out_specs=VMEM,
        scratch_shapes=scratch,
        compiler_params=PARAMS,
        cost_estimate=cost,
        name="second",
    )(arrived[1], high, low, down, best, row, col)
    answer = lax.all_to_all(
        result.reshape(2 * chips, 1, lanes), ("core",) + chip_axes, split_axis=0, concat_axis=0, tiled=True
    ).reshape(2 * chips, lanes)
    out = pl.pallas_call(
        pick_kernel,
        out_shape=f32((1, count)),
        in_specs=[VMEM] * 3,
        out_specs=VMEM,
        compiler_params=PARAMS,
        name="pick",
    )(answer, cl, rank)
    return out.reshape(count)


def solution(mesh):
    fine = Mesh(mesh.devices.reshape(4, 2, 2, 2, 4), POINTS)
    return jax.shard_map(
        on_device,
        mesh=fine,
        in_specs=(P(POINTS, None), P(POINTS), P(POINTS)),
        out_specs=P(POINTS),
        check_vma=False,
    )
```

```python
import functools

import jax
import jax.numpy as jnp
from jax import lax
from jax.experimental import pallas as pl
from jax.experimental.pallas import tpu as pltpu
from jax.sharding import Mesh, PartitionSpec as P

EPS = 1e-06
EMPTY = 1e9
TILE = 256
POINTS = ("y", "x_hi", "core", "x_lo", "z")
NT = (((1,), (1,)), ((), ()))
VMEM = pl.BlockSpec(memory_space=pltpu.VMEM)
PARAMS = pltpu.CompilerParams(vmem_limit_bytes=20 * 1024 * 1024)


def split(values):
    high = values.astype(jnp.bfloat16)
    low = (values - high.astype(jnp.float32)).astype(jnp.bfloat16)
    return high, low


def dot_f32(a, b, dims):
    return lax.dot_general(a, b, dims, preferred_element_type=jnp.float32)


def place_kernel(emb_hbm, cl_hbm, ix_hbm, send_ref, rank_ref, emb, cl_ref, ix_ref, emb_sem, cl_sem, ix_sem):
    count, width = emb.shape
    slots, lanes, turn, chips = 16, 128, 8, 64
    parts = 2
    step = count // parts
    copies = [
        pltpu.make_async_copy(
            emb_hbm.at[pl.ds(p * step, step)], emb.at[pl.ds(p * step, step)], emb_sem.at[p]
        )
        for p in range(parts)
    ]
    cl_copy = pltpu.make_async_copy(cl_hbm, cl_ref, cl_sem)
    ix_copy = pltpu.make_async_copy(ix_hbm, ix_ref, ix_sem)
    cl_copy.start()
    ix_copy.start()
    for copy in copies:
        copy.start()
    cl_copy.wait()
    ix_copy.wait()
    cl = cl_ref[...]
    ix = ix_ref[...]
    along = jnp.broadcast_to(cl.astype(jnp.float32), (count, count))
    down = along.T
    before = lax.broadcasted_iota(jnp.int32, (count, count), 0) < lax.broadcasted_iota(
        jnp.int32, (count, count), 1
    )
    rank = jnp.sum(
        jnp.where((along == down) & before, 1.0, 0.0), axis=0, keepdims=True
    ).astype(jnp.int32)
    rank_ref[...] = rank
    target = cl * slots + (rank + cl % turn) % slots
    owner = (lax.broadcasted_iota(jnp.int32, (chips, count), 0) == cl).astype(
        jnp.float32
    ).astype(jnp.bfloat16)
    at_rank = lax.broadcasted_iota(jnp.int32, (lanes, count), 0) == rank
    tag = ix + 1
    tag_high = jnp.where(at_rank, (tag // 256).astype(jnp.float32), 0.0).astype(jnp.bfloat16)
    tag_low = jnp.where(at_rank, (tag % 256).astype(jnp.float32), 0.0).astype(jnp.bfloat16)
    tags = 256.0 * dot_f32(owner, tag_high, NT) + dot_f32(owner, tag_low, NT)
    highs, lows = [], []
    for p in range(parts):
        copies[p].wait()
        x = emb[p * step : (p + 1) * step, :]
        unit = x * lax.rsqrt(jnp.sum(x * x, axis=1, keepdims=True) + EPS)
        high, low = split(unit)
        highs.append(high)
        lows.append(low)
    high = jnp.concatenate(highs, axis=0)
    low = jnp.concatenate(lows, axis=0)
    mm = (((1,), (0,)), ((), ()))
    chunks = width // lanes
    sub = lax.broadcasted_iota(jnp.int32, (8, lanes), 0)
    block = 2 * turn * slots
    for r in range(0, chips * slots, block):
        place = (
            lax.broadcasted_iota(jnp.int32, (block, count), 0) + r == target
        ).astype(jnp.float32).astype(jnp.bfloat16)
        moved = dot_f32(place, high, mm) + dot_f32(place, low, mm)
        for g in range(2):
            base = (r // slots + g * turn) * (chunks * slots + 1)

            def head(a, k):
                at = (g * turn + a) * slots
                return moved[at : at + 8, k * lanes : (k + 1) * lanes]

            def tag_of(a):
                at = r // slots + g * turn + a
                return jnp.broadcast_to(tags[at : at + 1, :], (8, lanes))

            for a in range(turn):
                for k in range(chunks):
                    tile = head(a, k)
                    if k > 0 and a > 0:
                        tile = jnp.where(sub < a, head(a, k - 1), tile)
                    elif k == 0 and a > 0:
                        tile = jnp.where(sub == a - 1, tag_of(a - 1), tile)
                        if a > 1:
                            tile = jnp.where(sub < a - 1, head(a - 1, chunks - 1), tile)
                    at = base + 8 * (12 * a + 2 * k)
                    send_ref[at : at + 8, :] = tile
                    whole = (g * turn + a) * slots + 8
                    send_ref[at + 8 : at + 16, :] = moved[
                        whole : whole + 8, k * lanes : (k + 1) * lanes
                    ]
            at = base + 8 * 12 * turn
            send_ref[at : at + 8, :] = jnp.where(
                sub == turn - 1, tag_of(turn - 1), head(turn - 1, chunks - 1)
            )


def slot_of(rows, lanes):
    row = lax.broadcasted_iota(jnp.int32, (rows, lanes), 0)
    return (row % 16 + 16 - (row // 16) % 8) % 16


def unpack(held_ref, first, chips, high_ref, low_ref, spread_ref):
    slots, lanes, turn = 16, 128, 8
    chunks = high_ref.shape[1] // lanes
    sub = lax.broadcasted_iota(jnp.int32, (8, lanes), 0)
    for s in range(first, first + chips):
        a = s % turn
        base = 97 * (s - a)

        def tile(t):
            at = base + 8 * t
            return held_ref[at : at + 8, :]

        for k in range(chunks):
            t = 12 * a + 2 * k
            top = tile(t)
            if a > 0:
                top = jnp.where(sub < a, tile(t + 2), top)
            high, low = split(jnp.concatenate([top, tile(t + 1)], axis=0))
            high_ref[s * slots : (s + 1) * slots, k * lanes : (k + 1) * lanes] = high
            low_ref[s * slots : (s + 1) * slots, k * lanes : (k + 1) * lanes] = low
        at = base + 97 * a + 96
        spread_ref[s * slots : (s + 1) * slots, :] = jnp.broadcast_to(
            held_ref[at : at + 1, :], (slots, lanes)
        )


def tags_of(spread, slot):
    lanes = spread.shape[1]
    lane = lax.broadcasted_iota(jnp.int32, spread.shape, 1)
    down = jnp.sum(jnp.where(lane == slot, spread, 0.0), axis=1, keepdims=True)
    down = jnp.where(down == 0.0, EMPTY, down)
    return jnp.broadcast_to(down, spread.shape)


def products(high_i, low_i, high_j, low_j):
    return dot_f32(high_i, high_j, NT) + (
        dot_f32(high_i, low_j, NT) + dot_f32(low_i, high_j, NT)
    )


def by_slot(best, slot):
    slots = 16
    rows, lanes = best.shape
    lane = lax.broadcasted_iota(jnp.int32, (rows, lanes), 1)
    picked = jnp.where(lane == slot, best, -2.0).reshape(rows // slots, slots, lanes)
    return jnp.max(picked, axis=1)


def own_kernel(held_ref, high_ref, low_ref, down_ref, best_ref, spread_ref):
    rows, lanes = down_ref.shape
    slot = slot_of(TILE, lanes)
    for j in range(0, rows, TILE):
        sj = slice(j, j + TILE)
        unpack(held_ref, j // 16, TILE // 16, high_ref, low_ref, spread_ref)
        down_j = tags_of(spread_ref[sj, :], slot)
        down_ref[sj, :] = down_j
        best_ref[sj, :] = jnp.full((TILE, lanes), -1.0, jnp.float32)
        end = j + TILE
        sims = products(high_ref[:end, :], low_ref[:end, :], high_ref[sj, :], low_ref[sj, :])
        down = down_ref[:end, :]
        best = best_ref[:end, :]
        over = []
        for c in range(0, TILE, lanes):
            col_ix = down_j[c : c + lanes, :].T[:1, :]
            part = sims[:, c : c + lanes]
            best = jnp.maximum(best, jnp.where(col_ix < down, part, -1.0))
            if j > 0:
                top = jnp.max(
                    jnp.where(down[:j] < col_ix, part[:j], -1.0), axis=0, keepdims=True
                )
                over.append(jnp.broadcast_to(top, (lanes, lanes)).T)
        if j > 0:
            best_ref[:j, :] = best[:j]
            best_ref[sj, :] = jnp.maximum(best[j:], jnp.concatenate(over, axis=0))
        else:
            best_ref[sj, :] = best


def cross(held_ref, high_ref, low_ref, down_ref, start, high_o, low_o, spread_ref, best_ref, total_ref):
    half, lanes = high_o.shape[0], down_ref.shape[1]
    slot = slot_of(TILE, lanes)
    cols, over = {}, {}

    def mine(i):
        return pl.ds(pl.multiple_of(start + i, TILE), TILE)

    def finish(i, j, sims):
        down = down_ref[mine(i), :]
        best = best_ref[mine(i), :] if j == 0 else total_ref[i : i + TILE, :]
        for n, col_ix in enumerate(cols[j]):
            part = sims[:, n * lanes : (n + 1) * lanes]
            best = jnp.maximum(best, jnp.where(col_ix < down, part, -1.0))
            top = jnp.where(down < col_ix, part, -1.0).reshape(TILE // 8, 8, lanes)
            top = jnp.max(top, axis=0)
            over[j, n] = top if i == 0 else jnp.maximum(over[j, n], top)
        total_ref[i : i + TILE, :] = best

    waiting = None
    for j in range(0, half, TILE):
        sj = slice(j, j + TILE)
        unpack(held_ref, j // 16, TILE // 16, high_o, low_o, spread_ref)
        down_j = tags_of(spread_ref[sj, :], slot)
        cols[j] = [down_j[c : c + lanes, :].T[:1, :] for c in range(0, TILE, lanes)]
        for i in range(0, half, TILE):
            sims = products(high_ref[mine(i), :], low_ref[mine(i), :], high_o[sj, :], low_o[sj, :])
            if waiting is not None:
                finish(*waiting)
            waiting = i, j, sims
    finish(*waiting)
    rows_out, cols_out = [], []
    for j in range(0, half, TILE):
        wide = [
            jnp.broadcast_to(jnp.max(over[j, n], axis=0, keepdims=True), (lanes, lanes)).T
            for n in range(TILE // lanes)
        ]
        cols_out.append(by_slot(jnp.concatenate(wide, axis=0), slot))
    for i in range(0, half, TILE):
        best = jnp.max(total_ref[i : i + TILE, :], axis=1, keepdims=True)
        rows_out.append(by_slot(jnp.broadcast_to(best, (TILE, lanes)), slot))
    return jnp.concatenate(rows_out, axis=0), jnp.concatenate(cols_out, axis=0)


def first_kernel(
    held_ref, high_ref, low_ref, down_ref, best_ref, row_ref, col_ref, high_o, low_o, spread_ref, total_ref
):
    start = lax.axis_index("core") * high_o.shape[0]
    row_ref[...], col_ref[...] = cross(
        held_ref, high_ref, low_ref, down_ref, start, high_o, low_o, spread_ref, best_ref, total_ref
    )


def second_kernel(
    held_ref, high_ref, low_ref, down_ref, best_ref, row_ref, col_ref, out_ref, high_o, low_o, spread_ref, total_ref
):
    core = lax.axis_index("core")
    rows, cols = cross(
        held_ref,
        high_ref,
        low_ref,
        down_ref,
        (1 - core) * high_o.shape[0],
        high_o,
        low_o,
        spread_ref,
        best_ref,
        total_ref,
    )
    chips = out_ref.shape[0] // 4
    first = core == 0
    own = jnp.where(first, row_ref[...], rows), jnp.where(first, rows, row_ref[...])
    other = col_ref[...], cols
    for h in range(2):
        out_ref[h * chips : (h + 1) * chips, :] = jnp.where(first, own[h], other[h])
        out_ref[(2 + h) * chips : (3 + h) * chips, :] = jnp.where(first, other[h], own[h])


def pick_kernel(answer_ref, cl_ref, rank_ref, out_ref):
    lanes = answer_ref.shape[1]
    chips = answer_ref.shape[0] // 2
    count = cl_ref.shape[1]
    owner = (lax.broadcasted_iota(jnp.int32, (chips, count), 0) == cl_ref[...]).astype(
        jnp.float32
    ).astype(jnp.bfloat16)
    tn = (((0,), (0,)), ((), ()))
    answer = jnp.maximum(answer_ref[:chips, :], answer_ref[chips:, :])
    high, rest = split(answer)
    middle, low = split(answer - high.astype(jnp.float32))
    by_rank = dot_f32(high, owner, tn) + (dot_f32(middle, owner, tn) + dot_f32(low, owner, tn))
    at_rank = lax.broadcasted_iota(jnp.int32, (lanes, count), 0) == rank_ref[...]
    out_ref[...] = jnp.sum(jnp.where(at_rank, by_rank, 0.0), axis=0, keepdims=True)


def on_device(embeddings, clusters, indices):
    count, width = embeddings.shape
    chip_axes = ("z", "y", "x_hi", "x_lo")
    chips, slots, lanes = 64, 16, 128
    rows = chips * slots
    length = slots * width // lanes + 1
    cl = clusters.reshape(1, count)
    ix = indices.reshape(1, count)
    f32 = functools.partial(jax.ShapeDtypeStruct, dtype=jnp.float32)
    bf16 = functools.partial(jax.ShapeDtypeStruct, dtype=jnp.bfloat16)
    dma = pltpu.SemaphoreType.DMA
    sending, rank = pl.pallas_call(
        place_kernel,
        out_shape=(f32((chips * length, lanes)), jax.ShapeDtypeStruct((1, count), jnp.int32)),
        in_specs=[pl.BlockSpec(memory_space=pltpu.HBM)] * 3,
        out_specs=(VMEM, VMEM),
        scratch_shapes=[
            pltpu.VMEM((count, width), jnp.float32),
            pltpu.VMEM((1, count), jnp.int32),
            pltpu.VMEM((1, count), jnp.int32),
            dma((2,)),
            dma,
            dma,
        ],
        compiler_params=PARAMS,
        name="place",
    )(*(pltpu.with_memory_space_constraint(v, pltpu.HBM) for v in (embeddings, cl, ix)))
    held = lax.all_to_all(
        sending.reshape(chips * length, 1, lanes), chip_axes, split_axis=0, concat_axis=0, tiled=True
    )
    part = chips * length // 2
    arrived = [
        lax.ppermute(held[h * part : (h + 1) * part], "core", [(0, 1), (1, 0)]).reshape(part, lanes)
        for h in range(2)
    ]
    held = held.reshape(chips * length, lanes)
    flops = 2 * rows * rows * width * 3
    high, low, down, best = pl.pallas_call(
        own_kernel,
        out_shape=(
            bf16((rows, width)),
            bf16((rows, width)),
            f32((rows, lanes)),
            f32((rows, lanes)),
        ),
        in_specs=[VMEM],
        out_specs=(VMEM,) * 4,
        scratch_shapes=[pltpu.VMEM((rows, lanes), jnp.float32)],
        compiler_params=PARAMS,
        cost_estimate=pl.CostEstimate(flops=flops, bytes_accessed=8 << 20, transcendentals=0),
        name="own",
    )(held)
    half = rows // 2
    scratch = [
        pltpu.VMEM((half, width), jnp.bfloat16),
        pltpu.VMEM((half, width), jnp.bfloat16),
        pltpu.VMEM((half, lanes), jnp.float32),
        pltpu.VMEM((half, lanes), jnp.float32),
    ]
    cost = pl.CostEstimate(flops=flops // 4, bytes_accessed=2 << 20, transcendentals=0)
    row, col = pl.pallas_call(
        first_kernel,
        out_shape=(f32((chips // 2, lanes)),) * 2,
        in_specs=[VMEM] * 5,
        out_specs=(VMEM,) * 2,
        scratch_shapes=scratch,
        compiler_params=PARAMS,
        cost_estimate=cost,
        name="first",
    )(arrived[0], high, low, down, best)
    result = pl.pallas_call(
        second_kernel,
        out_shape=f32((2 * chips, lanes)),
        in_specs=[VMEM] * 7,
        out_specs=VMEM,
        scratch_shapes=scratch,
        compiler_params=PARAMS,
        cost_estimate=cost,
        name="second",
    )(arrived[1], high, low, down, best, row, col)
    answer = lax.all_to_all(
        result.reshape(2 * chips, 1, lanes), ("core",) + chip_axes, split_axis=0, concat_axis=0, tiled=True
    ).reshape(2 * chips, lanes)
    out = pl.pallas_call(
        pick_kernel,
        out_shape=f32((1, count)),
        in_specs=[VMEM] * 3,
        out_specs=VMEM,
        compiler_params=PARAMS,
        name="pick",
    )(answer, cl, rank)
    return out.reshape(count)


def solution(mesh):
    fine = Mesh(mesh.devices.reshape(4, 2, 2, 2, 4), POINTS)
    return jax.shard_map(
        on_device,
        mesh=fine,
        in_specs=(P(POINTS, None), P(POINTS), P(POINTS)),
        out_specs=P(POINTS),
        check_vma=False,
    )
```

```python
import functools

import jax
import jax.numpy as jnp
from jax import lax
from jax.experimental import pallas as pl
from jax.experimental.pallas import tpu as pltpu
from jax.sharding import Mesh, PartitionSpec as P

EPS = 1e-06
EMPTY = 1e9
TILE = 256
POINTS = ("y", "x_hi", "core", "x_lo", "z")
NT = (((1,), (1,)), ((), ()))
VMEM = pl.BlockSpec(memory_space=pltpu.VMEM)
PARAMS = pltpu.CompilerParams(vmem_limit_bytes=20 * 1024 * 1024)


def split(values):
    high = values.astype(jnp.bfloat16)
    low = (values - high.astype(jnp.float32)).astype(jnp.bfloat16)
    return high, low


def dot_f32(a, b, dims):
    return lax.dot_general(a, b, dims, preferred_element_type=jnp.float32)


def place_kernel(emb_hbm, cl_hbm, ix_hbm, send_ref, rank_ref, emb, cl_ref, ix_ref, emb_sem, cl_sem, ix_sem):
    count, width = emb.shape
    slots, lanes, turn, chips = 16, 128, 8, 64
    parts = 2
    step = count // parts
    copies = [
        pltpu.make_async_copy(
            emb_hbm.at[pl.ds(p * step, step)], emb.at[pl.ds(p * step, step)], emb_sem.at[p]
        )
        for p in range(parts)
    ]
    cl_copy = pltpu.make_async_copy(cl_hbm, cl_ref, cl_sem)
    ix_copy = pltpu.make_async_copy(ix_hbm, ix_ref, ix_sem)
    cl_copy.start()
    ix_copy.start()
    for copy in copies:
        copy.start()
    cl_copy.wait()
    ix_copy.wait()
    cl = cl_ref[...]
    ix = ix_ref[...]
    along = jnp.broadcast_to(cl.astype(jnp.float32), (count, count))
    down = along.T
    before = lax.broadcasted_iota(jnp.int32, (count, count), 0) < lax.broadcasted_iota(
        jnp.int32, (count, count), 1
    )
    rank = jnp.sum(
        jnp.where((along == down) & before, 1.0, 0.0), axis=0, keepdims=True
    ).astype(jnp.int32)
    rank_ref[...] = rank
    target = cl * slots + (rank + cl % turn) % slots
    owner = (lax.broadcasted_iota(jnp.int32, (chips, count), 0) == cl).astype(
        jnp.float32
    ).astype(jnp.bfloat16)
    at_rank = lax.broadcasted_iota(jnp.int32, (lanes, count), 0) == rank
    tag = ix + 1
    tag_high = jnp.where(at_rank, (tag // 256).astype(jnp.float32), 0.0).astype(jnp.bfloat16)
    tag_low = jnp.where(at_rank, (tag % 256).astype(jnp.float32), 0.0).astype(jnp.bfloat16)
    tags = 256.0 * dot_f32(owner, tag_high, NT) + dot_f32(owner, tag_low, NT)
    highs, lows = [], []
    for p in range(parts):
        copies[p].wait()
        x = emb[p * step : (p + 1) * step, :]
        unit = x * lax.rsqrt(jnp.sum(x * x, axis=1, keepdims=True) + EPS)
        high, low = split(unit)
        highs.append(high)
        lows.append(low)
    high = jnp.concatenate(highs, axis=0)
    low = jnp.concatenate(lows, axis=0)
    mm = (((1,), (0,)), ((), ()))
    chunks = width // lanes
    sub = lax.broadcasted_iota(jnp.int32, (8, lanes), 0)
    block = 2 * turn * slots
    for r in range(0, chips * slots, block):
        place = (
            lax.broadcasted_iota(jnp.int32, (block, count), 0) + r == target
        ).astype(jnp.float32).astype(jnp.bfloat16)
        moved = dot_f32(place, high, mm) + dot_f32(place, low, mm)
        for g in range(2):
            base = (r // slots + g * turn) * (chunks * slots + 1)

            def head(a, k):
                at = (g * turn + a) * slots
                return moved[at : at + 8, k * lanes : (k + 1) * lanes]

            def tag_of(a):
                at = r // slots + g * turn + a
                return jnp.broadcast_to(tags[at : at + 1, :], (8, lanes))

            for a in range(turn):
                for k in range(chunks):
                    tile = head(a, k)
                    if k > 0 and a > 0:
                        tile = jnp.where(sub < a, head(a, k - 1), tile)
                    elif k == 0 and a > 0:
                        tile = jnp.where(sub == a - 1, tag_of(a - 1), tile)
                        if a > 1:
                            tile = jnp.where(sub < a - 1, head(a - 1, chunks - 1), tile)
                    at = base + 8 * (12 * a + 2 * k)
                    send_ref[at : at + 8, :] = tile
                    whole = (g * turn + a) * slots + 8
                    send_ref[at + 8 : at + 16, :] = moved[
                        whole : whole + 8, k * lanes : (k + 1) * lanes
                    ]
            at = base + 8 * 12 * turn
            send_ref[at : at + 8, :] = jnp.where(
                sub == turn - 1, tag_of(turn - 1), head(turn - 1, chunks - 1)
            )


def slot_of(rows, lanes):
    row = lax.broadcasted_iota(jnp.int32, (rows, lanes), 0)
    return (row % 16 + 16 - (row // 16) % 8) % 16


def unpack(held_ref, first, chips, high_ref, low_ref, spread_ref):
    slots, lanes, turn = 16, 128, 8
    chunks = high_ref.shape[1] // lanes
    sub = lax.broadcasted_iota(jnp.int32, (8, lanes), 0)
    for s in range(first, first + chips):
        a = s % turn
        base = 97 * (s - a)

        def tile(t):
            at = base + 8 * t
            return held_ref[at : at + 8, :]

        for k in range(chunks):
            t = 12 * a + 2 * k
            top = tile(t)
            if a > 0:
                top = jnp.where(sub < a, tile(t + 2), top)
            high, low = split(jnp.concatenate([top, tile(t + 1)], axis=0))
            high_ref[s * slots : (s + 1) * slots, k * lanes : (k + 1) * lanes] = high
            low_ref[s * slots : (s + 1) * slots, k * lanes : (k + 1) * lanes] = low
        at = base + 97 * a + 96
        spread_ref[s * slots : (s + 1) * slots, :] = jnp.broadcast_to(
            held_ref[at : at + 1, :], (slots, lanes)
        )


def tags_of(spread, slot):
    lanes = spread.shape[1]
    lane = lax.broadcasted_iota(jnp.int32, spread.shape, 1)
    down = jnp.sum(jnp.where(lane == slot, spread, 0.0), axis=1, keepdims=True)
    down = jnp.where(down == 0.0, EMPTY, down)
    return jnp.broadcast_to(down, spread.shape)


def products(high_i, low_i, high_j, low_j):
    return dot_f32(high_i, high_j, NT) + (
        dot_f32(high_i, low_j, NT) + dot_f32(low_i, high_j, NT)
    )


def by_slot(best, slot):
    slots = 16
    rows, lanes = best.shape
    lane = lax.broadcasted_iota(jnp.int32, (rows, lanes), 1)
    picked = jnp.where(lane == slot, best, -2.0).reshape(rows // slots, slots, lanes)
    return jnp.max(picked, axis=1)


def own_kernel(held_ref, high_ref, low_ref, down_ref, best_ref, spread_ref):
    rows, lanes = down_ref.shape
    slot = slot_of(TILE, lanes)
    for j in range(0, rows, TILE):
        sj = slice(j, j + TILE)
        unpack(held_ref, j // 16, TILE // 16, high_ref, low_ref, spread_ref)
        down_j = tags_of(spread_ref[sj, :], slot)
        down_ref[sj, :] = down_j
        best_ref[sj, :] = jnp.full((TILE, lanes), -1.0, jnp.float32)
        end = j + TILE
        sims = products(high_ref[:end, :], low_ref[:end, :], high_ref[sj, :], low_ref[sj, :])
        down = down_ref[:end, :]
        best = best_ref[:end, :]
        over = []
        for c in range(0, TILE, lanes):
            col_ix = down_j[c : c + lanes, :].T[:1, :]
            part = sims[:, c : c + lanes]
            best = jnp.maximum(best, jnp.where(col_ix < down, part, -1.0))
            if j > 0:
                top = jnp.max(
                    jnp.where(down[:j] < col_ix, part[:j], -1.0), axis=0, keepdims=True
                )
                over.append(jnp.broadcast_to(top, (lanes, lanes)).T)
        if j > 0:
            best_ref[:j, :] = best[:j]
            best_ref[sj, :] = jnp.maximum(best[j:], jnp.concatenate(over, axis=0))
        else:
            best_ref[sj, :] = best


def cross(held_ref, high_ref, low_ref, down_ref, parts, high_o, low_o, spread_ref, get, put):
    half, lanes = high_o.shape[0], down_ref.shape[1]
    slot = slot_of(TILE, lanes)
    cols, over = {}, {}

    def finish(i, rows, j, sims):
        down = down_ref[rows, :]
        best = get(i, j)
        for n, col_ix in enumerate(cols[j]):
            part = sims[:, n * lanes : (n + 1) * lanes]
            best = jnp.maximum(best, jnp.where(col_ix < down, part, -1.0))
            top = jnp.where(down < col_ix, part, -1.0).reshape(TILE // 8, 8, lanes)
            top = jnp.max(top, axis=0)
            over[j, n] = top if (j, n) not in over else jnp.maximum(over[j, n], top)
        put(i, j, best)

    waiting = None
    for j in range(half // TILE):
        sj = slice(j * TILE, (j + 1) * TILE)
        unpack(held_ref, sj.start // 16, TILE // 16, high_o, low_o, spread_ref)
        down_j = tags_of(spread_ref[sj, :], slot)
        cols[j] = [down_j[c : c + lanes, :].T[:1, :] for c in range(0, TILE, lanes)]
        for i, start in enumerate(parts(j)):
            rows = pl.ds(pl.multiple_of(start, TILE), TILE)
            sims = products(high_ref[rows, :], low_ref[rows, :], high_o[sj, :], low_o[sj, :])
            if waiting is not None:
                finish(*waiting)
            waiting = i, rows, j, sims
    finish(*waiting)
    out = []
    for j in range(half // TILE):
        wide = [
            jnp.broadcast_to(jnp.max(over[j, n], axis=0, keepdims=True), (lanes, lanes)).T
            for n in range(TILE // lanes)
        ]
        out.append(by_slot(jnp.concatenate(wide, axis=0), slot))
    return jnp.concatenate(out, axis=0)


def swapped(core, blocks):
    lanes = blocks[0].shape[1]
    slot = slot_of(TILE, lanes)
    one, two = (
        by_slot(jnp.broadcast_to(jnp.max(best, axis=1, keepdims=True), best.shape), slot)
        for best in blocks
    )
    return jnp.concatenate(
        [jnp.where(core == 0, one, two), jnp.where(core == 0, two, one)], axis=0
    )


def first_kernel(
    held_ref, high_ref, low_ref, down_ref, best_ref, row_ref, col_ref, total_ref, high_o, low_o, spread_ref
):
    half = high_o.shape[0]
    core = lax.axis_index("core")
    shared = [core * TILE, (1 - core) * TILE]
    done = {}

    def get(i, j):
        if i == 2:
            return best_ref[pl.ds(pl.multiple_of(shared[j], TILE), TILE), :]
        at = i * TILE
        return best_ref[half + at : half + at + TILE, :] if j == 0 else total_ref[at : at + TILE, :]

    def put(i, j, best):
        if i == 2:
            done[j] = best
        else:
            total_ref[i * TILE : (i + 1) * TILE, :] = best

    col_ref[...] = cross(
        held_ref,
        high_ref,
        low_ref,
        down_ref,
        lambda j: [half, half + TILE, shared[j]],
        high_o,
        low_o,
        spread_ref,
        get,
        put,
    )
    row_ref[...] = swapped(core, [done[0], done[1]])


def second_kernel(
    held_ref, high_ref, low_ref, down_ref, total_ref, row_ref, col_ref, out_ref, high_o, low_o, spread_ref
):
    half = high_o.shape[0]
    core = lax.axis_index("core")
    shared = [core * TILE, (1 - core) * TILE]
    done = {}
    cols = cross(
        held_ref,
        high_ref,
        low_ref,
        down_ref,
        lambda j: [half + shared[j]],
        high_o,
        low_o,
        spread_ref,
        lambda i, j: total_ref[pl.ds(pl.multiple_of(shared[j], TILE), TILE), :],
        lambda i, j, best: done.update({j: best}),
    )
    own = row_ref[...], swapped(core, [done[0], done[1]])
    other = col_ref[...], cols
    chips = out_ref.shape[0] // 4
    for h in range(2):
        out_ref[h * chips : (h + 1) * chips, :] = jnp.where(core == 0, own[h], other[h])
        out_ref[(2 + h) * chips : (3 + h) * chips, :] = jnp.where(core == 0, other[h], own[h])


def pick_kernel(answer_ref, cl_ref, rank_ref, out_ref):
    lanes = answer_ref.shape[1]
    chips = answer_ref.shape[0] // 2
    count = cl_ref.shape[1]
    owner = (lax.broadcasted_iota(jnp.int32, (chips, count), 0) == cl_ref[...]).astype(
        jnp.float32
    ).astype(jnp.bfloat16)
    tn = (((0,), (0,)), ((), ()))
    answer = jnp.maximum(answer_ref[:chips, :], answer_ref[chips:, :])
    high, rest = split(answer)
    middle, low = split(answer - high.astype(jnp.float32))
    by_rank = dot_f32(high, owner, tn) + (dot_f32(middle, owner, tn) + dot_f32(low, owner, tn))
    at_rank = lax.broadcasted_iota(jnp.int32, (lanes, count), 0) == rank_ref[...]
    out_ref[...] = jnp.sum(jnp.where(at_rank, by_rank, 0.0), axis=0, keepdims=True)


def on_device(embeddings, clusters, indices):
    count, width = embeddings.shape
    chip_axes = ("z", "y", "x_hi", "x_lo")
    chips, slots, lanes = 64, 16, 128
    rows = chips * slots
    length = slots * width // lanes + 1
    cl = clusters.reshape(1, count)
    ix = indices.reshape(1, count)
    f32 = functools.partial(jax.ShapeDtypeStruct, dtype=jnp.float32)
    bf16 = functools.partial(jax.ShapeDtypeStruct, dtype=jnp.bfloat16)
    dma = pltpu.SemaphoreType.DMA
    sending, rank = pl.pallas_call(
        place_kernel,
        out_shape=(f32((chips * length, lanes)), jax.ShapeDtypeStruct((1, count), jnp.int32)),
        in_specs=[pl.BlockSpec(memory_space=pltpu.HBM)] * 3,
        out_specs=(VMEM, VMEM),
        scratch_shapes=[
            pltpu.VMEM((count, width), jnp.float32),
            pltpu.VMEM((1, count), jnp.int32),
            pltpu.VMEM((1, count), jnp.int32),
            dma((2,)),
            dma,
            dma,
        ],
        compiler_params=PARAMS,
        name="place",
    )(*(pltpu.with_memory_space_constraint(v, pltpu.HBM) for v in (embeddings, cl, ix)))
    held = lax.all_to_all(
        sending.reshape(chips * length, 1, lanes), chip_axes, split_axis=0, concat_axis=0, tiled=True
    )
    part = chips * length // 2
    arrived = [
        lax.ppermute(held[h * part : (h + 1) * part], "core", [(0, 1), (1, 0)]).reshape(part, lanes)
        for h in range(2)
    ]
    held = held.reshape(chips * length, lanes)
    flops = 2 * rows * rows * width * 3
    high, low, down, best = pl.pallas_call(
        own_kernel,
        out_shape=(
            bf16((rows, width)),
            bf16((rows, width)),
            f32((rows, lanes)),
            f32((rows, lanes)),
        ),
        in_specs=[VMEM],
        out_specs=(VMEM,) * 4,
        scratch_shapes=[pltpu.VMEM((rows, lanes), jnp.float32)],
        compiler_params=PARAMS,
        cost_estimate=pl.CostEstimate(flops=flops, bytes_accessed=8 << 20, transcendentals=0),
        name="own",
    )(held)
    half = rows // 2
    scratch = [
        pltpu.VMEM((half, width), jnp.bfloat16),
        pltpu.VMEM((half, width), jnp.bfloat16),
        pltpu.VMEM((half, lanes), jnp.float32),
    ]
    row, col, total = pl.pallas_call(
        first_kernel,
        out_shape=(f32((chips // 2, lanes)), f32((chips // 2, lanes)), f32((half, lanes))),
        in_specs=[VMEM] * 5,
        out_specs=(VMEM,) * 3,
        scratch_shapes=scratch,
        compiler_params=PARAMS,
        cost_estimate=pl.CostEstimate(
            flops=3 * flops // 8, bytes_accessed=2 << 20, transcendentals=0
        ),
        name="first",
    )(arrived[0], high, low, down, best)
    result = pl.pallas_call(
        second_kernel,
        out_shape=f32((2 * chips, lanes)),
        in_specs=[VMEM] * 7,
        out_specs=VMEM,
        scratch_shapes=scratch,
        compiler_params=PARAMS,
        cost_estimate=pl.CostEstimate(flops=flops // 8, bytes_accessed=2 << 20, transcendentals=0),
        name="second",
    )(arrived[1], high, low, down, total, row, col)
    answer = lax.all_to_all(
        result.reshape(2 * chips, 1, lanes), ("core",) + chip_axes, split_axis=0, concat_axis=0, tiled=True
    ).reshape(2 * chips, lanes)
    out = pl.pallas_call(
        pick_kernel,
        out_shape=f32((1, count)),
        in_specs=[VMEM] * 3,
        out_specs=VMEM,
        compiler_params=PARAMS,
        name="pick",
    )(answer, cl, rank)
    return out.reshape(count)


def solution(mesh):
    fine = Mesh(mesh.devices.reshape(4, 2, 2, 2, 4), POINTS)
    return jax.shard_map(
        on_device,
        mesh=fine,
        in_specs=(P(POINTS, None), P(POINTS), P(POINTS)),
        out_specs=P(POINTS),
        check_vma=False,
    )
```

```python
import functools

import jax
import jax.numpy as jnp
from jax import lax
from jax.experimental import pallas as pl
from jax.experimental.pallas import tpu as pltpu
from jax.sharding import Mesh, PartitionSpec as P

EPS = 1e-06
EMPTY = 1e9
TILE = 256
POINTS = ("y", "x_hi", "core", "x_lo", "z")
NT = (((1,), (1,)), ((), ()))
VMEM = pl.BlockSpec(memory_space=pltpu.VMEM)
PARAMS = pltpu.CompilerParams(vmem_limit_bytes=20 * 1024 * 1024)


def split(values):
    high = values.astype(jnp.bfloat16)
    low = (values - high.astype(jnp.float32)).astype(jnp.bfloat16)
    return high, low


def dot_f32(a, b, dims):
    return lax.dot_general(a, b, dims, preferred_element_type=jnp.float32)


def place_kernel(emb_hbm, cl_hbm, ix_hbm, send_ref, rank_ref, emb, cl_ref, ix_ref, emb_sem, cl_sem, ix_sem):
    count, width = emb.shape
    slots, lanes, turn, chips = 16, 128, 8, 64
    parts = 2
    step = count // parts
    copies = [
        pltpu.make_async_copy(
            emb_hbm.at[pl.ds(p * step, step)], emb.at[pl.ds(p * step, step)], emb_sem.at[p]
        )
        for p in range(parts)
    ]
    cl_copy = pltpu.make_async_copy(cl_hbm, cl_ref, cl_sem)
    ix_copy = pltpu.make_async_copy(ix_hbm, ix_ref, ix_sem)
    cl_copy.start()
    ix_copy.start()
    for copy in copies:
        copy.start()
    cl_copy.wait()
    ix_copy.wait()
    cl = cl_ref[...]
    ix = ix_ref[...]
    along = jnp.broadcast_to(cl.astype(jnp.float32), (count, count))
    down = along.T
    before = lax.broadcasted_iota(jnp.int32, (count, count), 0) < lax.broadcasted_iota(
        jnp.int32, (count, count), 1
    )
    rank = jnp.sum(
        jnp.where((along == down) & before, 1.0, 0.0), axis=0, keepdims=True
    ).astype(jnp.int32)
    rank_ref[...] = rank
    target = cl * slots + (rank + cl % turn) % slots
    owner = (lax.broadcasted_iota(jnp.int32, (chips, count), 0) == cl).astype(
        jnp.float32
    ).astype(jnp.bfloat16)
    at_rank = lax.broadcasted_iota(jnp.int32, (lanes, count), 0) == rank
    tag = ix + 1
    tag_high = jnp.where(at_rank, (tag // 256).astype(jnp.float32), 0.0).astype(jnp.bfloat16)
    tag_low = jnp.where(at_rank, (tag % 256).astype(jnp.float32), 0.0).astype(jnp.bfloat16)
    tags = 256.0 * dot_f32(owner, tag_high, NT) + dot_f32(owner, tag_low, NT)
    highs, lows = [], []
    for p in range(parts):
        copies[p].wait()
        x = emb[p * step : (p + 1) * step, :]
        unit = x * lax.rsqrt(jnp.sum(x * x, axis=1, keepdims=True) + EPS)
        high, low = split(unit)
        highs.append(high)
        lows.append(low)
    high = jnp.concatenate(highs, axis=0)
    low = jnp.concatenate(lows, axis=0)
    mm = (((1,), (0,)), ((), ()))
    chunks = width // lanes
    sub = lax.broadcasted_iota(jnp.int32, (8, lanes), 0)
    block = 2 * turn * slots
    for r in range(0, chips * slots, block):
        place = (
            lax.broadcasted_iota(jnp.int32, (block, count), 0) + r == target
        ).astype(jnp.float32).astype(jnp.bfloat16)
        moved = dot_f32(place, high, mm) + dot_f32(place, low, mm)
        for g in range(2):
            base = (r // slots + g * turn) * (chunks * slots + 1)

            def head(a, k):
                at = (g * turn + a) * slots
                return moved[at : at + 8, k * lanes : (k + 1) * lanes]

            def tag_of(a):
                at = r // slots + g * turn + a
                return jnp.broadcast_to(tags[at : at + 1, :], (8, lanes))

            for a in range(turn):
                for k in range(chunks):
                    tile = head(a, k)
                    if k > 0 and a > 0:
                        tile = jnp.where(sub < a, head(a, k - 1), tile)
                    elif k == 0 and a > 0:
                        tile = jnp.where(sub == a - 1, tag_of(a - 1), tile)
                        if a > 1:
                            tile = jnp.where(sub < a - 1, head(a - 1, chunks - 1), tile)
                    at = base + 8 * (12 * a + 2 * k)
                    send_ref[at : at + 8, :] = tile
                    whole = (g * turn + a) * slots + 8
                    send_ref[at + 8 : at + 16, :] = moved[
                        whole : whole + 8, k * lanes : (k + 1) * lanes
                    ]
            at = base + 8 * 12 * turn
            send_ref[at : at + 8, :] = jnp.where(
                sub == turn - 1, tag_of(turn - 1), head(turn - 1, chunks - 1)
            )


def slot_of(rows, lanes):
    row = lax.broadcasted_iota(jnp.int32, (rows, lanes), 0)
    return (row % 16 + 16 - (row // 16) % 8) % 16


def unpack(held_ref, first, chips, high_ref, low_ref, spread_ref):
    slots, lanes, turn = 16, 128, 8
    chunks = high_ref.shape[1] // lanes
    sub = lax.broadcasted_iota(jnp.int32, (8, lanes), 0)
    for s in range(first, first + chips):
        a = s % turn
        base = 97 * (s - a)

        def tile(t):
            at = base + 8 * t
            return held_ref[at : at + 8, :]

        for k in range(chunks):
            t = 12 * a + 2 * k
            top = tile(t)
            if a > 0:
                top = jnp.where(sub < a, tile(t + 2), top)
            high, low = split(jnp.concatenate([top, tile(t + 1)], axis=0))
            high_ref[s * slots : (s + 1) * slots, k * lanes : (k + 1) * lanes] = high
            low_ref[s * slots : (s + 1) * slots, k * lanes : (k + 1) * lanes] = low
        at = base + 97 * a + 96
        spread_ref[s * slots : (s + 1) * slots, :] = jnp.broadcast_to(
            held_ref[at : at + 1, :], (slots, lanes)
        )


def tags_of(spread, slot):
    lanes = spread.shape[1]
    lane = lax.broadcasted_iota(jnp.int32, spread.shape, 1)
    down = jnp.sum(jnp.where(lane == slot, spread, 0.0), axis=1, keepdims=True)
    down = jnp.where(down == 0.0, EMPTY, down)
    return jnp.broadcast_to(down, spread.shape)


def products(high_i, low_i, high_j, low_j):
    return dot_f32(high_i, high_j, NT) + (
        dot_f32(high_i, low_j, NT) + dot_f32(low_i, high_j, NT)
    )


def by_slot(best, slot):
    slots = 16
    rows, lanes = best.shape
    lane = lax.broadcasted_iota(jnp.int32, (rows, lanes), 1)
    picked = jnp.where(lane == slot, best, -2.0).reshape(rows // slots, slots, lanes)
    return jnp.max(picked, axis=1)


def own_kernel(held_ref, high_ref, low_ref, down_ref, best_ref, spread_ref):
    rows, lanes = down_ref.shape
    slot = slot_of(TILE, lanes)
    for j in range(0, rows, TILE):
        sj = slice(j, j + TILE)
        unpack(held_ref, j // 16, TILE // 16, high_ref, low_ref, spread_ref)
        down_j = tags_of(spread_ref[sj, :], slot)
        down_ref[sj, :] = down_j
        cols = [down_j[c : c + lanes, :].T[:1, :] for c in range(0, TILE, lanes)]
        high_j, low_j = high_ref[sj, :], low_ref[sj, :]
        mixed = dot_f32(high_j, low_j, NT)
        square = dot_f32(high_j, high_j, NT) + (mixed + mixed.T)
        best_j = jnp.full((TILE, lanes), -1.0, jnp.float32)
        for n, col_ix in enumerate(cols):
            part = square[:, n * lanes : (n + 1) * lanes]
            best_j = jnp.maximum(best_j, jnp.where(col_ix < down_j, part, -1.0))
        if j > 0:
            sims = products(high_ref[:j, :], low_ref[:j, :], high_j, low_j)
            down = down_ref[:j, :]
            best = best_ref[:j, :]
            over = []
            for n, col_ix in enumerate(cols):
                part = sims[:, n * lanes : (n + 1) * lanes]
                best = jnp.maximum(best, jnp.where(col_ix < down, part, -1.0))
                top = jnp.max(jnp.where(down < col_ix, part, -1.0), axis=0, keepdims=True)
                over.append(jnp.broadcast_to(top, (lanes, lanes)).T)
            best_ref[:j, :] = best
            best_j = jnp.maximum(best_j, jnp.concatenate(over, axis=0))
        best_ref[sj, :] = best_j


def cross(held_ref, high_ref, low_ref, down_ref, parts, high_o, low_o, spread_ref, get, put):
    half, lanes = high_o.shape[0], down_ref.shape[1]
    slot = slot_of(TILE, lanes)
    cols, over = {}, {}

    def finish(i, rows, j, sims):
        down = down_ref[rows, :]
        best = get(i, j)
        for n, col_ix in enumerate(cols[j]):
            part = sims[:, n * lanes : (n + 1) * lanes]
            best = jnp.maximum(best, jnp.where(col_ix < down, part, -1.0))
            top = jnp.where(down < col_ix, part, -1.0).reshape(TILE // 8, 8, lanes)
            top = jnp.max(top, axis=0)
            over[j, n] = top if (j, n) not in over else jnp.maximum(over[j, n], top)
        put(i, j, best)

    waiting = None
    for j in range(half // TILE):
        sj = slice(j * TILE, (j + 1) * TILE)
        unpack(held_ref, sj.start // 16, TILE // 16, high_o, low_o, spread_ref)
        down_j = tags_of(spread_ref[sj, :], slot)
        cols[j] = [down_j[c : c + lanes, :].T[:1, :] for c in range(0, TILE, lanes)]
        for i, start in enumerate(parts(j)):
            rows = pl.ds(pl.multiple_of(start, TILE), TILE)
            sims = products(high_ref[rows, :], low_ref[rows, :], high_o[sj, :], low_o[sj, :])
            if waiting is not None:
                finish(*waiting)
            waiting = i, rows, j, sims
    finish(*waiting)
    out = []
    for j in range(half // TILE):
        wide = [
            jnp.broadcast_to(jnp.max(over[j, n], axis=0, keepdims=True), (lanes, lanes)).T
            for n in range(TILE // lanes)
        ]
        out.append(by_slot(jnp.concatenate(wide, axis=0), slot))
    return jnp.concatenate(out, axis=0)


def swapped(core, blocks):
    lanes = blocks[0].shape[1]
    slot = slot_of(TILE, lanes)
    one, two = (
        by_slot(jnp.broadcast_to(jnp.max(best, axis=1, keepdims=True), best.shape), slot)
        for best in blocks
    )
    return jnp.concatenate(
        [jnp.where(core == 0, one, two), jnp.where(core == 0, two, one)], axis=0
    )


def first_kernel(
    held_ref, high_ref, low_ref, down_ref, best_ref, row_ref, col_ref, total_ref, high_o, low_o, spread_ref
):
    half = high_o.shape[0]
    core = lax.axis_index("core")
    shared = [core * TILE, (1 - core) * TILE]
    done = {}

    def get(i, j):
        if i == 2:
            return best_ref[pl.ds(pl.multiple_of(shared[j], TILE), TILE), :]
        at = i * TILE
        return best_ref[half + at : half + at + TILE, :] if j == 0 else total_ref[at : at + TILE, :]

    def put(i, j, best):
        if i == 2:
            done[j] = best
        else:
            total_ref[i * TILE : (i + 1) * TILE, :] = best

    col_ref[...] = cross(
        held_ref,
        high_ref,
        low_ref,
        down_ref,
        lambda j: [half, half + TILE, shared[j]],
        high_o,
        low_o,
        spread_ref,
        get,
        put,
    )
    row_ref[...] = swapped(core, [done[0], done[1]])


def second_kernel(
    held_ref, high_ref, low_ref, down_ref, total_ref, row_ref, col_ref, out_ref, high_o, low_o, spread_ref
):
    half = high_o.shape[0]
    core = lax.axis_index("core")
    shared = [core * TILE, (1 - core) * TILE]
    done = {}
    cols = cross(
        held_ref,
        high_ref,
        low_ref,
        down_ref,
        lambda j: [half + shared[j]],
        high_o,
        low_o,
        spread_ref,
        lambda i, j: total_ref[pl.ds(pl.multiple_of(shared[j], TILE), TILE), :],
        lambda i, j, best: done.update({j: best}),
    )
    own = row_ref[...], swapped(core, [done[0], done[1]])
    other = col_ref[...], cols
    chips = out_ref.shape[0] // 4
    for h in range(2):
        out_ref[h * chips : (h + 1) * chips, :] = jnp.where(core == 0, own[h], other[h])
        out_ref[(2 + h) * chips : (3 + h) * chips, :] = jnp.where(core == 0, other[h], own[h])


def pick_kernel(answer_ref, cl_ref, rank_ref, out_ref):
    lanes = answer_ref.shape[1]
    chips = answer_ref.shape[0] // 2
    count = cl_ref.shape[1]
    owner = (lax.broadcasted_iota(jnp.int32, (chips, count), 0) == cl_ref[...]).astype(
        jnp.float32
    ).astype(jnp.bfloat16)
    tn = (((0,), (0,)), ((), ()))
    answer = jnp.maximum(answer_ref[:chips, :], answer_ref[chips:, :])
    high, rest = split(answer)
    middle, low = split(answer - high.astype(jnp.float32))
    by_rank = dot_f32(high, owner, tn) + (dot_f32(middle, owner, tn) + dot_f32(low, owner, tn))
    at_rank = lax.broadcasted_iota(jnp.int32, (lanes, count), 0) == rank_ref[...]
    out_ref[...] = jnp.sum(jnp.where(at_rank, by_rank, 0.0), axis=0, keepdims=True)


def on_device(embeddings, clusters, indices):
    count, width = embeddings.shape
    chip_axes = ("z", "y", "x_hi", "x_lo")
    chips, slots, lanes = 64, 16, 128
    rows = chips * slots
    length = slots * width // lanes + 1
    cl = clusters.reshape(1, count)
    ix = indices.reshape(1, count)
    f32 = functools.partial(jax.ShapeDtypeStruct, dtype=jnp.float32)
    bf16 = functools.partial(jax.ShapeDtypeStruct, dtype=jnp.bfloat16)
    dma = pltpu.SemaphoreType.DMA
    sending, rank = pl.pallas_call(
        place_kernel,
        out_shape=(f32((chips * length, lanes)), jax.ShapeDtypeStruct((1, count), jnp.int32)),
        in_specs=[pl.BlockSpec(memory_space=pltpu.HBM)] * 3,
        out_specs=(VMEM, VMEM),
        scratch_shapes=[
            pltpu.VMEM((count, width), jnp.float32),
            pltpu.VMEM((1, count), jnp.int32),
            pltpu.VMEM((1, count), jnp.int32),
            dma((2,)),
            dma,
            dma,
        ],
        compiler_params=PARAMS,
        name="place",
    )(*(pltpu.with_memory_space_constraint(v, pltpu.HBM) for v in (embeddings, cl, ix)))
    held = lax.all_to_all(
        sending.reshape(chips * length, 1, lanes), chip_axes, split_axis=0, concat_axis=0, tiled=True
    )
    part = chips * length // 2
    arrived = [
        lax.ppermute(held[h * part : (h + 1) * part], "core", [(0, 1), (1, 0)]).reshape(part, lanes)
        for h in range(2)
    ]
    held = held.reshape(chips * length, lanes)
    flops = 2 * rows * rows * width * 3
    high, low, down, best = pl.pallas_call(
        own_kernel,
        out_shape=(
            bf16((rows, width)),
            bf16((rows, width)),
            f32((rows, lanes)),
            f32((rows, lanes)),
        ),
        in_specs=[VMEM],
        out_specs=(VMEM,) * 4,
        scratch_shapes=[pltpu.VMEM((rows, lanes), jnp.float32)],
        compiler_params=PARAMS,
        cost_estimate=pl.CostEstimate(flops=flops, bytes_accessed=8 << 20, transcendentals=0),
        name="own",
    )(held)
    half = rows // 2
    scratch = [
        pltpu.VMEM((half, width), jnp.bfloat16),
        pltpu.VMEM((half, width), jnp.bfloat16),
        pltpu.VMEM((half, lanes), jnp.float32),
    ]
    row, col, total = pl.pallas_call(
        first_kernel,
        out_shape=(f32((chips // 2, lanes)), f32((chips // 2, lanes)), f32((half, lanes))),
        in_specs=[VMEM] * 5,
        out_specs=(VMEM,) * 3,
        scratch_shapes=scratch,
        compiler_params=PARAMS,
        cost_estimate=pl.CostEstimate(
            flops=3 * flops // 8, bytes_accessed=2 << 20, transcendentals=0
        ),
        name="first",
    )(arrived[0], high, low, down, best)
    result = pl.pallas_call(
        second_kernel,
        out_shape=f32((2 * chips, lanes)),
        in_specs=[VMEM] * 7,
        out_specs=VMEM,
        scratch_shapes=scratch,
        compiler_params=PARAMS,
        cost_estimate=pl.CostEstimate(flops=flops // 8, bytes_accessed=2 << 20, transcendentals=0),
        name="second",
    )(arrived[1], high, low, down, total, row, col)
    answer = lax.all_to_all(
        result.reshape(2 * chips, 1, lanes), ("core",) + chip_axes, split_axis=0, concat_axis=0, tiled=True
    ).reshape(2 * chips, lanes)
    out = pl.pallas_call(
        pick_kernel,
        out_shape=f32((1, count)),
        in_specs=[VMEM] * 3,
        out_specs=VMEM,
        compiler_params=PARAMS,
        name="pick",
    )(answer, cl, rank)
    return out.reshape(count)


def solution(mesh):
    fine = Mesh(mesh.devices.reshape(4, 2, 2, 2, 4), POINTS)
    return jax.shard_map(
        on_device,
        mesh=fine,
        in_specs=(P(POINTS, None), P(POINTS), P(POINTS)),
        out_specs=P(POINTS),
        check_vma=False,
    )
```

```python
import functools

import jax
import jax.numpy as jnp
from jax import lax
from jax.experimental import pallas as pl
from jax.experimental.pallas import tpu as pltpu
from jax.sharding import Mesh, PartitionSpec as P

EPS = 1e-06
EMPTY = 1e9
TILE = 256
POINTS = ("y", "x_hi", "core", "x_lo", "z")
NT = (((1,), (1,)), ((), ()))
VMEM = pl.BlockSpec(memory_space=pltpu.VMEM)
PARAMS = pltpu.CompilerParams(vmem_limit_bytes=20 * 1024 * 1024)


def split(values):
    high = values.astype(jnp.bfloat16)
    low = (values - high.astype(jnp.float32)).astype(jnp.bfloat16)
    return high, low


def dot_f32(a, b, dims):
    return lax.dot_general(a, b, dims, preferred_element_type=jnp.float32)


def place_kernel(emb_hbm, cl_hbm, ix_hbm, send_ref, rank_ref, emb, cl_ref, ix_ref, emb_sem, cl_sem, ix_sem):
    count, width = emb.shape
    slots, lanes, turn, chips = 16, 128, 8, 64
    parts = 2
    step = count // parts
    copies = [
        pltpu.make_async_copy(
            emb_hbm.at[pl.ds(p * step, step)], emb.at[pl.ds(p * step, step)], emb_sem.at[p]
        )
        for p in range(parts)
    ]
    cl_copy = pltpu.make_async_copy(cl_hbm, cl_ref, cl_sem)
    ix_copy = pltpu.make_async_copy(ix_hbm, ix_ref, ix_sem)
    cl_copy.start()
    ix_copy.start()
    for copy in copies:
        copy.start()
    cl_copy.wait()
    ix_copy.wait()
    cl = cl_ref[...]
    ix = ix_ref[...]
    along = jnp.broadcast_to(cl.astype(jnp.float32), (count, count))
    down = along.T
    before = lax.broadcasted_iota(jnp.int32, (count, count), 0) < lax.broadcasted_iota(
        jnp.int32, (count, count), 1
    )
    rank = jnp.sum(
        jnp.where((along == down) & before, 1.0, 0.0), axis=0, keepdims=True
    ).astype(jnp.int32)
    rank_ref[...] = rank
    target = cl * slots + (rank + cl % turn) % slots
    owner = (lax.broadcasted_iota(jnp.int32, (chips, count), 0) == cl).astype(
        jnp.float32
    ).astype(jnp.bfloat16)
    at_rank = lax.broadcasted_iota(jnp.int32, (lanes, count), 0) == rank
    tag = ix + 1
    tag_high = jnp.where(at_rank, (tag // 256).astype(jnp.float32), 0.0).astype(jnp.bfloat16)
    tag_low = jnp.where(at_rank, (tag % 256).astype(jnp.float32), 0.0).astype(jnp.bfloat16)
    tags = 256.0 * dot_f32(owner, tag_high, NT) + dot_f32(owner, tag_low, NT)
    highs, lows = [], []
    for p in range(parts):
        copies[p].wait()
        x = emb[p * step : (p + 1) * step, :]
        unit = x * lax.rsqrt(jnp.sum(x * x, axis=1, keepdims=True) + EPS)
        high, low = split(unit)
        highs.append(high)
        lows.append(low)
    high = jnp.concatenate(highs, axis=0)
    low = jnp.concatenate(lows, axis=0)
    mm = (((1,), (0,)), ((), ()))
    chunks = width // lanes
    sub = lax.broadcasted_iota(jnp.int32, (8, lanes), 0)
    block = 8 * turn * slots
    for r in range(0, chips * slots, block):
        place = (
            lax.broadcasted_iota(jnp.int32, (block, count), 0) + r == target
        ).astype(jnp.float32).astype(jnp.bfloat16)
        moved = dot_f32(place, high, mm) + dot_f32(place, low, mm)
        for g in range(8):
            base = (r // slots + g * turn) * (chunks * slots + 1)

            def head(a, k):
                at = (g * turn + a) * slots
                return moved[at : at + 8, k * lanes : (k + 1) * lanes]

            def tag_of(a):
                at = r // slots + g * turn + a
                return jnp.broadcast_to(tags[at : at + 1, :], (8, lanes))

            for a in range(turn):
                for k in range(chunks):
                    tile = head(a, k)
                    if k > 0 and a > 0:
                        tile = jnp.where(sub < a, head(a, k - 1), tile)
                    elif k == 0 and a > 0:
                        tile = jnp.where(sub == a - 1, tag_of(a - 1), tile)
                        if a > 1:
                            tile = jnp.where(sub < a - 1, head(a - 1, chunks - 1), tile)
                    at = base + 8 * (12 * a + 2 * k)
                    send_ref[at : at + 8, :] = tile
                    whole = (g * turn + a) * slots + 8
                    send_ref[at + 8 : at + 16, :] = moved[
                        whole : whole + 8, k * lanes : (k + 1) * lanes
                    ]
            at = base + 8 * 12 * turn
            send_ref[at : at + 8, :] = jnp.where(
                sub == turn - 1, tag_of(turn - 1), head(turn - 1, chunks - 1)
            )


def slot_of(rows, lanes):
    row = lax.broadcasted_iota(jnp.int32, (rows, lanes), 0)
    return (row % 16 + 16 - (row // 16) % 8) % 16


def unpack(held_ref, first, chips, high_ref, low_ref, spread_ref):
    slots, lanes, turn = 16, 128, 8
    chunks = high_ref.shape[1] // lanes
    sub = lax.broadcasted_iota(jnp.int32, (8, lanes), 0)
    for s in range(first, first + chips):
        a = s % turn
        base = 97 * (s - a)

        def tile(t):
            at = base + 8 * t
            return held_ref[at : at + 8, :]

        for k in range(chunks):
            t = 12 * a + 2 * k
            top = tile(t)
            if a > 0:
                top = jnp.where(sub < a, tile(t + 2), top)
            high, low = split(jnp.concatenate([top, tile(t + 1)], axis=0))
            high_ref[s * slots : (s + 1) * slots, k * lanes : (k + 1) * lanes] = high
            low_ref[s * slots : (s + 1) * slots, k * lanes : (k + 1) * lanes] = low
        at = base + 97 * a + 96
        spread_ref[s * slots : (s + 1) * slots, :] = jnp.broadcast_to(
            held_ref[at : at + 1, :], (slots, lanes)
        )


def tags_of(spread, slot):
    lanes = spread.shape[1]
    lane = lax.broadcasted_iota(jnp.int32, spread.shape, 1)
    down = jnp.sum(jnp.where(lane == slot, spread, 0.0), axis=1, keepdims=True)
    down = jnp.where(down == 0.0, EMPTY, down)
    return jnp.broadcast_to(down, spread.shape)


def products(high_i, low_i, high_j, low_j):
    return dot_f32(high_i, high_j, NT) + (
        dot_f32(high_i, low_j, NT) + dot_f32(low_i, high_j, NT)
    )


def by_slot(best, slot):
    slots = 16
    rows, lanes = best.shape
    lane = lax.broadcasted_iota(jnp.int32, (rows, lanes), 1)
    picked = jnp.where(lane == slot, best, -2.0).reshape(rows // slots, slots, lanes)
    return jnp.max(picked, axis=1)


def own_kernel(held_ref, high_ref, low_ref, down_ref, best_ref, spread_ref):
    rows, lanes = down_ref.shape
    slot = slot_of(TILE, lanes)
    for j in range(0, rows, TILE):
        sj = slice(j, j + TILE)
        unpack(held_ref, j // 16, TILE // 16, high_ref, low_ref, spread_ref)
        down_j = tags_of(spread_ref[sj, :], slot)
        down_ref[sj, :] = down_j
        cols = [down_j[c : c + lanes, :].T[:1, :] for c in range(0, TILE, lanes)]
        high_j, low_j = high_ref[sj, :], low_ref[sj, :]
        mixed = dot_f32(high_j, low_j, NT)
        square = dot_f32(high_j, high_j, NT) + (mixed + mixed.T)
        best_j = jnp.full((TILE, lanes), -1.0, jnp.float32)
        for n, col_ix in enumerate(cols):
            part = square[:, n * lanes : (n + 1) * lanes]
            best_j = jnp.maximum(best_j, jnp.where(col_ix < down_j, part, -1.0))
        if j > 0:
            sims = products(high_ref[:j, :], low_ref[:j, :], high_j, low_j)
            down = down_ref[:j, :]
            best = best_ref[:j, :]
            over = []
            for n, col_ix in enumerate(cols):
                part = sims[:, n * lanes : (n + 1) * lanes]
                best = jnp.maximum(best, jnp.where(col_ix < down, part, -1.0))
                top = jnp.max(jnp.where(down < col_ix, part, -1.0), axis=0, keepdims=True)
                over.append(jnp.broadcast_to(top, (lanes, lanes)).T)
            best_ref[:j, :] = best
            best_j = jnp.maximum(best_j, jnp.concatenate(over, axis=0))
        best_ref[sj, :] = best_j


def cross(held_ref, high_ref, low_ref, down_ref, parts, high_o, low_o, spread_ref, get, put):
    half, lanes = high_o.shape[0], down_ref.shape[1]
    slot = slot_of(TILE, lanes)
    cols, over = {}, {}

    def finish(i, rows, j, sims):
        down = down_ref[rows, :]
        best = get(i, j)
        for n, col_ix in enumerate(cols[j]):
            part = sims[:, n * lanes : (n + 1) * lanes]
            best = jnp.maximum(best, jnp.where(col_ix < down, part, -1.0))
            top = jnp.where(down < col_ix, part, -1.0).reshape(part.shape[0] // 8, 8, lanes)
            top = jnp.max(top, axis=0)
            over[j, n] = top if (j, n) not in over else jnp.maximum(over[j, n], top)
        put(i, j, best)

    waiting = None
    for j in range(half // TILE):
        sj = slice(j * TILE, (j + 1) * TILE)
        unpack(held_ref, sj.start // 16, TILE // 16, high_o, low_o, spread_ref)
        down_j = tags_of(spread_ref[sj, :], slot)
        cols[j] = [down_j[c : c + lanes, :].T[:1, :] for c in range(0, TILE, lanes)]
        for i, (start, size) in enumerate(parts(j)):
            rows = pl.ds(pl.multiple_of(start, TILE), size)
            sims = products(high_ref[rows, :], low_ref[rows, :], high_o[sj, :], low_o[sj, :])
            if waiting is not None:
                finish(*waiting)
            waiting = i, rows, j, sims
    finish(*waiting)
    out = []
    for j in range(half // TILE):
        wide = [
            jnp.broadcast_to(jnp.max(over[j, n], axis=0, keepdims=True), (lanes, lanes)).T
            for n in range(TILE // lanes)
        ]
        out.append(by_slot(jnp.concatenate(wide, axis=0), slot))
    return jnp.concatenate(out, axis=0)


def swapped(core, blocks):
    lanes = blocks[0].shape[1]
    slot = slot_of(TILE, lanes)
    one, two = (
        by_slot(jnp.broadcast_to(jnp.max(best, axis=1, keepdims=True), best.shape), slot)
        for best in blocks
    )
    return jnp.concatenate(
        [jnp.where(core == 0, one, two), jnp.where(core == 0, two, one)], axis=0
    )


def first_kernel(
    held_ref, high_ref, low_ref, down_ref, best_ref, row_ref, col_ref, total_ref, high_o, low_o, spread_ref
):
    half = high_o.shape[0]
    core = lax.axis_index("core")
    shared = [core * TILE, (1 - core) * TILE]
    done = {}

    def get(i, j):
        if i == 1:
            return best_ref[pl.ds(pl.multiple_of(shared[j], TILE), TILE), :]
        return best_ref[half:, :] if j == 0 else total_ref[...]

    def put(i, j, best):
        if i == 1:
            done[j] = best
        else:
            total_ref[...] = best

    col_ref[...] = cross(
        held_ref,
        high_ref,
        low_ref,
        down_ref,
        lambda j: [(half, half), (shared[j], TILE)],
        high_o,
        low_o,
        spread_ref,
        get,
        put,
    )
    row_ref[...] = swapped(core, [done[0], done[1]])


def second_kernel(
    held_ref, high_ref, low_ref, down_ref, total_ref, row_ref, col_ref, out_ref, high_o, low_o, spread_ref
):
    half = high_o.shape[0]
    core = lax.axis_index("core")
    shared = [core * TILE, (1 - core) * TILE]
    done = {}
    cols = cross(
        held_ref,
        high_ref,
        low_ref,
        down_ref,
        lambda j: [(half + shared[j], TILE)],
        high_o,
        low_o,
        spread_ref,
        lambda i, j: total_ref[pl.ds(pl.multiple_of(shared[j], TILE), TILE), :],
        lambda i, j, best: done.update({j: best}),
    )
    own = row_ref[...], swapped(core, [done[0], done[1]])
    other = col_ref[...], cols
    chips = out_ref.shape[0] // 4
    for h in range(2):
        out_ref[h * chips : (h + 1) * chips, :] = jnp.where(core == 0, own[h], other[h])
        out_ref[(2 + h) * chips : (3 + h) * chips, :] = jnp.where(core == 0, other[h], own[h])


def pick_kernel(answer_ref, cl_ref, rank_ref, out_ref):
    lanes = answer_ref.shape[1]
    chips = answer_ref.shape[0] // 2
    count = cl_ref.shape[1]
    owner = (lax.broadcasted_iota(jnp.int32, (chips, count), 0) == cl_ref[...]).astype(
        jnp.float32
    ).astype(jnp.bfloat16)
    tn = (((0,), (0,)), ((), ()))
    answer = jnp.maximum(answer_ref[:chips, :], answer_ref[chips:, :])
    high, rest = split(answer)
    middle, low = split(answer - high.astype(jnp.float32))
    by_rank = dot_f32(high, owner, tn) + (dot_f32(middle, owner, tn) + dot_f32(low, owner, tn))
    at_rank = lax.broadcasted_iota(jnp.int32, (lanes, count), 0) == rank_ref[...]
    out_ref[...] = jnp.sum(jnp.where(at_rank, by_rank, 0.0), axis=0, keepdims=True)


def on_device(embeddings, clusters, indices):
    count, width = embeddings.shape
    chip_axes = ("z", "y", "x_hi", "x_lo")
    chips, slots, lanes = 64, 16, 128
    rows = chips * slots
    length = slots * width // lanes + 1
    cl = clusters.reshape(1, count)
    ix = indices.reshape(1, count)
    f32 = functools.partial(jax.ShapeDtypeStruct, dtype=jnp.float32)
    bf16 = functools.partial(jax.ShapeDtypeStruct, dtype=jnp.bfloat16)
    dma = pltpu.SemaphoreType.DMA
    sending, rank = pl.pallas_call(
        place_kernel,
        out_shape=(f32((chips * length, lanes)), jax.ShapeDtypeStruct((1, count), jnp.int32)),
        in_specs=[pl.BlockSpec(memory_space=pltpu.HBM)] * 3,
        out_specs=(VMEM, VMEM),
        scratch_shapes=[
            pltpu.VMEM((count, width), jnp.float32),
            pltpu.VMEM((1, count), jnp.int32),
            pltpu.VMEM((1, count), jnp.int32),
            dma((2,)),
            dma,
            dma,
        ],
        compiler_params=PARAMS,
        name="place",
    )(*(pltpu.with_memory_space_constraint(v, pltpu.HBM) for v in (embeddings, cl, ix)))
    held = lax.all_to_all(
        sending.reshape(chips * length, 1, lanes), chip_axes, split_axis=0, concat_axis=0, tiled=True
    )
    part = chips * length // 2
    arrived = [
        lax.ppermute(held[h * part : (h + 1) * part], "core", [(0, 1), (1, 0)]).reshape(part, lanes)
        for h in range(2)
    ]
    held = held.reshape(chips * length, lanes)
    flops = 2 * rows * rows * width * 3
    high, low, down, best = pl.pallas_call(
        own_kernel,
        out_shape=(
            bf16((rows, width)),
            bf16((rows, width)),
            f32((rows, lanes)),
            f32((rows, lanes)),
        ),
        in_specs=[VMEM],
        out_specs=(VMEM,) * 4,
        scratch_shapes=[pltpu.VMEM((rows, lanes), jnp.float32)],
        compiler_params=PARAMS,
        cost_estimate=pl.CostEstimate(flops=flops, bytes_accessed=8 << 20, transcendentals=0),
        name="own",
    )(held)
    half = rows // 2
    scratch = [
        pltpu.VMEM((half, width), jnp.bfloat16),
        pltpu.VMEM((half, width), jnp.bfloat16),
        pltpu.VMEM((half, lanes), jnp.float32),
    ]
    row, col, total = pl.pallas_call(
        first_kernel,
        out_shape=(f32((chips // 2, lanes)), f32((chips // 2, lanes)), f32((half, lanes))),
        in_specs=[VMEM] * 5,
        out_specs=(VMEM,) * 3,
        scratch_shapes=scratch,
        compiler_params=PARAMS,
        cost_estimate=pl.CostEstimate(
            flops=3 * flops // 8, bytes_accessed=2 << 20, transcendentals=0
        ),
        name="first",
    )(arrived[0], high, low, down, best)
    result = pl.pallas_call(
        second_kernel,
        out_shape=f32((2 * chips, lanes)),
        in_specs=[VMEM] * 7,
        out_specs=VMEM,
        scratch_shapes=scratch,
        compiler_params=PARAMS,
        cost_estimate=pl.CostEstimate(flops=flops // 8, bytes_accessed=2 << 20, transcendentals=0),
        name="second",
    )(arrived[1], high, low, down, total, row, col)
    answer = lax.all_to_all(
        result.reshape(2 * chips, 1, lanes), ("core",) + chip_axes, split_axis=0, concat_axis=0, tiled=True
    ).reshape(2 * chips, lanes)
    out = pl.pallas_call(
        pick_kernel,
        out_shape=f32((1, count)),
        in_specs=[VMEM] * 3,
        out_specs=VMEM,
        compiler_params=PARAMS,
        name="pick",
    )(answer, cl, rank)
    return out.reshape(count)


def solution(mesh):
    fine = Mesh(mesh.devices.reshape(4, 2, 2, 2, 4), POINTS)
    return jax.shard_map(
        on_device,
        mesh=fine,
        in_specs=(P(POINTS, None), P(POINTS), P(POINTS)),
        out_specs=P(POINTS),
        check_vma=False,
    )
```

```python
import functools

import jax
import jax.numpy as jnp
from jax import lax
from jax.experimental import pallas as pl
from jax.experimental.pallas import tpu as pltpu
from jax.sharding import Mesh, PartitionSpec as P

EPS = 1e-06
EMPTY = 1e9
TILE = 256
POINTS = ("y", "x_hi", "core", "x_lo", "z")
NT = (((1,), (1,)), ((), ()))
VMEM = pl.BlockSpec(memory_space=pltpu.VMEM)
PARAMS = pltpu.CompilerParams(vmem_limit_bytes=20 * 1024 * 1024)


def split(values):
    high = values.astype(jnp.bfloat16)
    low = (values - high.astype(jnp.float32)).astype(jnp.bfloat16)
    return high, low


def dot_f32(a, b, dims):
    return lax.dot_general(a, b, dims, preferred_element_type=jnp.float32)


def place_kernel(emb_hbm, cl_hbm, ix_hbm, send_ref, rank_ref, emb, cl_ref, ix_ref, emb_sem, cl_sem, ix_sem):
    count, width = emb.shape
    slots, lanes, turn, chips = 16, 128, 8, 64
    parts = 2
    step = count // parts
    copies = [
        pltpu.make_async_copy(
            emb_hbm.at[pl.ds(p * step, step)], emb.at[pl.ds(p * step, step)], emb_sem.at[p]
        )
        for p in range(parts)
    ]
    cl_copy = pltpu.make_async_copy(cl_hbm, cl_ref, cl_sem)
    ix_copy = pltpu.make_async_copy(ix_hbm, ix_ref, ix_sem)
    cl_copy.start()
    ix_copy.start()
    for copy in copies:
        copy.start()
    cl_copy.wait()
    ix_copy.wait()
    cl = cl_ref[...]
    ix = ix_ref[...]
    along = jnp.broadcast_to(cl.astype(jnp.float32), (count, count))
    down = along.T
    before = lax.broadcasted_iota(jnp.int32, (count, count), 0) < lax.broadcasted_iota(
        jnp.int32, (count, count), 1
    )
    rank = jnp.sum(
        jnp.where((along == down) & before, 1.0, 0.0), axis=0, keepdims=True
    ).astype(jnp.int32)
    rank_ref[...] = rank
    target = cl * slots + (rank + cl % turn) % slots
    owner = (lax.broadcasted_iota(jnp.int32, (chips, count), 0) == cl).astype(
        jnp.float32
    ).astype(jnp.bfloat16)
    at_rank = lax.broadcasted_iota(jnp.int32, (lanes, count), 0) == rank
    tag = ix + 1
    tag_high = jnp.where(at_rank, (tag // 256).astype(jnp.float32), 0.0).astype(jnp.bfloat16)
    tag_low = jnp.where(at_rank, (tag % 256).astype(jnp.float32), 0.0).astype(jnp.bfloat16)
    tags = 256.0 * dot_f32(owner, tag_high, NT) + dot_f32(owner, tag_low, NT)
    highs, lows = [], []
    for p in range(parts):
        copies[p].wait()
        x = emb[p * step : (p + 1) * step, :]
        unit = x * lax.rsqrt(jnp.sum(x * x, axis=1, keepdims=True) + EPS)
        high, low = split(unit)
        highs.append(high)
        lows.append(low)
    high = jnp.concatenate(highs, axis=0)
    low = jnp.concatenate(lows, axis=0)
    mm = (((1,), (0,)), ((), ()))
    chunks = width // lanes
    sub = lax.broadcasted_iota(jnp.int32, (8, lanes), 0)
    block = 8 * turn * slots
    for r in range(0, chips * slots, block):
        place = (
            lax.broadcasted_iota(jnp.int32, (block, count), 0) + r == target
        ).astype(jnp.float32).astype(jnp.bfloat16)
        moved = dot_f32(place, high, mm) + dot_f32(place, low, mm)
        for g in range(8):
            base = (r // slots + g * turn) * (chunks * slots + 1)

            def head(a, k):
                at = (g * turn + a) * slots
                return moved[at : at + 8, k * lanes : (k + 1) * lanes]

            def tag_of(a):
                at = r // slots + g * turn + a
                return jnp.broadcast_to(tags[at : at + 1, :], (8, lanes))

            for a in range(turn):
                for k in range(chunks):
                    tile = head(a, k)
                    if k > 0 and a > 0:
                        tile = jnp.where(sub < a, head(a, k - 1), tile)
                    elif k == 0 and a > 0:
                        tile = jnp.where(sub == a - 1, tag_of(a - 1), tile)
                        if a > 1:
                            tile = jnp.where(sub < a - 1, head(a - 1, chunks - 1), tile)
                    at = base + 8 * (12 * a + 2 * k)
                    send_ref[at : at + 8, :] = tile
                    whole = (g * turn + a) * slots + 8
                    send_ref[at + 8 : at + 16, :] = moved[
                        whole : whole + 8, k * lanes : (k + 1) * lanes
                    ]
            at = base + 8 * 12 * turn
            send_ref[at : at + 8, :] = jnp.where(
                sub == turn - 1, tag_of(turn - 1), head(turn - 1, chunks - 1)
            )


def slot_of(rows, lanes):
    row = lax.broadcasted_iota(jnp.int32, (rows, lanes), 0)
    return (row % 16 + 16 - (row // 16) % 8) % 16


def unpack(held_ref, first, chips, high_ref, low_ref, spread_ref):
    slots, lanes, turn = 16, 128, 8
    chunks = high_ref.shape[1] // lanes
    sub = lax.broadcasted_iota(jnp.int32, (8, lanes), 0)
    for s in range(first, first + chips):
        a = s % turn
        base = 97 * (s - a)

        def tile(t):
            at = base + 8 * t
            return held_ref[at : at + 8, :]

        for k in range(chunks):
            t = 12 * a + 2 * k
            top = tile(t)
            if a > 0:
                top = jnp.where(sub < a, tile(t + 2), top)
            high, low = split(jnp.concatenate([top, tile(t + 1)], axis=0))
            high_ref[s * slots : (s + 1) * slots, k * lanes : (k + 1) * lanes] = high
            low_ref[s * slots : (s + 1) * slots, k * lanes : (k + 1) * lanes] = low
        at = base + 97 * a + 96
        spread_ref[s * slots : (s + 1) * slots, :] = jnp.broadcast_to(
            held_ref[at : at + 1, :], (slots, lanes)
        )


def tags_of(spread, slot):
    lanes = spread.shape[1]
    lane = lax.broadcasted_iota(jnp.int32, spread.shape, 1)
    down = jnp.sum(jnp.where(lane == slot, spread, 0.0), axis=1, keepdims=True)
    down = jnp.where(down == 0.0, EMPTY, down)
    return jnp.broadcast_to(down, spread.shape)


def products(high_i, low_i, high_j, low_j):
    return dot_f32(high_i, high_j, NT) + (
        dot_f32(high_i, low_j, NT) + dot_f32(low_i, high_j, NT)
    )


def by_slot(best, slot):
    slots = 16
    rows, lanes = best.shape
    lane = lax.broadcasted_iota(jnp.int32, (rows, lanes), 1)
    picked = jnp.where(lane == slot, best, -2.0).reshape(rows // slots, slots, lanes)
    return jnp.max(picked, axis=1)


def own_kernel(held_ref, high_ref, low_ref, down_ref, best_ref, spread_ref):
    rows, lanes = down_ref.shape
    slot = slot_of(TILE, lanes)
    for j in range(0, rows, TILE):
        sj = slice(j, j + TILE)
        unpack(held_ref, j // 16, TILE // 16, high_ref, low_ref, spread_ref)
        down_j = tags_of(spread_ref[sj, :], slot)
        down_ref[sj, :] = down_j
        cols = [down_j[c : c + lanes, :].T[:1, :] for c in range(0, TILE, lanes)]
        high_j, low_j = high_ref[sj, :], low_ref[sj, :]
        mixed = dot_f32(high_j, low_j, NT)
        square = dot_f32(high_j, high_j, NT) + (mixed + mixed.T)
        best_j = jnp.full((TILE, lanes), -1.0, jnp.float32)
        for n, col_ix in enumerate(cols):
            part = square[:, n * lanes : (n + 1) * lanes]
            best_j = jnp.maximum(best_j, jnp.where(col_ix < down_j, part, -1.0))
        if j > 0:
            sims = products(high_ref[:j, :], low_ref[:j, :], high_j, low_j)
            down = down_ref[:j, :]
            best = best_ref[:j, :]
            over = []
            for n, col_ix in enumerate(cols):
                part = sims[:, n * lanes : (n + 1) * lanes]
                best = jnp.maximum(best, jnp.where(col_ix < down, part, -1.0))
                top = jnp.max(jnp.where(down < col_ix, part, -1.0), axis=0, keepdims=True)
                over.append(jnp.broadcast_to(top, (lanes, lanes)).T)
            best_ref[:j, :] = best
            best_j = jnp.maximum(best_j, jnp.concatenate(over, axis=0))
        best_ref[sj, :] = best_j


def cross(held_ref, high_ref, low_ref, down_ref, parts, high_o, low_o, spread_ref, get, put):
    half, lanes = high_o.shape[0], down_ref.shape[1]
    slot = slot_of(TILE, lanes)
    cols, over = {}, {}

    def finish(i, rows, j, sims):
        down = down_ref[rows, :]
        best = get(i, j)
        for n, col_ix in enumerate(cols[j]):
            part = sims[:, n * lanes : (n + 1) * lanes]
            best = jnp.maximum(best, jnp.where(col_ix < down, part, -1.0))
            top = jnp.where(down < col_ix, part, -1.0).reshape(part.shape[0] // 8, 8, lanes)
            top = jnp.max(top, axis=0)
            over[j, n] = top if (j, n) not in over else jnp.maximum(over[j, n], top)
        put(i, j, best)

    waiting = None
    for j in range(half // TILE):
        sj = slice(j * TILE, (j + 1) * TILE)
        unpack(held_ref, sj.start // 16, TILE // 16, high_o, low_o, spread_ref)
        down_j = tags_of(spread_ref[sj, :], slot)
        cols[j] = [down_j[c : c + lanes, :].T[:1, :] for c in range(0, TILE, lanes)]
        for i, (start, size) in enumerate(parts(j)):
            rows = pl.ds(pl.multiple_of(start, TILE), size)
            sims = products(high_ref[rows, :], low_ref[rows, :], high_o[sj, :], low_o[sj, :])
            if waiting is not None:
                finish(*waiting)
            waiting = i, rows, j, sims
    finish(*waiting)
    out = []
    for j in range(half // TILE):
        wide = [
            jnp.broadcast_to(jnp.max(over[j, n], axis=0, keepdims=True), (lanes, lanes)).T
            for n in range(TILE // lanes)
        ]
        out.append(by_slot(jnp.concatenate(wide, axis=0), slot))
    return jnp.concatenate(out, axis=0)


def swapped(core, blocks):
    lanes = blocks[0].shape[1]
    slot = slot_of(TILE, lanes)
    one, two = (
        by_slot(jnp.broadcast_to(jnp.max(best, axis=1, keepdims=True), best.shape), slot)
        for best in blocks
    )
    return jnp.concatenate(
        [jnp.where(core == 0, one, two), jnp.where(core == 0, two, one)], axis=0
    )


def first_kernel(
    held_ref, high_ref, low_ref, down_ref, best_ref, row_ref, col_ref, total_ref, high_o, low_o, spread_ref
):
    half = high_o.shape[0]
    core = lax.axis_index("core")
    shared = [core * TILE, (1 - core) * TILE]
    done = {}

    def get(i, j):
        if i == 1:
            return best_ref[pl.ds(pl.multiple_of(shared[j], TILE), TILE), :]
        return best_ref[half:, :] if j == 0 else total_ref[...]

    def put(i, j, best):
        if i == 1:
            done[j] = best
        else:
            total_ref[...] = best

    col_ref[...] = cross(
        held_ref,
        high_ref,
        low_ref,
        down_ref,
        lambda j: [(half, half), (shared[j], TILE)],
        high_o,
        low_o,
        spread_ref,
        get,
        put,
    )
    row_ref[...] = swapped(core, [done[0], done[1]])


def second_kernel(
    held_ref, high_ref, low_ref, down_ref, total_ref, row_ref, col_ref, out_ref, high_o, low_o, spread_ref
):
    half = high_o.shape[0]
    core = lax.axis_index("core")
    shared = [core * TILE, (1 - core) * TILE]
    done = {}
    cols = cross(
        held_ref,
        high_ref,
        low_ref,
        down_ref,
        lambda j: [(half + shared[j], TILE)],
        high_o,
        low_o,
        spread_ref,
        lambda i, j: total_ref[pl.ds(pl.multiple_of(shared[j], TILE), TILE), :],
        lambda i, j, best: done.update({j: best}),
    )
    own = row_ref[...], swapped(core, [done[0], done[1]])
    other = col_ref[...], cols
    layer = out_ref.shape[0] // 8
    for h in range(2):
        for z in range(2):
            mine, its = (v[h][z * layer : (z + 1) * layer, :] for v in (own, other))
            at = 2 * layer * (2 * h + z)
            out_ref[at : at + layer, :] = jnp.where(core == 0, mine, its)
            out_ref[at + layer : at + 2 * layer, :] = jnp.where(core == 0, its, mine)


def pick_kernel(answer_ref, cl_ref, rank_ref, out_ref):
    lanes = answer_ref.shape[1]
    chips = answer_ref.shape[0] // 2
    count = cl_ref.shape[1]
    owner = (lax.broadcasted_iota(jnp.int32, (chips, count), 0) == cl_ref[...]).astype(
        jnp.float32
    ).astype(jnp.bfloat16)
    tn = (((0,), (0,)), ((), ()))
    answer = jnp.max(answer_ref[...].reshape(4, 2, chips // 4, lanes), axis=1)
    answer = answer.reshape(chips, lanes)
    high, rest = split(answer)
    middle, low = split(answer - high.astype(jnp.float32))
    by_rank = dot_f32(high, owner, tn) + (dot_f32(middle, owner, tn) + dot_f32(low, owner, tn))
    at_rank = lax.broadcasted_iota(jnp.int32, (lanes, count), 0) == rank_ref[...]
    out_ref[...] = jnp.sum(jnp.where(at_rank, by_rank, 0.0), axis=0, keepdims=True)


def on_device(embeddings, clusters, indices):
    count, width = embeddings.shape
    chip_axes = ("z", "y", "x_hi", "x_lo")
    chips, slots, lanes = 64, 16, 128
    rows = chips * slots
    length = slots * width // lanes + 1
    cl = clusters.reshape(1, count)
    ix = indices.reshape(1, count)
    f32 = functools.partial(jax.ShapeDtypeStruct, dtype=jnp.float32)
    bf16 = functools.partial(jax.ShapeDtypeStruct, dtype=jnp.bfloat16)
    dma = pltpu.SemaphoreType.DMA
    sending, rank = pl.pallas_call(
        place_kernel,
        out_shape=(f32((chips * length, lanes)), jax.ShapeDtypeStruct((1, count), jnp.int32)),
        in_specs=[pl.BlockSpec(memory_space=pltpu.HBM)] * 3,
        out_specs=(VMEM, VMEM),
        scratch_shapes=[
            pltpu.VMEM((count, width), jnp.float32),
            pltpu.VMEM((1, count), jnp.int32),
            pltpu.VMEM((1, count), jnp.int32),
            dma((2,)),
            dma,
            dma,
        ],
        compiler_params=PARAMS,
        name="place",
    )(*(pltpu.with_memory_space_constraint(v, pltpu.HBM) for v in (embeddings, cl, ix)))
    held = lax.all_to_all(
        sending.reshape(chips * length, 1, lanes), chip_axes, split_axis=0, concat_axis=0, tiled=True
    )
    part = chips * length // 2
    arrived = [
        lax.ppermute(held[h * part : (h + 1) * part], "core", [(0, 1), (1, 0)]).reshape(part, lanes)
        for h in range(2)
    ]
    held = held.reshape(chips * length, lanes)
    flops = 2 * rows * rows * width * 3
    high, low, down, best = pl.pallas_call(
        own_kernel,
        out_shape=(
            bf16((rows, width)),
            bf16((rows, width)),
            f32((rows, lanes)),
            f32((rows, lanes)),
        ),
        in_specs=[VMEM],
        out_specs=(VMEM,) * 4,
        scratch_shapes=[pltpu.VMEM((rows, lanes), jnp.float32)],
        compiler_params=PARAMS,
        cost_estimate=pl.CostEstimate(flops=flops, bytes_accessed=8 << 20, transcendentals=0),
        name="own",
    )(held)
    half = rows // 2
    scratch = [
        pltpu.VMEM((half, width), jnp.bfloat16),
        pltpu.VMEM((half, width), jnp.bfloat16),
        pltpu.VMEM((half, lanes), jnp.float32),
    ]
    row, col, total = pl.pallas_call(
        first_kernel,
        out_shape=(f32((chips // 2, lanes)), f32((chips // 2, lanes)), f32((half, lanes))),
        in_specs=[VMEM] * 5,
        out_specs=(VMEM,) * 3,
        scratch_shapes=scratch,
        compiler_params=PARAMS,
        cost_estimate=pl.CostEstimate(
            flops=3 * flops // 8, bytes_accessed=2 << 20, transcendentals=0
        ),
        name="first",
    )(arrived[0], high, low, down, best)
    result = pl.pallas_call(
        second_kernel,
        out_shape=f32((2 * chips, lanes)),
        in_specs=[VMEM] * 7,
        out_specs=VMEM,
        scratch_shapes=scratch,
        compiler_params=PARAMS,
        cost_estimate=pl.CostEstimate(flops=flops // 8, bytes_accessed=2 << 20, transcendentals=0),
        name="second",
    )(arrived[1], high, low, down, total, row, col)
    answer = lax.all_to_all(
        result.reshape(2 * chips, 1, lanes), chip_axes[:1] + ("core",) + chip_axes[1:], split_axis=0, concat_axis=0, tiled=True
    ).reshape(2 * chips, lanes)
    out = pl.pallas_call(
        pick_kernel,
        out_shape=f32((1, count)),
        in_specs=[VMEM] * 3,
        out_specs=VMEM,
        compiler_params=PARAMS,
        name="pick",
    )(answer, cl, rank)
    return out.reshape(count)


def solution(mesh):
    fine = Mesh(mesh.devices.reshape(4, 2, 2, 2, 4), POINTS)
    return jax.shard_map(
        on_device,
        mesh=fine,
        in_specs=(P(POINTS, None), P(POINTS), P(POINTS)),
        out_specs=P(POINTS),
        check_vma=False,
    )
```

```python
import functools

import jax
import jax.numpy as jnp
from jax import lax
from jax.experimental import pallas as pl
from jax.experimental.pallas import tpu as pltpu
from jax.sharding import Mesh, PartitionSpec as P

EPS = 1e-06
EMPTY = 1e9
TILE = 256
POINTS = ("y", "x_hi", "core", "x_lo", "z")
NT = (((1,), (1,)), ((), ()))
VMEM = pl.BlockSpec(memory_space=pltpu.VMEM)
PARAMS = pltpu.CompilerParams(vmem_limit_bytes=20 * 1024 * 1024)


def split(values):
    high = values.astype(jnp.bfloat16)
    low = (values - high.astype(jnp.float32)).astype(jnp.bfloat16)
    return high, low


def dot_f32(a, b, dims):
    return lax.dot_general(a, b, dims, preferred_element_type=jnp.float32)


def place_kernel(emb_hbm, cl_hbm, ix_hbm, send_ref, rank_ref, emb, cl_ref, ix_ref, emb_sem, cl_sem, ix_sem):
    count, width = emb.shape
    slots, lanes, turn, chips = 16, 128, 8, 64
    parts = 2
    step = count // parts
    copies = [
        pltpu.make_async_copy(
            emb_hbm.at[pl.ds(p * step, step)], emb.at[pl.ds(p * step, step)], emb_sem.at[p]
        )
        for p in range(parts)
    ]
    cl_copy = pltpu.make_async_copy(cl_hbm, cl_ref, cl_sem)
    ix_copy = pltpu.make_async_copy(ix_hbm, ix_ref, ix_sem)
    cl_copy.start()
    ix_copy.start()
    for copy in copies:
        copy.start()
    cl_copy.wait()
    ix_copy.wait()
    cl = cl_ref[...]
    ix = ix_ref[...]
    along = jnp.broadcast_to(cl.astype(jnp.float32), (count, count))
    down = along.T
    before = lax.broadcasted_iota(jnp.int32, (count, count), 0) < lax.broadcasted_iota(
        jnp.int32, (count, count), 1
    )
    rank = jnp.sum(
        jnp.where((along == down) & before, 1.0, 0.0), axis=0, keepdims=True
    ).astype(jnp.int32)
    rank_ref[...] = rank
    target = cl * slots + (rank + cl % turn) % slots
    owner = (lax.broadcasted_iota(jnp.int32, (chips, count), 0) == cl).astype(
        jnp.float32
    ).astype(jnp.bfloat16)
    at_rank = lax.broadcasted_iota(jnp.int32, (lanes, count), 0) == rank
    tag = ix + 1
    tag_high = jnp.where(at_rank, (tag // 256).astype(jnp.float32), 0.0).astype(jnp.bfloat16)
    tag_low = jnp.where(at_rank, (tag % 256).astype(jnp.float32), 0.0).astype(jnp.bfloat16)
    tags = 256.0 * dot_f32(owner, tag_high, NT) + dot_f32(owner, tag_low, NT)
    highs, lows = [], []
    for p in range(parts):
        copies[p].wait()
        x = emb[p * step : (p + 1) * step, :]
        unit = x * lax.rsqrt(jnp.sum(x * x, axis=1, keepdims=True) + EPS)
        high, low = split(unit)
        highs.append(high)
        lows.append(low)
    high = jnp.concatenate(highs, axis=0)
    low = jnp.concatenate(lows, axis=0)
    mm = (((1,), (0,)), ((), ()))
    chunks = width // lanes
    sub = lax.broadcasted_iota(jnp.int32, (8, lanes), 0)
    block = 8 * turn * slots
    for r in range(0, chips * slots, block):
        place = (
            lax.broadcasted_iota(jnp.int32, (block, count), 0) + r == target
        ).astype(jnp.float32).astype(jnp.bfloat16)
        moved = dot_f32(place, high, mm) + dot_f32(place, low, mm)
        for g in range(8):
            base = (r // slots + g * turn) * (chunks * slots + 1)

            def head(a, k):
                at = (g * turn + a) * slots
                return moved[at : at + 8, k * lanes : (k + 1) * lanes]

            def tag_of(a):
                at = r // slots + g * turn + a
                return jnp.broadcast_to(tags[at : at + 1, :], (8, lanes))

            for a in range(turn):
                for k in range(chunks):
                    tile = head(a, k)
                    if k > 0 and a > 0:
                        tile = jnp.where(sub < a, head(a, k - 1), tile)
                    elif k == 0 and a > 0:
                        tile = jnp.where(sub == a - 1, tag_of(a - 1), tile)
                        if a > 1:
                            tile = jnp.where(sub < a - 1, head(a - 1, chunks - 1), tile)
                    at = base + 8 * (12 * a + 2 * k)
                    send_ref[at : at + 8, :] = tile
                    whole = (g * turn + a) * slots + 8
                    send_ref[at + 8 : at + 16, :] = moved[
                        whole : whole + 8, k * lanes : (k + 1) * lanes
                    ]
            at = base + 8 * 12 * turn
            send_ref[at : at + 8, :] = jnp.where(
                sub == turn - 1, tag_of(turn - 1), head(turn - 1, chunks - 1)
            )


def slot_of(rows, lanes):
    row = lax.broadcasted_iota(jnp.int32, (rows, lanes), 0)
    return (row % 16 + 16 - (row // 16) % 8) % 16


def unpack(held_ref, first, chips, high_ref, low_ref, spread_ref):
    slots, lanes, turn = 16, 128, 8
    chunks = high_ref.shape[1] // lanes
    sub = lax.broadcasted_iota(jnp.int32, (8, lanes), 0)
    for s in range(first, first + chips):
        a = s % turn
        base = 97 * (s - a)

        def tile(t):
            at = base + 8 * t
            return held_ref[at : at + 8, :]

        for k in range(chunks):
            t = 12 * a + 2 * k
            top = tile(t)
            if a > 0:
                top = jnp.where(sub < a, tile(t + 2), top)
            high, low = split(jnp.concatenate([top, tile(t + 1)], axis=0))
            high_ref[s * slots : (s + 1) * slots, k * lanes : (k + 1) * lanes] = high
            low_ref[s * slots : (s + 1) * slots, k * lanes : (k + 1) * lanes] = low
        at = base + 97 * a + 96
        spread_ref[s * slots : (s + 1) * slots, :] = jnp.broadcast_to(
            held_ref[at : at + 1, :], (slots, lanes)
        )


def tags_of(spread, slot):
    lanes = spread.shape[1]
    lane = lax.broadcasted_iota(jnp.int32, spread.shape, 1)
    down = jnp.sum(jnp.where(lane == slot, spread, 0.0), axis=1, keepdims=True)
    down = jnp.where(down == 0.0, EMPTY, down)
    return jnp.broadcast_to(down, spread.shape)


def products(high_i, low_i, high_j, low_j):
    return dot_f32(high_i, high_j, NT) + (
        dot_f32(high_i, low_j, NT) + dot_f32(low_i, high_j, NT)
    )


def by_slot(best, slot):
    slots = 16
    rows, lanes = best.shape
    lane = lax.broadcasted_iota(jnp.int32, (rows, lanes), 1)
    picked = jnp.where(lane == slot, best, -2.0).reshape(rows // slots, slots, lanes)
    return jnp.max(picked, axis=1)


def own_kernel(held_ref, high_ref, low_ref, down_ref, best_ref, spread_ref):
    rows, lanes = down_ref.shape
    slot = slot_of(TILE, lanes)
    for j in range(0, rows, TILE):
        sj = slice(j, j + TILE)
        unpack(held_ref, j // 16, TILE // 16, high_ref, low_ref, spread_ref)
        down_j = tags_of(spread_ref[sj, :], slot)
        down_ref[sj, :] = down_j
        cols = [down_j[c : c + lanes, :].T[:1, :] for c in range(0, TILE, lanes)]
        high_j, low_j = high_ref[sj, :], low_ref[sj, :]
        mixed = dot_f32(high_j, low_j, NT)
        square = dot_f32(high_j, high_j, NT) + (mixed + mixed.T)
        best_j = jnp.full((TILE, lanes), -1.0, jnp.float32)
        for n, col_ix in enumerate(cols):
            part = square[:, n * lanes : (n + 1) * lanes]
            best_j = jnp.maximum(best_j, jnp.where(col_ix < down_j, part, -1.0))
        if j > 0:
            sims = products(high_ref[:j, :], low_ref[:j, :], high_j, low_j)
            down = down_ref[:j, :]
            best = best_ref[:j, :]
            over = []
            for n, col_ix in enumerate(cols):
                part = sims[:, n * lanes : (n + 1) * lanes]
                best = jnp.maximum(best, jnp.where(col_ix < down, part, -1.0))
                top = jnp.max(jnp.where(down < col_ix, part, -1.0), axis=0, keepdims=True)
                over.append(jnp.broadcast_to(top, (lanes, lanes)).T)
            best_ref[:j, :] = best
            best_j = jnp.maximum(best_j, jnp.concatenate(over, axis=0))
        best_ref[sj, :] = best_j


def cross(held_ref, high_ref, low_ref, down_ref, parts, high_o, low_o, spread_ref, get, put):
    half, lanes = high_o.shape[0], down_ref.shape[1]
    slot = slot_of(TILE, lanes)
    cols, over = {}, {}

    def finish(i, rows, j, sims):
        down = down_ref[rows, :]
        best = get(i, j)
        for n, col_ix in enumerate(cols[j]):
            part = sims[:, n * lanes : (n + 1) * lanes]
            best = jnp.maximum(best, jnp.where(col_ix < down, part, -1.0))
            top = jnp.where(down < col_ix, part, -1.0).reshape(part.shape[0] // 8, 8, lanes)
            top = jnp.max(top, axis=0)
            over[j, n] = top if (j, n) not in over else jnp.maximum(over[j, n], top)
        put(i, j, best)

    waiting = None
    for j in range(half // TILE):
        sj = slice(j * TILE, (j + 1) * TILE)
        unpack(held_ref, sj.start // 16, TILE // 16, high_o, low_o, spread_ref)
        down_j = tags_of(spread_ref[sj, :], slot)
        cols[j] = [down_j[c : c + lanes, :].T[:1, :] for c in range(0, TILE, lanes)]
        for i, (start, size) in enumerate(parts(j)):
            rows = pl.ds(pl.multiple_of(start, TILE), size)
            sims = products(high_ref[rows, :], low_ref[rows, :], high_o[sj, :], low_o[sj, :])
            if waiting is not None:
                finish(*waiting)
            waiting = i, rows, j, sims
    finish(*waiting)
    out = []
    for j in range(half // TILE):
        wide = [
            jnp.broadcast_to(jnp.max(over[j, n], axis=0, keepdims=True), (lanes, lanes)).T
            for n in range(TILE // lanes)
        ]
        out.append(by_slot(jnp.concatenate(wide, axis=0), slot))
    return jnp.concatenate(out, axis=0)


def swapped(core, blocks):
    lanes = blocks[0].shape[1]
    slot = slot_of(TILE, lanes)
    one, two = (
        by_slot(jnp.broadcast_to(jnp.max(best, axis=1, keepdims=True), best.shape), slot)
        for best in blocks
    )
    return jnp.concatenate(
        [jnp.where(core == 0, one, two), jnp.where(core == 0, two, one)], axis=0
    )


def first_kernel(
    held_ref, high_ref, low_ref, down_ref, best_ref, row_ref, col_ref, total_ref, high_o, low_o, spread_ref
):
    half = high_o.shape[0]
    core = lax.axis_index("core")
    shared = [core * TILE, (1 - core) * TILE]
    done = {}

    def get(i, j):
        if i == 1:
            return best_ref[pl.ds(pl.multiple_of(shared[j], TILE), TILE), :]
        return best_ref[half:, :] if j == 0 else total_ref[...]

    def put(i, j, best):
        if i == 1:
            done[j] = best
        else:
            total_ref[...] = best

    col_ref[...] = cross(
        held_ref,
        high_ref,
        low_ref,
        down_ref,
        lambda j: [(half, half), (shared[j], TILE)],
        high_o,
        low_o,
        spread_ref,
        get,
        put,
    )
    row_ref[...] = swapped(core, [done[0], done[1]])


def second_kernel(
    held_ref, high_ref, low_ref, down_ref, total_ref, row_ref, col_ref, out_ref, high_o, low_o, spread_ref
):
    half = high_o.shape[0]
    core = lax.axis_index("core")
    shared = [core * TILE, (1 - core) * TILE]
    done = {}
    cols = cross(
        held_ref,
        high_ref,
        low_ref,
        down_ref,
        lambda j: [(half + shared[j], TILE)],
        high_o,
        low_o,
        spread_ref,
        lambda i, j: total_ref[pl.ds(pl.multiple_of(shared[j], TILE), TILE), :],
        lambda i, j, best: done.update({j: best}),
    )
    own = row_ref[...], swapped(core, [done[0], done[1]])
    other = col_ref[...], cols
    chips = out_ref.shape[0] // 4
    for h in range(2):
        out_ref[h * chips : (h + 1) * chips, :] = jnp.where(core == 0, own[h], other[h])
        out_ref[(2 + h) * chips : (3 + h) * chips, :] = jnp.where(core == 0, other[h], own[h])


def pick_kernel(answer_ref, cl_ref, rank_ref, out_ref):
    lanes = answer_ref.shape[1]
    chips = answer_ref.shape[0] // 2
    count = cl_ref.shape[1]
    owner = (lax.broadcasted_iota(jnp.int32, (chips, count), 0) == cl_ref[...]).astype(
        jnp.float32
    ).astype(jnp.bfloat16)
    tn = (((0,), (0,)), ((), ()))
    answer = jnp.maximum(answer_ref[:chips, :], answer_ref[chips:, :])
    high, rest = split(answer)
    middle, low = split(answer - high.astype(jnp.float32))
    by_rank = dot_f32(high, owner, tn) + (dot_f32(middle, owner, tn) + dot_f32(low, owner, tn))
    at_rank = lax.broadcasted_iota(jnp.int32, (lanes, count), 0) == rank_ref[...]
    out_ref[...] = jnp.sum(jnp.where(at_rank, by_rank, 0.0), axis=0, keepdims=True)


def on_device(embeddings, clusters, indices):
    count, width = embeddings.shape
    chip_axes = ("z", "y", "x_hi", "x_lo")
    chips, slots, lanes = 64, 16, 128
    rows = chips * slots
    length = slots * width // lanes + 1
    cl = clusters.reshape(1, count)
    ix = indices.reshape(1, count)
    f32 = functools.partial(jax.ShapeDtypeStruct, dtype=jnp.float32)
    bf16 = functools.partial(jax.ShapeDtypeStruct, dtype=jnp.bfloat16)
    dma = pltpu.SemaphoreType.DMA
    sending, rank = pl.pallas_call(
        place_kernel,
        out_shape=(f32((chips * length, lanes)), jax.ShapeDtypeStruct((1, count), jnp.int32)),
        in_specs=[pl.BlockSpec(memory_space=pltpu.HBM)] * 3,
        out_specs=(VMEM, VMEM),
        scratch_shapes=[
            pltpu.VMEM((count, width), jnp.float32),
            pltpu.VMEM((1, count), jnp.int32),
            pltpu.VMEM((1, count), jnp.int32),
            dma((2,)),
            dma,
            dma,
        ],
        compiler_params=PARAMS,
        name="place",
    )(*(pltpu.with_memory_space_constraint(v, pltpu.HBM) for v in (embeddings, cl, ix)))
    held = lax.all_to_all(
        sending.reshape(chips * length, 1, lanes), chip_axes, split_axis=0, concat_axis=0, tiled=True
    )
    part = chips * length // 2
    swap = [(0, 1), (1, 0)]
    half_1, later = lax.optimization_barrier((held[:part], held))
    arrived = [
        lax.ppermute(half, "core", swap).reshape(part, lanes) for half in (half_1, later[part:])
    ]
    held = held.reshape(chips * length, lanes)
    flops = 2 * rows * rows * width * 3
    high, low, down, best = pl.pallas_call(
        own_kernel,
        out_shape=(
            bf16((rows, width)),
            bf16((rows, width)),
            f32((rows, lanes)),
            f32((rows, lanes)),
        ),
        in_specs=[VMEM],
        out_specs=(VMEM,) * 4,
        scratch_shapes=[pltpu.VMEM((rows, lanes), jnp.float32)],
        compiler_params=PARAMS,
        cost_estimate=pl.CostEstimate(flops=flops, bytes_accessed=8 << 20, transcendentals=0),
        name="own",
    )(held)
    half = rows // 2
    scratch = [
        pltpu.VMEM((half, width), jnp.bfloat16),
        pltpu.VMEM((half, width), jnp.bfloat16),
        pltpu.VMEM((half, lanes), jnp.float32),
    ]
    row, col, total = pl.pallas_call(
        first_kernel,
        out_shape=(f32((chips // 2, lanes)), f32((chips // 2, lanes)), f32((half, lanes))),
        in_specs=[VMEM] * 5,
        out_specs=(VMEM,) * 3,
        scratch_shapes=scratch,
        compiler_params=PARAMS,
        cost_estimate=pl.CostEstimate(
            flops=3 * flops // 8, bytes_accessed=2 << 20, transcendentals=0
        ),
        name="first",
    )(arrived[0], high, low, down, best)
    result = pl.pallas_call(
        second_kernel,
        out_shape=f32((2 * chips, lanes)),
        in_specs=[VMEM] * 7,
        out_specs=VMEM,
        scratch_shapes=scratch,
        compiler_params=PARAMS,
        cost_estimate=pl.CostEstimate(flops=flops // 8, bytes_accessed=2 << 20, transcendentals=0),
        name="second",
    )(arrived[1], high, low, down, total, row, col)
    answer = lax.all_to_all(
        result.reshape(2 * chips, 1, lanes), ("core",) + chip_axes, split_axis=0, concat_axis=0, tiled=True
    ).reshape(2 * chips, lanes)
    out = pl.pallas_call(
        pick_kernel,
        out_shape=f32((1, count)),
        in_specs=[VMEM] * 3,
        out_specs=VMEM,
        compiler_params=PARAMS,
        name="pick",
    )(answer, cl, rank)
    return out.reshape(count)


def solution(mesh):
    fine = Mesh(mesh.devices.reshape(4, 2, 2, 2, 4), POINTS)
    return jax.shard_map(
        on_device,
        mesh=fine,
        in_specs=(P(POINTS, None), P(POINTS), P(POINTS)),
        out_specs=P(POINTS),
        check_vma=False,
    )
```

```python
import functools

import jax
import jax.numpy as jnp
from jax import lax
from jax.experimental import pallas as pl
from jax.experimental.pallas import tpu as pltpu
from jax.sharding import Mesh, PartitionSpec as P

EPS = 1e-06
EMPTY = 1e9
TILE = 256
POINTS = ("y", "x_hi", "core", "x_lo", "z")
NT = (((1,), (1,)), ((), ()))
VMEM = pl.BlockSpec(memory_space=pltpu.VMEM)
PARAMS = pltpu.CompilerParams(vmem_limit_bytes=20 * 1024 * 1024)


def split(values):
    high = values.astype(jnp.bfloat16)
    low = (values - high.astype(jnp.float32)).astype(jnp.bfloat16)
    return high, low


def dot_f32(a, b, dims):
    return lax.dot_general(a, b, dims, preferred_element_type=jnp.float32)


def place_kernel(emb_hbm, cl_hbm, ix_hbm, send_ref, rank_ref, emb, cl_ref, ix_ref, emb_sem, cl_sem, ix_sem):
    count, width = emb.shape
    slots, lanes, turn, chips = 16, 128, 8, 64
    parts = 2
    step = count // parts
    copies = [
        pltpu.make_async_copy(
            emb_hbm.at[pl.ds(p * step, step)], emb.at[pl.ds(p * step, step)], emb_sem.at[p]
        )
        for p in range(parts)
    ]
    cl_copy = pltpu.make_async_copy(cl_hbm, cl_ref, cl_sem)
    ix_copy = pltpu.make_async_copy(ix_hbm, ix_ref, ix_sem)
    cl_copy.start()
    ix_copy.start()
    for copy in copies:
        copy.start()
    cl_copy.wait()
    ix_copy.wait()
    cl = cl_ref[...]
    ix = ix_ref[...]
    along = jnp.broadcast_to(cl.astype(jnp.float32), (count, count))
    down = along.T
    before = lax.broadcasted_iota(jnp.int32, (count, count), 0) < lax.broadcasted_iota(
        jnp.int32, (count, count), 1
    )
    rank = jnp.sum(
        jnp.where((along == down) & before, 1.0, 0.0), axis=0, keepdims=True
    ).astype(jnp.int32)
    rank_ref[...] = rank
    target = cl * slots + (rank + cl % turn) % slots
    owner = (lax.broadcasted_iota(jnp.int32, (chips, count), 0) == cl).astype(
        jnp.float32
    ).astype(jnp.bfloat16)
    at_rank = lax.broadcasted_iota(jnp.int32, (lanes, count), 0) == rank
    tag = ix + 1
    tag_high = jnp.where(at_rank, (tag // 256).astype(jnp.float32), 0.0).astype(jnp.bfloat16)
    tag_low = jnp.where(at_rank, (tag % 256).astype(jnp.float32), 0.0).astype(jnp.bfloat16)
    tags = 256.0 * dot_f32(owner, tag_high, NT) + dot_f32(owner, tag_low, NT)
    highs, lows = [], []
    for p in range(parts):
        copies[p].wait()
        x = emb[p * step : (p + 1) * step, :]
        unit = x * lax.rsqrt(jnp.sum(x * x, axis=1, keepdims=True) + EPS)
        high, low = split(unit)
        highs.append(high)
        lows.append(low)
    high = jnp.concatenate(highs, axis=0)
    low = jnp.concatenate(lows, axis=0)
    mm = (((1,), (0,)), ((), ()))
    chunks = width // lanes
    sub = lax.broadcasted_iota(jnp.int32, (8, lanes), 0)
    block = 8 * turn * slots
    for r in range(0, chips * slots, block):
        place = (
            lax.broadcasted_iota(jnp.int32, (block, count), 0) + r == target
        ).astype(jnp.float32).astype(jnp.bfloat16)
        moved = dot_f32(place, high, mm) + dot_f32(place, low, mm)
        for g in range(8):
            base = (r // slots + g * turn) * (chunks * slots + 1)

            def head(a, k):
                at = (g * turn + a) * slots
                return moved[at : at + 8, k * lanes : (k + 1) * lanes]

            def tag_of(a):
                at = r // slots + g * turn + a
                return jnp.broadcast_to(tags[at : at + 1, :], (8, lanes))

            for a in range(turn):
                for k in range(chunks):
                    tile = head(a, k)
                    if k > 0 and a > 0:
                        tile = jnp.where(sub < a, head(a, k - 1), tile)
                    elif k == 0 and a > 0:
                        tile = jnp.where(sub == a - 1, tag_of(a - 1), tile)
                        if a > 1:
                            tile = jnp.where(sub < a - 1, head(a - 1, chunks - 1), tile)
                    at = base + 8 * (12 * a + 2 * k)
                    send_ref[at : at + 8, :] = tile
                    whole = (g * turn + a) * slots + 8
                    send_ref[at + 8 : at + 16, :] = moved[
                        whole : whole + 8, k * lanes : (k + 1) * lanes
                    ]
            at = base + 8 * 12 * turn
            send_ref[at : at + 8, :] = jnp.where(
                sub == turn - 1, tag_of(turn - 1), head(turn - 1, chunks - 1)
            )


def slot_of(rows, lanes):
    row = lax.broadcasted_iota(jnp.int32, (rows, lanes), 0)
    return (row % 16 + 16 - (row // 16) % 8) % 16


def unpack(held_ref, first, chips, high_ref, low_ref, spread_ref):
    slots, lanes, turn = 16, 128, 8
    chunks = high_ref.shape[1] // lanes
    sub = lax.broadcasted_iota(jnp.int32, (8, lanes), 0)
    for s in range(first, first + chips):
        a = s % turn
        base = 97 * (s - a)

        def tile(t):
            at = base + 8 * t
            return held_ref[at : at + 8, :]

        for k in range(chunks):
            t = 12 * a + 2 * k
            top = tile(t)
            if a > 0:
                top = jnp.where(sub < a, tile(t + 2), top)
            high, low = split(jnp.concatenate([top, tile(t + 1)], axis=0))
            high_ref[s * slots : (s + 1) * slots, k * lanes : (k + 1) * lanes] = high
            low_ref[s * slots : (s + 1) * slots, k * lanes : (k + 1) * lanes] = low
        at = base + 97 * a + 96
        spread_ref[s * slots : (s + 1) * slots, :] = jnp.broadcast_to(
            held_ref[at : at + 1, :], (slots, lanes)
        )


def tags_of(spread, slot):
    lanes = spread.shape[1]
    lane = lax.broadcasted_iota(jnp.int32, spread.shape, 1)
    down = jnp.sum(jnp.where(lane == slot, spread, 0.0), axis=1, keepdims=True)
    down = jnp.where(down == 0.0, EMPTY, down)
    return jnp.broadcast_to(down, spread.shape)


def products(high_i, low_i, high_j, low_j):
    return dot_f32(high_i, high_j, NT) + (
        dot_f32(high_i, low_j, NT) + dot_f32(low_i, high_j, NT)
    )


def by_slot(best, slot):
    slots = 16
    rows, lanes = best.shape
    lane = lax.broadcasted_iota(jnp.int32, (rows, lanes), 1)
    picked = jnp.where(lane == slot, best, -2.0).reshape(rows // slots, slots, lanes)
    return jnp.max(picked, axis=1)


def own_kernel(held_ref, high_ref, low_ref, down_ref, best_ref, spread_ref):
    rows, lanes = down_ref.shape
    slot = slot_of(TILE, lanes)
    for j in range(0, rows, TILE):
        sj = slice(j, j + TILE)
        unpack(held_ref, j // 16, TILE // 16, high_ref, low_ref, spread_ref)
        down_j = tags_of(spread_ref[sj, :], slot)
        down_ref[sj, :] = down_j
        cols = [down_j[c : c + lanes, :].T[:1, :] for c in range(0, TILE, lanes)]
        high_j, low_j = high_ref[sj, :], low_ref[sj, :]
        mixed = dot_f32(high_j, low_j, NT)
        square = dot_f32(high_j, high_j, NT) + (mixed + mixed.T)
        best_j = jnp.full((TILE, lanes), -1.0, jnp.float32)
        for n, col_ix in enumerate(cols):
            part = square[:, n * lanes : (n + 1) * lanes]
            best_j = jnp.maximum(best_j, jnp.where(col_ix < down_j, part, -1.0))
        if j > 0:
            sims = products(high_ref[:j, :], low_ref[:j, :], high_j, low_j)
            down = down_ref[:j, :]
            best = best_ref[:j, :]
            over = []
            for n, col_ix in enumerate(cols):
                part = sims[:, n * lanes : (n + 1) * lanes]
                best = jnp.maximum(best, jnp.where(col_ix < down, part, -1.0))
                top = jnp.max(jnp.where(down < col_ix, part, -1.0), axis=0, keepdims=True)
                over.append(jnp.broadcast_to(top, (lanes, lanes)).T)
            best_ref[:j, :] = best
            best_j = jnp.maximum(best_j, jnp.concatenate(over, axis=0))
        best_ref[sj, :] = best_j


def cross(held_ref, high_ref, low_ref, down_ref, parts, high_o, low_o, spread_ref, get, put):
    half, lanes = high_o.shape[0], down_ref.shape[1]
    slot = slot_of(TILE, lanes)
    cols, over = {}, {}

    def finish(i, rows, j, sims):
        down = down_ref[rows, :]
        best = get(i, j)
        for n, col_ix in enumerate(cols[j]):
            part = sims[:, n * lanes : (n + 1) * lanes]
            best = jnp.maximum(best, jnp.where(col_ix < down, part, -1.0))
            top = jnp.where(down < col_ix, part, -1.0).reshape(part.shape[0] // 8, 8, lanes)
            top = jnp.max(top, axis=0)
            over[j, n] = top if (j, n) not in over else jnp.maximum(over[j, n], top)
        put(i, j, best)

    waiting = None
    for j in range(half // TILE):
        sj = slice(j * TILE, (j + 1) * TILE)
        unpack(held_ref, sj.start // 16, TILE // 16, high_o, low_o, spread_ref)
        down_j = tags_of(spread_ref[sj, :], slot)
        cols[j] = [down_j[c : c + lanes, :].T[:1, :] for c in range(0, TILE, lanes)]
        for i, (start, size) in enumerate(parts(j)):
            rows = pl.ds(pl.multiple_of(start, TILE), size)
            sims = products(high_ref[rows, :], low_ref[rows, :], high_o[sj, :], low_o[sj, :])
            if waiting is not None:
                finish(*waiting)
            waiting = i, rows, j, sims
    finish(*waiting)
    out = []
    for j in range(half // TILE):
        wide = [
            jnp.broadcast_to(jnp.max(over[j, n], axis=0, keepdims=True), (lanes, lanes)).T
            for n in range(TILE // lanes)
        ]
        out.append(by_slot(jnp.concatenate(wide, axis=0), slot))
    return jnp.concatenate(out, axis=0)


def swapped(core, blocks):
    lanes = blocks[0].shape[1]
    slot = slot_of(TILE, lanes)
    one, two = (
        by_slot(jnp.broadcast_to(jnp.max(best, axis=1, keepdims=True), best.shape), slot)
        for best in blocks
    )
    return jnp.concatenate(
        [jnp.where(core == 0, one, two), jnp.where(core == 0, two, one)], axis=0
    )


def first_kernel(
    held_ref, high_ref, low_ref, down_ref, best_ref, row_ref, col_ref, total_ref, high_o, low_o, spread_ref
):
    half = high_o.shape[0]
    core = lax.axis_index("core")
    shared = [core * TILE, (1 - core) * TILE]
    done = {}

    def get(i, j):
        if i == 1:
            return best_ref[pl.ds(pl.multiple_of(shared[j], TILE), TILE), :]
        return best_ref[half:, :] if j == 0 else total_ref[...]

    def put(i, j, best):
        if i == 1:
            done[j] = best
        else:
            total_ref[...] = best

    col_ref[...] = cross(
        held_ref,
        high_ref,
        low_ref,
        down_ref,
        lambda j: [(half, half), (shared[j], TILE)],
        high_o,
        low_o,
        spread_ref,
        get,
        put,
    )
    row_ref[...] = swapped(core, [done[0], done[1]])


def second_kernel(
    held_ref, high_ref, low_ref, down_ref, total_ref, row_ref, col_ref, out_ref, high_o, low_o, spread_ref
):
    half = high_o.shape[0]
    core = lax.axis_index("core")
    shared = [core * TILE, (1 - core) * TILE]
    done = {}
    cols = cross(
        held_ref,
        high_ref,
        low_ref,
        down_ref,
        lambda j: [(half + shared[j], TILE)],
        high_o,
        low_o,
        spread_ref,
        lambda i, j: total_ref[pl.ds(pl.multiple_of(shared[j], TILE), TILE), :],
        lambda i, j, best: done.update({j: best}),
    )
    own = row_ref[...], swapped(core, [done[0], done[1]])
    other = col_ref[...], cols
    chips = out_ref.shape[0] // 4
    for h in range(2):
        out_ref[h * chips : (h + 1) * chips, :] = jnp.where(core == 0, own[h], other[h])
        out_ref[(2 + h) * chips : (3 + h) * chips, :] = jnp.where(core == 0, other[h], own[h])


def pick_kernel(answer_ref, cl_ref, rank_ref, out_ref):
    lanes = answer_ref.shape[1]
    chips = answer_ref.shape[0] // 2
    count = cl_ref.shape[1]
    owner = (lax.broadcasted_iota(jnp.int32, (chips, count), 0) == cl_ref[...]).astype(
        jnp.float32
    ).astype(jnp.bfloat16)
    tn = (((0,), (0,)), ((), ()))
    answer = jnp.maximum(answer_ref[:chips, :], answer_ref[chips:, :])
    high, low = split(answer)
    by_rank = dot_f32(high, owner, tn) + dot_f32(low, owner, tn)
    at_rank = lax.broadcasted_iota(jnp.int32, (lanes, count), 0) == rank_ref[...]
    out_ref[...] = jnp.sum(jnp.where(at_rank, by_rank, 0.0), axis=0, keepdims=True)


def on_device(embeddings, clusters, indices):
    count, width = embeddings.shape
    chip_axes = ("z", "y", "x_hi", "x_lo")
    chips, slots, lanes = 64, 16, 128
    rows = chips * slots
    length = slots * width // lanes + 1
    cl = clusters.reshape(1, count)
    ix = indices.reshape(1, count)
    f32 = functools.partial(jax.ShapeDtypeStruct, dtype=jnp.float32)
    bf16 = functools.partial(jax.ShapeDtypeStruct, dtype=jnp.bfloat16)
    dma = pltpu.SemaphoreType.DMA
    sending, rank = pl.pallas_call(
        place_kernel,
        out_shape=(f32((chips * length, lanes)), jax.ShapeDtypeStruct((1, count), jnp.int32)),
        in_specs=[pl.BlockSpec(memory_space=pltpu.HBM)] * 3,
        out_specs=(VMEM, VMEM),
        scratch_shapes=[
            pltpu.VMEM((count, width), jnp.float32),
            pltpu.VMEM((1, count), jnp.int32),
            pltpu.VMEM((1, count), jnp.int32),
            dma((2,)),
            dma,
            dma,
        ],
        compiler_params=PARAMS,
        name="place",
    )(*(pltpu.with_memory_space_constraint(v, pltpu.HBM) for v in (embeddings, cl, ix)))
    held = lax.all_to_all(
        sending.reshape(chips * length, 1, lanes), chip_axes, split_axis=0, concat_axis=0, tiled=True
    )
    part = chips * length // 2
    arrived = [
        lax.ppermute(held[h * part : (h + 1) * part], "core", [(0, 1), (1, 0)]).reshape(part, lanes)
        for h in range(2)
    ]
    held = held.reshape(chips * length, lanes)
    flops = 2 * rows * rows * width * 3
    high, low, down, best = pl.pallas_call(
        own_kernel,
        out_shape=(
            bf16((rows, width)),
            bf16((rows, width)),
            f32((rows, lanes)),
            f32((rows, lanes)),
        ),
        in_specs=[VMEM],
        out_specs=(VMEM,) * 4,
        scratch_shapes=[pltpu.VMEM((rows, lanes), jnp.float32)],
        compiler_params=PARAMS,
        cost_estimate=pl.CostEstimate(flops=flops, bytes_accessed=8 << 20, transcendentals=0),
        name="own",
    )(held)
    half = rows // 2
    scratch = [
        pltpu.VMEM((half, width), jnp.bfloat16),
        pltpu.VMEM((half, width), jnp.bfloat16),
        pltpu.VMEM((half, lanes), jnp.float32),
    ]
    row, col, total = pl.pallas_call(
        first_kernel,
        out_shape=(f32((chips // 2, lanes)), f32((chips // 2, lanes)), f32((half, lanes))),
        in_specs=[VMEM] * 5,
        out_specs=(VMEM,) * 3,
        scratch_shapes=scratch,
        compiler_params=PARAMS,
        cost_estimate=pl.CostEstimate(
            flops=3 * flops // 8, bytes_accessed=2 << 20, transcendentals=0
        ),
        name="first",
    )(arrived[0], high, low, down, best)
    result = pl.pallas_call(
        second_kernel,
        out_shape=f32((2 * chips, lanes)),
        in_specs=[VMEM] * 7,
        out_specs=VMEM,
        scratch_shapes=scratch,
        compiler_params=PARAMS,
        cost_estimate=pl.CostEstimate(flops=flops // 8, bytes_accessed=2 << 20, transcendentals=0),
        name="second",
    )(arrived[1], high, low, down, total, row, col)
    answer = lax.all_to_all(
        result.reshape(2 * chips, 1, lanes), ("core",) + chip_axes, split_axis=0, concat_axis=0, tiled=True
    ).reshape(2 * chips, lanes)
    out = pl.pallas_call(
        pick_kernel,
        out_shape=f32((1, count)),
        in_specs=[VMEM] * 3,
        out_specs=VMEM,
        compiler_params=PARAMS,
        name="pick",
    )(answer, cl, rank)
    return out.reshape(count)


def solution(mesh):
    fine = Mesh(mesh.devices.reshape(4, 2, 2, 2, 4), POINTS)
    return jax.shard_map(
        on_device,
        mesh=fine,
        in_specs=(P(POINTS, None), P(POINTS), P(POINTS)),
        out_specs=P(POINTS),
        check_vma=False,
    )
```

```python
import functools

import jax
import jax.numpy as jnp
from jax import lax
from jax.experimental import pallas as pl
from jax.experimental.pallas import tpu as pltpu
from jax.sharding import Mesh, PartitionSpec as P

EPS = 1e-06
EMPTY = 1e9
TILE = 256
POINTS = ("y", "x_hi", "core", "x_lo", "z")
NT = (((1,), (1,)), ((), ()))
VMEM = pl.BlockSpec(memory_space=pltpu.VMEM)
PARAMS = pltpu.CompilerParams(vmem_limit_bytes=20 * 1024 * 1024)


def split(values):
    high = values.astype(jnp.bfloat16)
    low = (values - high.astype(jnp.float32)).astype(jnp.bfloat16)
    return high, low


def dot_f32(a, b, dims):
    return lax.dot_general(a, b, dims, preferred_element_type=jnp.float32)


def place_kernel(emb_hbm, cl_hbm, ix_hbm, send_ref, rank_ref, emb, cl_ref, ix_ref, emb_sem, cl_sem, ix_sem):
    count, width = emb.shape
    slots, lanes, turn, chips = 16, 128, 8, 64
    parts = 2
    step = count // parts
    copies = [
        pltpu.make_async_copy(
            emb_hbm.at[pl.ds(p * step, step)], emb.at[pl.ds(p * step, step)], emb_sem.at[p]
        )
        for p in range(parts)
    ]
    cl_copy = pltpu.make_async_copy(cl_hbm, cl_ref, cl_sem)
    ix_copy = pltpu.make_async_copy(ix_hbm, ix_ref, ix_sem)
    cl_copy.start()
    ix_copy.start()
    for copy in copies:
        copy.start()
    cl_copy.wait()
    ix_copy.wait()
    cl = cl_ref[...]
    ix = ix_ref[...]
    along = jnp.broadcast_to(cl.astype(jnp.float32), (count, count))
    down = along.T
    before = lax.broadcasted_iota(jnp.int32, (count, count), 0) < lax.broadcasted_iota(
        jnp.int32, (count, count), 1
    )
    rank = jnp.sum(
        jnp.where((along == down) & before, 1.0, 0.0), axis=0, keepdims=True
    ).astype(jnp.int32)
    rank_ref[...] = rank
    target = cl * slots + (rank + cl % turn) % slots
    owner = (lax.broadcasted_iota(jnp.int32, (chips, count), 0) == cl).astype(
        jnp.float32
    ).astype(jnp.bfloat16)
    at_rank = lax.broadcasted_iota(jnp.int32, (lanes, count), 0) == rank
    tag = ix + 1
    tag_high = jnp.where(at_rank, (tag // 256).astype(jnp.float32), 0.0).astype(jnp.bfloat16)
    tag_low = jnp.where(at_rank, (tag % 256).astype(jnp.float32), 0.0).astype(jnp.bfloat16)
    tags = 256.0 * dot_f32(owner, tag_high, NT) + dot_f32(owner, tag_low, NT)
    highs, lows = [], []
    for p in range(parts):
        copies[p].wait()
        x = emb[p * step : (p + 1) * step, :]
        unit = x * lax.rsqrt(jnp.sum(x * x, axis=1, keepdims=True) + EPS)
        high, low = split(unit)
        highs.append(high)
        lows.append(low)
    high = jnp.concatenate(highs, axis=0)
    low = jnp.concatenate(lows, axis=0)
    mm = (((1,), (0,)), ((), ()))
    chunks = width // lanes
    sub = lax.broadcasted_iota(jnp.int32, (8, lanes), 0)
    block = 8 * turn * slots
    for r in range(0, chips * slots, block):
        place = (
            lax.broadcasted_iota(jnp.int32, (block, count), 0) + r == target
        ).astype(jnp.float32).astype(jnp.bfloat16)
        moved = dot_f32(place, high, mm) + dot_f32(place, low, mm)
        for g in range(8):
            base = (r // slots + g * turn) * (chunks * slots + 1)

            def head(a, k):
                at = (g * turn + a) * slots
                return moved[at : at + 8, k * lanes : (k + 1) * lanes]

            def tag_of(a):
                at = r // slots + g * turn + a
                return jnp.broadcast_to(tags[at : at + 1, :], (8, lanes))

            for a in range(turn):
                for k in range(chunks):
                    tile = head(a, k)
                    if k > 0 and a > 0:
                        tile = jnp.where(sub < a, head(a, k - 1), tile)
                    elif k == 0 and a > 0:
                        tile = jnp.where(sub == a - 1, tag_of(a - 1), tile)
                        if a > 1:
                            tile = jnp.where(sub < a - 1, head(a - 1, chunks - 1), tile)
                    at = base + 8 * (12 * a + 2 * k)
                    send_ref[at : at + 8, :] = tile
                    whole = (g * turn + a) * slots + 8
                    send_ref[at + 8 : at + 16, :] = moved[
                        whole : whole + 8, k * lanes : (k + 1) * lanes
                    ]
            at = base + 8 * 12 * turn
            send_ref[at : at + 8, :] = jnp.where(
                sub == turn - 1, tag_of(turn - 1), head(turn - 1, chunks - 1)
            )


def slot_of(rows, lanes):
    row = lax.broadcasted_iota(jnp.int32, (rows, lanes), 0)
    return (row % 16 + 16 - (row // 16) % 8) % 16


def unpack(held_ref, first, chips, high_ref, low_ref, spread_ref):
    slots, lanes, turn = 16, 128, 8
    chunks = high_ref.shape[1] // lanes
    sub = lax.broadcasted_iota(jnp.int32, (8, lanes), 0)
    for s in range(first, first + chips):
        a = s % turn
        base = 97 * (s - a)

        def tile(t):
            at = base + 8 * t
            return held_ref[at : at + 8, :]

        for k in range(chunks):
            t = 12 * a + 2 * k
            top = tile(t)
            if a > 0:
                top = jnp.where(sub < a, tile(t + 2), top)
            high, low = split(jnp.concatenate([top, tile(t + 1)], axis=0))
            high_ref[s * slots : (s + 1) * slots, k * lanes : (k + 1) * lanes] = high
            low_ref[s * slots : (s + 1) * slots, k * lanes : (k + 1) * lanes] = low
        at = base + 97 * a + 96
        spread_ref[s * slots : (s + 1) * slots, :] = jnp.broadcast_to(
            held_ref[at : at + 1, :], (slots, lanes)
        )


def tags_of(spread, slot):
    lanes = spread.shape[1]
    lane = lax.broadcasted_iota(jnp.int32, spread.shape, 1)
    down = jnp.sum(jnp.where(lane == slot, spread, 0.0), axis=1, keepdims=True)
    down = jnp.where(down == 0.0, EMPTY, down)
    return jnp.broadcast_to(down, spread.shape)


def products(high_i, low_i, high_j, low_j):
    return dot_f32(high_i, high_j, NT) + (
        dot_f32(high_i, low_j, NT) + dot_f32(low_i, high_j, NT)
    )


def by_slot(best, slot):
    slots = 16
    rows, lanes = best.shape
    lane = lax.broadcasted_iota(jnp.int32, (rows, lanes), 1)
    picked = jnp.where(lane == slot, best, -2.0).reshape(rows // slots, slots, lanes)
    return jnp.max(picked, axis=1)


def own_kernel(held_ref, high_ref, low_ref, down_ref, best_ref, spread_ref):
    rows, lanes = down_ref.shape
    slot = slot_of(TILE, lanes)
    for j in range(0, rows, TILE):
        sj = slice(j, j + TILE)
        unpack(held_ref, j // 16, TILE // 16, high_ref, low_ref, spread_ref)
        down_j = tags_of(spread_ref[sj, :], slot)
        down_ref[sj, :] = down_j
        cols = [down_j[c : c + lanes, :].T[:1, :] for c in range(0, TILE, lanes)]
        high_j, low_j = high_ref[sj, :], low_ref[sj, :]
        mixed = dot_f32(high_j, low_j, NT)
        square = dot_f32(high_j, high_j, NT) + (mixed + mixed.T)
        best_j = jnp.full((TILE, lanes), -1.0, jnp.float32)
        for n, col_ix in enumerate(cols):
            part = square[:, n * lanes : (n + 1) * lanes]
            best_j = jnp.maximum(best_j, jnp.where(col_ix < down_j, part, -1.0))
        if j > 0:
            sims = products(high_ref[:j, :], low_ref[:j, :], high_j, low_j)
            down = down_ref[:j, :]
            best = best_ref[:j, :]
            over = []
            for n, col_ix in enumerate(cols):
                part = sims[:, n * lanes : (n + 1) * lanes]
                best = jnp.maximum(best, jnp.where(col_ix < down, part, -1.0))
                top = jnp.max(jnp.where(down < col_ix, part, -1.0), axis=0, keepdims=True)
                over.append(jnp.broadcast_to(top, (lanes, lanes)).T)
            best_ref[:j, :] = best
            best_j = jnp.maximum(best_j, jnp.concatenate(over, axis=0))
        best_ref[sj, :] = best_j


def cross(held_ref, high_ref, low_ref, down_ref, parts, high_o, low_o, spread_ref, get, put):
    half, lanes = high_o.shape[0], down_ref.shape[1]
    slot = slot_of(TILE, lanes)
    cols, over = {}, {}

    def finish(i, rows, j, sims):
        down = down_ref[rows, :]
        best = get(i, j)
        for n, col_ix in enumerate(cols[j]):
            part = sims[:, n * lanes : (n + 1) * lanes]
            best = jnp.maximum(best, jnp.where(col_ix < down, part, -1.0))
            top = jnp.where(down < col_ix, part, -1.0).reshape(part.shape[0] // 8, 8, lanes)
            top = jnp.max(top, axis=0)
            over[j, n] = top if (j, n) not in over else jnp.maximum(over[j, n], top)
        put(i, j, best)

    waiting = None
    for j in range(half // TILE):
        sj = slice(j * TILE, (j + 1) * TILE)
        unpack(held_ref, sj.start // 16, TILE // 16, high_o, low_o, spread_ref)
        down_j = tags_of(spread_ref[sj, :], slot)
        cols[j] = [down_j[c : c + lanes, :].T[:1, :] for c in range(0, TILE, lanes)]
        for i, (start, size) in enumerate(parts(j)):
            rows = pl.ds(pl.multiple_of(start, TILE), size)
            sims = products(high_ref[rows, :], low_ref[rows, :], high_o[sj, :], low_o[sj, :])
            if waiting is not None:
                finish(*waiting)
            waiting = i, rows, j, sims
    finish(*waiting)
    out = []
    for j in range(half // TILE):
        wide = [
            jnp.broadcast_to(jnp.max(over[j, n], axis=0, keepdims=True), (lanes, lanes)).T
            for n in range(TILE // lanes)
        ]
        out.append(by_slot(jnp.concatenate(wide, axis=0), slot))
    return jnp.concatenate(out, axis=0)


def swapped(core, blocks):
    lanes = blocks[0].shape[1]
    slot = slot_of(TILE, lanes)
    one, two = (
        by_slot(jnp.broadcast_to(jnp.max(best, axis=1, keepdims=True), best.shape), slot)
        for best in blocks
    )
    return jnp.concatenate(
        [jnp.where(core == 0, one, two), jnp.where(core == 0, two, one)], axis=0
    )


def first_kernel(
    held_ref, high_ref, low_ref, down_ref, best_ref, row_ref, col_ref, total_ref, high_o, low_o, spread_ref
):
    half = high_o.shape[0]
    core = lax.axis_index("core")
    shared = [core * TILE, (1 - core) * TILE]
    done = {}

    def get(i, j):
        if i == 1:
            return best_ref[pl.ds(pl.multiple_of(shared[j], TILE), TILE), :]
        return best_ref[half:, :] if j == 0 else total_ref[...]

    def put(i, j, best):
        if i == 1:
            done[j] = best
        else:
            total_ref[...] = best

    col_ref[...] = cross(
        held_ref,
        high_ref,
        low_ref,
        down_ref,
        lambda j: [(half, half), (shared[j], TILE)],
        high_o,
        low_o,
        spread_ref,
        get,
        put,
    )
    row_ref[...] = swapped(core, [done[0], done[1]])


def second_kernel(
    held_ref, high_ref, low_ref, down_ref, total_ref, row_ref, col_ref, out_ref, high_o, low_o, spread_ref
):
    half = high_o.shape[0]
    core = lax.axis_index("core")
    shared = [core * TILE, (1 - core) * TILE]
    done = {}
    cols = cross(
        held_ref,
        high_ref,
        low_ref,
        down_ref,
        lambda j: [(half + shared[j], TILE)],
        high_o,
        low_o,
        spread_ref,
        lambda i, j: total_ref[pl.ds(pl.multiple_of(shared[j], TILE), TILE), :],
        lambda i, j, best: done.update({j: best}),
    )
    own = row_ref[...], swapped(core, [done[0], done[1]])
    other = col_ref[...], cols
    chips = out_ref.shape[0] // 4
    for h in range(2):
        out_ref[h * chips : (h + 1) * chips, :] = jnp.where(core == 0, own[h], other[h])
        out_ref[(2 + h) * chips : (3 + h) * chips, :] = jnp.where(core == 0, other[h], own[h])


def pick_kernel(answer_ref, cl_ref, rank_ref, out_ref):
    lanes = answer_ref.shape[1]
    chips = answer_ref.shape[0] // 2
    count = cl_ref.shape[1]
    owner = (lax.broadcasted_iota(jnp.int32, (chips, count), 0) == cl_ref[...]).astype(
        jnp.float32
    ).astype(jnp.bfloat16)
    tn = (((0,), (0,)), ((), ()))
    answer = jnp.maximum(answer_ref[:chips, :], answer_ref[chips:, :])
    high, low = split(answer)
    by_rank = dot_f32(
        jnp.concatenate([high, low], axis=0), jnp.concatenate([owner, owner], axis=0), tn
    )
    at_rank = lax.broadcasted_iota(jnp.int32, (lanes, count), 0) == rank_ref[...]
    out_ref[...] = jnp.sum(jnp.where(at_rank, by_rank, 0.0), axis=0, keepdims=True)


def on_device(embeddings, clusters, indices):
    count, width = embeddings.shape
    chip_axes = ("z", "y", "x_hi", "x_lo")
    chips, slots, lanes = 64, 16, 128
    rows = chips * slots
    length = slots * width // lanes + 1
    cl = clusters.reshape(1, count)
    ix = indices.reshape(1, count)
    f32 = functools.partial(jax.ShapeDtypeStruct, dtype=jnp.float32)
    bf16 = functools.partial(jax.ShapeDtypeStruct, dtype=jnp.bfloat16)
    dma = pltpu.SemaphoreType.DMA
    sending, rank = pl.pallas_call(
        place_kernel,
        out_shape=(f32((chips * length, lanes)), jax.ShapeDtypeStruct((1, count), jnp.int32)),
        in_specs=[pl.BlockSpec(memory_space=pltpu.HBM)] * 3,
        out_specs=(VMEM, VMEM),
        scratch_shapes=[
            pltpu.VMEM((count, width), jnp.float32),
            pltpu.VMEM((1, count), jnp.int32),
            pltpu.VMEM((1, count), jnp.int32),
            dma((2,)),
            dma,
            dma,
        ],
        compiler_params=PARAMS,
        name="place",
    )(*(pltpu.with_memory_space_constraint(v, pltpu.HBM) for v in (embeddings, cl, ix)))
    held = lax.all_to_all(
        sending.reshape(chips * length, 1, lanes), chip_axes, split_axis=0, concat_axis=0, tiled=True
    )
    part = chips * length // 2
    arrived = [
        lax.ppermute(held[h * part : (h + 1) * part], "core", [(0, 1), (1, 0)]).reshape(part, lanes)
        for h in range(2)
    ]
    held = held.reshape(chips * length, lanes)
    flops = 2 * rows * rows * width * 3
    high, low, down, best = pl.pallas_call(
        own_kernel,
        out_shape=(
            bf16((rows, width)),
            bf16((rows, width)),
            f32((rows, lanes)),
            f32((rows, lanes)),
        ),
        in_specs=[VMEM],
        out_specs=(VMEM,) * 4,
        scratch_shapes=[pltpu.VMEM((rows, lanes), jnp.float32)],
        compiler_params=PARAMS,
        cost_estimate=pl.CostEstimate(flops=flops, bytes_accessed=8 << 20, transcendentals=0),
        name="own",
    )(held)
    half = rows // 2
    scratch = [
        pltpu.VMEM((half, width), jnp.bfloat16),
        pltpu.VMEM((half, width), jnp.bfloat16),
        pltpu.VMEM((half, lanes), jnp.float32),
    ]
    row, col, total = pl.pallas_call(
        first_kernel,
        out_shape=(f32((chips // 2, lanes)), f32((chips // 2, lanes)), f32((half, lanes))),
        in_specs=[VMEM] * 5,
        out_specs=(VMEM,) * 3,
        scratch_shapes=scratch,
        compiler_params=PARAMS,
        cost_estimate=pl.CostEstimate(
            flops=3 * flops // 8, bytes_accessed=2 << 20, transcendentals=0
        ),
        name="first",
    )(arrived[0], high, low, down, best)
    result = pl.pallas_call(
        second_kernel,
        out_shape=f32((2 * chips, lanes)),
        in_specs=[VMEM] * 7,
        out_specs=VMEM,
        scratch_shapes=scratch,
        compiler_params=PARAMS,
        cost_estimate=pl.CostEstimate(flops=flops // 8, bytes_accessed=2 << 20, transcendentals=0),
        name="second",
    )(arrived[1], high, low, down, total, row, col)
    answer = lax.all_to_all(
        result.reshape(2 * chips, 1, lanes), ("core",) + chip_axes, split_axis=0, concat_axis=0, tiled=True
    ).reshape(2 * chips, lanes)
    out = pl.pallas_call(
        pick_kernel,
        out_shape=f32((1, count)),
        in_specs=[VMEM] * 3,
        out_specs=VMEM,
        compiler_params=PARAMS,
        name="pick",
    )(answer, cl, rank)
    return out.reshape(count)


def solution(mesh):
    fine = Mesh(mesh.devices.reshape(4, 2, 2, 2, 4), POINTS)
    return jax.shard_map(
        on_device,
        mesh=fine,
        in_specs=(P(POINTS, None), P(POINTS), P(POINTS)),
        out_specs=P(POINTS),
        check_vma=False,
    )
```

```python
import functools

import jax
import jax.numpy as jnp
from jax import lax
from jax.experimental import pallas as pl
from jax.experimental.pallas import tpu as pltpu
from jax.sharding import Mesh, PartitionSpec as P

EPS = 1e-06
EMPTY = 1e9
TILE = 256
POINTS = ("y", "x_hi", "core", "x_lo", "z")
NT = (((1,), (1,)), ((), ()))
VMEM = pl.BlockSpec(memory_space=pltpu.VMEM)
PARAMS = pltpu.CompilerParams(vmem_limit_bytes=20 * 1024 * 1024)


def split(values):
    high = values.astype(jnp.bfloat16)
    low = (values - high.astype(jnp.float32)).astype(jnp.bfloat16)
    return high, low


def dot_f32(a, b, dims):
    return lax.dot_general(a, b, dims, preferred_element_type=jnp.float32)


def place_kernel(emb_hbm, cl_hbm, ix_hbm, send_ref, rank_ref, emb, cl_ref, ix_ref, emb_sem, cl_sem, ix_sem):
    count, width = emb.shape
    slots, lanes, turn, chips = 16, 128, 8, 64
    parts = 2
    step = count // parts
    copies = [
        pltpu.make_async_copy(
            emb_hbm.at[pl.ds(p * step, step)], emb.at[pl.ds(p * step, step)], emb_sem.at[p]
        )
        for p in range(parts)
    ]
    cl_copy = pltpu.make_async_copy(cl_hbm, cl_ref, cl_sem)
    ix_copy = pltpu.make_async_copy(ix_hbm, ix_ref, ix_sem)
    cl_copy.start()
    ix_copy.start()
    for copy in copies:
        copy.start()
    cl_copy.wait()
    ix_copy.wait()
    cl = cl_ref[...]
    ix = ix_ref[...]
    along = jnp.broadcast_to(cl.astype(jnp.float32), (count, count))
    down = along.T
    before = lax.broadcasted_iota(jnp.int32, (count, count), 0) < lax.broadcasted_iota(
        jnp.int32, (count, count), 1
    )
    rank = jnp.sum(
        jnp.where((along == down) & before, 1.0, 0.0), axis=0, keepdims=True
    ).astype(jnp.int32)
    rank_ref[...] = rank
    target = cl * slots + (rank + cl % turn) % slots
    owner = (lax.broadcasted_iota(jnp.int32, (chips, count), 0) == cl).astype(
        jnp.float32
    ).astype(jnp.bfloat16)
    at_rank = lax.broadcasted_iota(jnp.int32, (lanes, count), 0) == rank
    tag = ix + 1
    tag_high = jnp.where(at_rank, (tag // 256).astype(jnp.float32), 0.0).astype(jnp.bfloat16)
    tag_low = jnp.where(at_rank, (tag % 256).astype(jnp.float32), 0.0).astype(jnp.bfloat16)
    tags = 256.0 * dot_f32(owner, tag_high, NT) + dot_f32(owner, tag_low, NT)
    highs, lows = [], []
    for p in range(parts):
        copies[p].wait()
        x = emb[p * step : (p + 1) * step, :]
        unit = x * lax.rsqrt(jnp.sum(x * x, axis=1, keepdims=True) + EPS)
        high, low = split(unit)
        highs.append(high)
        lows.append(low)
    high = jnp.concatenate(highs, axis=0)
    low = jnp.concatenate(lows, axis=0)
    mm = (((1,), (0,)), ((), ()))
    chunks = width // lanes
    sub = lax.broadcasted_iota(jnp.int32, (8, lanes), 0)
    block = 8 * turn * slots
    for r in range(0, chips * slots, block):
        place = (
            lax.broadcasted_iota(jnp.int32, (block, count), 0) + r == target
        ).astype(jnp.float32).astype(jnp.bfloat16)
        moved = dot_f32(place, high, mm) + dot_f32(place, low, mm)
        for g in range(8):
            base = (r // slots + g * turn) * (chunks * slots + 1)

            def head(a, k):
                at = (g * turn + a) * slots
                return moved[at : at + 8, k * lanes : (k + 1) * lanes]

            def tag_of(a):
                at = r // slots + g * turn + a
                return jnp.broadcast_to(tags[at : at + 1, :], (8, lanes))

            for a in range(turn):
                for k in range(chunks):
                    tile = head(a, k)
                    if k > 0 and a > 0:
                        tile = jnp.where(sub < a, head(a, k - 1), tile)
                    elif k == 0 and a > 0:
                        tile = jnp.where(sub == a - 1, tag_of(a - 1), tile)
                        if a > 1:
                            tile = jnp.where(sub < a - 1, head(a - 1, chunks - 1), tile)
                    at = base + 8 * (12 * a + 2 * k)
                    send_ref[at : at + 8, :] = tile
                    whole = (g * turn + a) * slots + 8
                    send_ref[at + 8 : at + 16, :] = moved[
                        whole : whole + 8, k * lanes : (k + 1) * lanes
                    ]
            at = base + 8 * 12 * turn
            send_ref[at : at + 8, :] = jnp.where(
                sub == turn - 1, tag_of(turn - 1), head(turn - 1, chunks - 1)
            )


def slot_of(rows, lanes):
    row = lax.broadcasted_iota(jnp.int32, (rows, lanes), 0)
    return (row % 16 + 16 - (row // 16) % 8) % 16


def unpack(held_ref, first, chips, high_ref, low_ref, spread_ref):
    slots, lanes, turn = 16, 128, 8
    chunks = high_ref.shape[1] // lanes
    sub = lax.broadcasted_iota(jnp.int32, (8, lanes), 0)
    for s in range(first, first + chips):
        a = s % turn
        base = 97 * (s - a)

        def tile(t):
            at = base + 8 * t
            return held_ref[at : at + 8, :]

        for k in range(chunks):
            t = 12 * a + 2 * k
            top = tile(t)
            if a > 0:
                top = jnp.where(sub < a, tile(t + 2), top)
            high, low = split(jnp.concatenate([top, tile(t + 1)], axis=0))
            high_ref[s * slots : (s + 1) * slots, k * lanes : (k + 1) * lanes] = high
            low_ref[s * slots : (s + 1) * slots, k * lanes : (k + 1) * lanes] = low
        at = base + 97 * a + 96
        spread_ref[s * slots : (s + 1) * slots, :] = jnp.broadcast_to(
            held_ref[at : at + 1, :], (slots, lanes)
        )


def tags_of(spread, slot):
    lanes = spread.shape[1]
    lane = lax.broadcasted_iota(jnp.int32, spread.shape, 1)
    down = jnp.sum(jnp.where(lane == slot, spread, 0.0), axis=1, keepdims=True)
    down = jnp.where(down == 0.0, EMPTY, down)
    return jnp.broadcast_to(down, spread.shape)


def products(high_i, low_i, high_j, low_j):
    return dot_f32(high_i, high_j, NT) + (
        dot_f32(high_i, low_j, NT) + dot_f32(low_i, high_j, NT)
    )


def by_slot(best, slot):
    slots = 16
    rows, lanes = best.shape
    lane = lax.broadcasted_iota(jnp.int32, (rows, lanes), 1)
    picked = jnp.where(lane == slot, best, -2.0).reshape(rows // slots, slots, lanes)
    return jnp.max(picked, axis=1)


def own_kernel(held_ref, high_ref, low_ref, down_ref, best_ref, spread_ref):
    rows, lanes = down_ref.shape
    slot = slot_of(TILE, lanes)
    for j in range(0, rows, TILE):
        sj = slice(j, j + TILE)
        unpack(held_ref, j // 16, TILE // 16, high_ref, low_ref, spread_ref)
        down_j = tags_of(spread_ref[sj, :], slot)
        down_ref[sj, :] = down_j
        cols = [down_j[c : c + lanes, :].T[:1, :] for c in range(0, TILE, lanes)]
        high_j, low_j = high_ref[sj, :], low_ref[sj, :]
        mixed = dot_f32(high_j, low_j, NT)
        square = dot_f32(high_j, high_j, NT) + (mixed + mixed.T)
        best_j = jnp.full((TILE, lanes), -1.0, jnp.float32)
        for n, col_ix in enumerate(cols):
            part = square[:, n * lanes : (n + 1) * lanes]
            best_j = jnp.maximum(best_j, jnp.where(col_ix < down_j, part, -1.0))
        if j > 0:
            sims = products(high_ref[:j, :], low_ref[:j, :], high_j, low_j)
            down = down_ref[:j, :]
            best = best_ref[:j, :]
            over = []
            for n, col_ix in enumerate(cols):
                part = sims[:, n * lanes : (n + 1) * lanes]
                best = jnp.maximum(best, jnp.where(col_ix < down, part, -1.0))
                top = jnp.max(jnp.where(down < col_ix, part, -1.0), axis=0, keepdims=True)
                over.append(jnp.broadcast_to(top, (lanes, lanes)).T)
            best_ref[:j, :] = best
            best_j = jnp.maximum(best_j, jnp.concatenate(over, axis=0))
        best_ref[sj, :] = best_j


def cross(held_ref, high_ref, low_ref, down_ref, parts, high_o, low_o, spread_ref, get, put):
    half, lanes = high_o.shape[0], down_ref.shape[1]
    slot = slot_of(TILE, lanes)
    cols, over = {}, {}

    def finish(i, rows, j, sims):
        down = down_ref[rows, :]
        best = get(i, j)
        for n, col_ix in enumerate(cols[j]):
            part = sims[:, n * lanes : (n + 1) * lanes]
            best = jnp.maximum(best, jnp.where(col_ix < down, part, -1.0))
            top = jnp.where(down < col_ix, part, -1.0).reshape(part.shape[0] // 8, 8, lanes)
            top = jnp.max(top, axis=0)
            over[j, n] = top if (j, n) not in over else jnp.maximum(over[j, n], top)
        put(i, j, best)

    waiting = None
    for j in range(half // TILE):
        sj = slice(j * TILE, (j + 1) * TILE)
        unpack(held_ref, sj.start // 16, TILE // 16, high_o, low_o, spread_ref)
        down_j = tags_of(spread_ref[sj, :], slot)
        cols[j] = [down_j[c : c + lanes, :].T[:1, :] for c in range(0, TILE, lanes)]
        for i, (start, size) in enumerate(parts(j)):
            rows = pl.ds(pl.multiple_of(start, TILE), size)
            sims = products(high_ref[rows, :], low_ref[rows, :], high_o[sj, :], low_o[sj, :])
            if waiting is not None:
                finish(*waiting)
            waiting = i, rows, j, sims
    finish(*waiting)
    out = []
    for j in range(half // TILE):
        wide = [
            jnp.broadcast_to(jnp.max(over[j, n], axis=0, keepdims=True), (lanes, lanes)).T
            for n in range(TILE // lanes)
        ]
        out.append(by_slot(jnp.concatenate(wide, axis=0), slot))
    return jnp.concatenate(out, axis=0)


def swapped(core, blocks):
    lanes = blocks[0].shape[1]
    slot = slot_of(TILE, lanes)
    one, two = (
        by_slot(jnp.broadcast_to(jnp.max(best, axis=1, keepdims=True), best.shape), slot)
        for best in blocks
    )
    return jnp.concatenate(
        [jnp.where(core == 0, one, two), jnp.where(core == 0, two, one)], axis=0
    )


def first_kernel(
    held_ref, high_ref, low_ref, down_ref, best_ref, row_ref, col_ref, total_ref, high_o, low_o, spread_ref
):
    half = high_o.shape[0]
    core = lax.axis_index("core")
    shared = [core * TILE, (1 - core) * TILE]
    done = {}

    def get(i, j):
        if i == 1:
            return best_ref[pl.ds(pl.multiple_of(shared[j], TILE), TILE), :]
        return best_ref[half:, :] if j == 0 else total_ref[...]

    def put(i, j, best):
        if i == 1:
            done[j] = best
        else:
            total_ref[...] = best

    col_ref[...] = cross(
        held_ref,
        high_ref,
        low_ref,
        down_ref,
        lambda j: [(half, half), (shared[j], TILE)],
        high_o,
        low_o,
        spread_ref,
        get,
        put,
    )
    row_ref[...] = swapped(core, [done[0], done[1]])


def second_kernel(
    held_ref, high_ref, low_ref, down_ref, total_ref, row_ref, col_ref, out_ref, high_o, low_o, spread_ref
):
    half = high_o.shape[0]
    core = lax.axis_index("core")
    shared = [core * TILE, (1 - core) * TILE]
    done = {}
    cols = cross(
        held_ref,
        high_ref,
        low_ref,
        down_ref,
        lambda j: [(half + shared[j], TILE)],
        high_o,
        low_o,
        spread_ref,
        lambda i, j: total_ref[pl.ds(pl.multiple_of(shared[j], TILE), TILE), :],
        lambda i, j, best: done.update({j: best}),
    )
    own = row_ref[...], swapped(core, [done[0], done[1]])
    other = col_ref[...], cols
    chips = out_ref.shape[0] // 4
    for h in range(2):
        out_ref[h * chips : (h + 1) * chips, :] = jnp.where(core == 0, own[h], other[h])
        out_ref[(2 + h) * chips : (3 + h) * chips, :] = jnp.where(core == 0, other[h], own[h])


def pick_kernel(answer_ref, cl_ref, rank_ref, out_ref):
    lanes = answer_ref.shape[1]
    chips = answer_ref.shape[0] // 2
    count = cl_ref.shape[1]
    owner = (lax.broadcasted_iota(jnp.int32, (chips, count), 0) == cl_ref[...]).astype(
        jnp.float32
    ).astype(jnp.bfloat16)
    tn = (((0,), (0,)), ((), ()))
    answer = jnp.maximum(answer_ref[:chips, :], answer_ref[chips:, :])
    high, low = split(answer)
    by_rank = dot_f32(
        jnp.concatenate([high, low], axis=0), jnp.concatenate([owner, owner], axis=0), tn
    )
    slots = 16
    at_rank = lax.broadcasted_iota(jnp.int32, (slots, count), 0) == rank_ref[...]
    out_ref[...] = jnp.sum(jnp.where(at_rank, by_rank[:slots, :], 0.0), axis=0, keepdims=True)


def on_device(embeddings, clusters, indices):
    count, width = embeddings.shape
    chip_axes = ("z", "y", "x_hi", "x_lo")
    chips, slots, lanes = 64, 16, 128
    rows = chips * slots
    length = slots * width // lanes + 1
    cl = clusters.reshape(1, count)
    ix = indices.reshape(1, count)
    f32 = functools.partial(jax.ShapeDtypeStruct, dtype=jnp.float32)
    bf16 = functools.partial(jax.ShapeDtypeStruct, dtype=jnp.bfloat16)
    dma = pltpu.SemaphoreType.DMA
    sending, rank = pl.pallas_call(
        place_kernel,
        out_shape=(f32((chips * length, lanes)), jax.ShapeDtypeStruct((1, count), jnp.int32)),
        in_specs=[pl.BlockSpec(memory_space=pltpu.HBM)] * 3,
        out_specs=(VMEM, VMEM),
        scratch_shapes=[
            pltpu.VMEM((count, width), jnp.float32),
            pltpu.VMEM((1, count), jnp.int32),
            pltpu.VMEM((1, count), jnp.int32),
            dma((2,)),
            dma,
            dma,
        ],
        compiler_params=PARAMS,
        name="place",
    )(*(pltpu.with_memory_space_constraint(v, pltpu.HBM) for v in (embeddings, cl, ix)))
    held = lax.all_to_all(
        sending.reshape(chips * length, 1, lanes), chip_axes, split_axis=0, concat_axis=0, tiled=True
    )
    part = chips * length // 2
    arrived = [
        lax.ppermute(held[h * part : (h + 1) * part], "core", [(0, 1), (1, 0)]).reshape(part, lanes)
        for h in range(2)
    ]
    held = held.reshape(chips * length, lanes)
    flops = 2 * rows * rows * width * 3
    high, low, down, best = pl.pallas_call(
        own_kernel,
        out_shape=(
            bf16((rows, width)),
            bf16((rows, width)),
            f32((rows, lanes)),
            f32((rows, lanes)),
        ),
        in_specs=[VMEM],
        out_specs=(VMEM,) * 4,
        scratch_shapes=[pltpu.VMEM((rows, lanes), jnp.float32)],
        compiler_params=PARAMS,
        cost_estimate=pl.CostEstimate(flops=flops, bytes_accessed=8 << 20, transcendentals=0),
        name="own",
    )(held)
    half = rows // 2
    scratch = [
        pltpu.VMEM((half, width), jnp.bfloat16),
        pltpu.VMEM((half, width), jnp.bfloat16),
        pltpu.VMEM((half, lanes), jnp.float32),
    ]
    row, col, total = pl.pallas_call(
        first_kernel,
        out_shape=(f32((chips // 2, lanes)), f32((chips // 2, lanes)), f32((half, lanes))),
        in_specs=[VMEM] * 5,
        out_specs=(VMEM,) * 3,
        scratch_shapes=scratch,
        compiler_params=PARAMS,
        cost_estimate=pl.CostEstimate(
            flops=3 * flops // 8, bytes_accessed=2 << 20, transcendentals=0
        ),
        name="first",
    )(arrived[0], high, low, down, best)
    result = pl.pallas_call(
        second_kernel,
        out_shape=f32((2 * chips, lanes)),
        in_specs=[VMEM] * 7,
        out_specs=VMEM,
        scratch_shapes=scratch,
        compiler_params=PARAMS,
        cost_estimate=pl.CostEstimate(flops=flops // 8, bytes_accessed=2 << 20, transcendentals=0),
        name="second",
    )(arrived[1], high, low, down, total, row, col)
    answer = lax.all_to_all(
        result.reshape(2 * chips, 1, lanes), ("core",) + chip_axes, split_axis=0, concat_axis=0, tiled=True
    ).reshape(2 * chips, lanes)
    out = pl.pallas_call(
        pick_kernel,
        out_shape=f32((1, count)),
        in_specs=[VMEM] * 3,
        out_specs=VMEM,
        compiler_params=PARAMS,
        name="pick",
    )(answer, cl, rank)
    return out.reshape(count)


def solution(mesh):
    fine = Mesh(mesh.devices.reshape(4, 2, 2, 2, 4), POINTS)
    return jax.shard_map(
        on_device,
        mesh=fine,
        in_specs=(P(POINTS, None), P(POINTS), P(POINTS)),
        out_specs=P(POINTS),
        check_vma=False,
    )
```
